32 devices in a mesh: section: 2 (over core), dp: 4 (over y, x), seq: 4 (over z).
Axes of the slice: x: 2, y: 2, z: 4, core: 2. Of those that a mesh axis runs over, the one named last changes fastest.
Arguments:
- tokens: bfloat16 [16, 1024, 512], P('dp', 'seq'), may hold values from -6 to 6
- cotangent: bfloat16 [16, 1024, 512], P('dp', 'seq'), may hold values from -6 to 6
- tap_masks: int32 [2, 9, 16, 1024], P('section', None, 'dp', 'seq'), may hold values from 0 to 1, as said below
- conv_weight: bfloat16 [2, 512, 9, 512], P('section'), may hold values from -0.09375 to 0.09375
- up_weight: bfloat16 [2, 512, 2048], P('section'), may hold values from -0.25 to 0.25
- up_bias: float32 [2, 2048], P('section'), may hold values from -1.5 to 1.5
- down_weight: bfloat16 [2, 2048, 512], P('section'), may hold values from -0.125 to 0.125
- norm_gains: float32 [2, 512, 2], P('section'), may hold values from 0.25 to 1.75
- shift_terms: float32 [2, 512, 4], P('section'), may hold values from -1.5 to 1.5
Outputs:
- activations: bfloat16 [2, 16, 1024, 512], P('section', 'dp', 'seq')
- in_grads: float32 [2, 16, 1024, 512], P('section', 'dp', 'seq')
- conv_grad: float32 [2, 512, 9, 512], P('section', ('dp', 'seq'))
- up_grad: float32 [2, 512, 2048], P('section', ('dp', 'seq'))
- up_bias_grad: float32 [2, 2048], P('section', ('dp', 'seq'))
- down_grad: float32 [2, 2048, 512], P('section', ('dp', 'seq'))
- gain_grad: float32 [2, 512, 2], P('section', ('dp', 'seq'))
- shift_grad: float32 [2, 512, 4], P('section', ('dp', 'seq'))
The draws below stay inside these ranges and needn't reach their ends.
Inputs may be any that keep to these rules, and one draw needn't show every extreme that they name: tap_masks[s, k, r, p] is 1 exactly when position p + (k - 4) * d of row r lies inside the row and in the same contig (a run of positions) as p, with d = 2 for s = 0 and 32 for s = 1.
All inputs are finite; a program needn't handle non-finite values.
Results may differ from the reference program's by a relative error of at most 0.0095.
Values may be sent and summed in bfloat16 or wider, within the bound.
A program may use at most 192 MiB of HBM per device.

```python
import jax
import jax.numpy as jnp
from jax import lax

D = 512
FF = 2048
KERNEL_TAPS = 9
DILATION_TIGHT = 2
DILATION_WIDE = 32
SEQ_LEN = 1024
ROWS_DEV = 4
ROWS = 16


def draw_tap_masks(key, part):
    key = jax.random.fold_in(key, 11)
    start_key, pick_key = jax.random.split(key)
    starts = jax.random.randint(start_key, (ROWS, SEQ_LEN), 0, SEQ_LEN) < 3
    chosen = jax.random.randint(pick_key, (ROWS // ROWS_DEV,), 0, ROWS_DEV)
    row_index = jnp.arange(ROWS, dtype=jnp.int32)
    whole_row = row_index % ROWS_DEV == jnp.repeat(chosen, ROWS_DEV)
    starts = jnp.where(whole_row[:, None], False, starts)
    contig = jnp.cumsum(starts.astype(jnp.int32), axis=1)
    position = jnp.arange(SEQ_LEN, dtype=jnp.int32)
    sections = []
    for dilation_spacing in (DILATION_TIGHT, DILATION_WIDE):
        tap_list = []
        for tap_index in range(KERNEL_TAPS):
            offset = (tap_index - KERNEL_TAPS // 2) * dilation_spacing
            source = position + offset
            inside = (source >= 0) & (source < SEQ_LEN)
            clipped = jnp.clip(source, 0, SEQ_LEN - 1)
            same_contig = contig[:, clipped] == contig
            tap_list.append((inside[None, :] & same_contig).astype(jnp.int32))
        sections.append(jnp.stack(tap_list))
    return jnp.stack(sections)


def block_scale(stream_key, extent, cuts, least, top_value):
    level = 1.0
    for dim, parts in cuts:
        heights = jax.random.uniform(jax.random.fold_in(jax.random.fold_in(stream_key, 6), dim), (parts,), jnp.float32, least / len(cuts), top_value / len(cuts))
        level = level * jnp.repeat(jnp.exp(heights), extent[dim] // parts).reshape((-1,) + (1,) * (len(extent) - 1 - dim))
    return level


def noise(own_key, shape, scale, most, cuts=(), held_as=jnp.bfloat16):
    entries = scale * jax.random.normal(own_key, shape, jnp.float32)
    if cuts:
        entries = entries * block_scale(own_key, shape, cuts, -0.22, 0.18)
    return jnp.clip(entries, -most, most).astype(held_as)


def setup_inputs(seed: int = 0) -> dict:
    key_list = jax.random.split(jax.random.key(seed), 10)
    return {
        "tokens": noise(key_list[0], (ROWS, SEQ_LEN, D), 1.0, 6.0, ((0, 4), (1, 4))),
        "cotangent": noise(key_list[1], (ROWS, SEQ_LEN, D), 1.0, 6.0, ((0, 4), (1, 4))),
        "tap_masks": draw_tap_masks(jax.random.fold_in(key_list[9], 71), 0),
        "conv_weight": noise(key_list[3], (2, D, KERNEL_TAPS, D), (KERNEL_TAPS * D) ** -0.5, 0.09375, ((0, 2),)),
        "up_weight": noise(key_list[4], (2, D, FF), D ** -0.5, 0.25, ((0, 2),)),
        "up_bias": noise(key_list[5], (2, FF), 0.3, 1.5, ((0, 2),), jnp.float32),
        "down_weight": noise(key_list[6], (2, FF, D), FF ** -0.5, 0.125, ((0, 2),)),
        "norm_gains": jnp.clip(1.0 + 0.15 * jax.random.normal(key_list[7], (2, D, 2), jnp.float32), 0.25, 1.75),
        "shift_terms": noise(key_list[8], (2, D, 4), 0.3, 1.5, ((0, 2),), jnp.float32),
    }


@jax.custom_vjp
def low(v):
    return lax.optimization_barrier(v.astype(jnp.bfloat16)).astype(jnp.float32)

@jax.custom_vjp
def low_back(v):
    return v

def low_keep(v):
    return (low(v), None)

def low_pass(kept, grad):
    return (grad,)

def back_keep(v):
    return (v, None)

def back_low(kept, grad):
    return (low(grad),)
low.defvjp(low_keep, low_pass)
low_back.defvjp(back_keep, back_low)
HIGHEST_PRECISION = lax.Precision.HIGHEST

def layer_norm(values):
    centred = values - lax.optimization_barrier(jnp.mean(values, axis=-1, keepdims=True))
    return centred * lax.rsqrt(lax.optimization_barrier(jnp.mean(centred * centred, axis=-1, keepdims=True)) + 1e-05)

def convolution_unit(input_tokens, tap_mask, dilation_spacing, kernel_weight, up_matrix, up_projection_bias, down_matrix, norm_scale_vector, shifted_columns):
    length = input_tokens.shape[1]
    border_width = KERNEL_TAPS // 2 * dilation_spacing
    padded_tokens = jnp.pad(input_tokens, ((0, 0), (border_width, border_width), (0, 0)))
    tap_stack = jnp.stack([padded_tokens[:, tap_index * dilation_spacing:tap_index * dilation_spacing + length, :] for tap_index in range(KERNEL_TAPS)], axis=2)
    tap_stack = tap_stack * jnp.transpose(tap_mask, (1, 2, 0))[..., None]
    conv_out = low_back(jnp.einsum('rpki,iko->rpo', tap_stack, kernel_weight, precision=HIGHEST_PRECISION) + shifted_columns[:, 0])
    mixed_sum = input_tokens + layer_norm(jax.nn.gelu(conv_out)) * norm_scale_vector[:, 0] + shifted_columns[:, 1]
    hidden = low_back(jnp.einsum('rpd,df->rpf', low(mixed_sum), up_matrix, precision=HIGHEST_PRECISION) + up_projection_bias)
    upper_low = low(jax.nn.gelu(hidden))
    ffn_out = low_back(jnp.einsum('rpf,fd->rpd', upper_low, down_matrix, precision=HIGHEST_PRECISION) + shifted_columns[:, 2])
    return mixed_sum + layer_norm(ffn_out) * norm_scale_vector[:, 1] + shifted_columns[:, 3]

def reference(tokens, cotangent, tap_masks, conv_weight, up_weight, up_bias, down_weight, norm_gains, shift_terms):
    group_rows = max(1, min(ROWS_DEV, 4096 // SEQ_LEN))
    group_count = ROWS // group_rows
    mask_vals = tap_masks.astype(jnp.float32)
    params = (conv_weight.astype(jnp.float32), up_weight.astype(jnp.float32), up_bias, down_weight.astype(jnp.float32), norm_gains, shift_terms)

    def two_blocks(params, token_vals, nudges):
        kernel_weight, up_matrix, up_projection_bias, down_matrix, norm_scale_vector, shifted_columns = params

        def section_pair(group_args):
            grouped_rows, grouped_masks, nudge_group = group_args
            first_block_output = convolution_unit(grouped_rows, grouped_masks[0], DILATION_TIGHT, kernel_weight[0], up_matrix[0], up_projection_bias[0], down_matrix[0], norm_scale_vector[0], shifted_columns[0])
            handed_tokens = low_back(low(first_block_output) + nudge_group)
            second_block_output = convolution_unit(handed_tokens, grouped_masks[1], DILATION_WIDE, kernel_weight[1], up_matrix[1], up_projection_bias[1], down_matrix[1], norm_scale_vector[1], shifted_columns[1])
            return (first_block_output, second_block_output)
        grouped = (token_vals.reshape(group_count, group_rows, SEQ_LEN, D), jnp.moveaxis(mask_vals.reshape(2, KERNEL_TAPS, group_count, group_rows, SEQ_LEN), 2, 0), nudges.reshape(group_count, group_rows, SEQ_LEN, D))
        first_block_output, second_block_output = lax.map(jax.checkpoint(section_pair), grouped)
        return (first_block_output.reshape(ROWS, SEQ_LEN, D), second_block_output.reshape(ROWS, SEQ_LEN, D))
    token_vals = tokens.astype(jnp.float32)
    nudges = jnp.zeros((ROWS, SEQ_LEN, D), jnp.float32)
    outputs, pullback = jax.vjp(two_blocks, params, token_vals, nudges)
    grad_params, grad_tokens, grad_passed = pullback((jnp.zeros_like(outputs[0]), cotangent.astype(jnp.float32)))
    activations = jnp.stack([outputs[0], outputs[1]]).astype(jnp.bfloat16)
    in_grads = jnp.stack([grad_tokens, grad_passed])
    conv_grad, up_grad, up_bias_grad, down_grad, gain_grad, shift_grad = grad_params
    return (activations, in_grads, conv_grad, up_grad, up_bias_grad, down_grad, gain_grad, shift_grad)
```

```python
import functools

import jax
import jax.numpy as jnp
from jax import lax
from jax.experimental import pallas as pl
from jax.experimental.pallas import tpu as pltpu
from jax.sharding import PartitionSpec as P

TAPS = 9
CENTRE = TAPS // 2
TIGHT = 2
WIDE = 32
HALO = CENTRE * WIDE
EDGE = 16
EPS = 1e-05
MESH = pl.DeviceIdType.MESH
BF16 = jnp.bfloat16
F32 = jnp.float32
LAGS = (0, 3, 5, 7)
TANH_SCALE = 0.7978845608028654
TANH_CUBE = TANH_SCALE * 0.044715


def gelu_pair(z):
    square = z * z
    half = 0.5 + 0.5 * jnp.tanh(z * (TANH_SCALE + TANH_CUBE * square))
    value = z * half
    return value, half + value * (1.0 - half) * (2.0 * TANH_SCALE + 6.0 * TANH_CUBE * square)


def normalise(values):
    centred = values - jnp.mean(values, axis=-1, keepdims=True)
    scale = lax.rsqrt(jnp.mean(centred * centred, axis=-1, keepdims=True) + EPS)
    return centred * scale, scale


def norm_backward(weighted, unit):
    return (
        weighted
        - jnp.mean(weighted, axis=-1, keepdims=True)
        - unit * jnp.mean(weighted * unit, axis=-1, keepdims=True)
    )


def column_sum(values):
    return jnp.sum(values, axis=0, keepdims=True)


def dot(a, b):
    return jnp.dot(a, b, preferred_element_type=F32)


def dot_nt(a, b):
    return lax.dot_general(a, b, (((1,), (1,)), ((), ())), preferred_element_type=F32)


def dot_tn(a, b):
    return lax.dot_general(a, b, (((0,), (0,)), ((), ())), preferred_element_type=F32)


class Geometry:
    def __init__(self, dp, seq, rows, length, width, hidden):
        self.dp, self.seq = dp, seq
        self.rows, self.length, self.width = rows, length, width
        self.tokens = rows * length
        self.chunks = hidden // width
        self.low = max(1, 16 * dp * seq // width)
        self.owners = dp * seq // self.low
        self.share = width // self.owners
        self.final_share = width // (dp * seq)
        self.bias_share = hidden // (dp * seq)
        dp_bits = [("dp", 1 << i) for i in range(dp.bit_length() - 1)]
        seq_all = [("seq", 1 << i) for i in range(seq.bit_length() - 1)]
        seq_bits = [bit for bit in seq_all if bit[1] >= self.low]
        self.bits = dp_bits + seq_bits
        self.all_bits = dp_bits + seq_all
        back = dp_bits[::-1]
        first = seq_bits[:1]
        orders = [
            dp_bits + seq_bits,
            back + seq_bits,
            first + dp_bits + seq_bits[1:],
            dp_bits + seq_bits,
            back + seq_bits,
            first + back + seq_bits[1:],
        ]
        self.orders = [[self.bits.index(bit) for bit in order] for order in orders]
        self.stages = len(self.bits)
        self.slices = 2 * self.chunks + TAPS
        lags = list(LAGS)
        while len(lags) < self.stages:
            lags.append(lags[-1] + 2)
        self.lags = lags[: self.stages]
        self.last_lag = self.lags[-1] + 1


def body(
    geo,
    tokens_hbm,
    cotangent_hbm,
    conv_hbm,
    up_hbm,
    down_hbm,
    masks,
    bias,
    gains,
    shifts,
    act_hbm,
    grads_hbm,
    conv_out,
    up_out,
    down_out,
    bias_out,
    gain_out,
    shift_out,
    fields,
    conv_grads,
    conv_w,
    up_w,
    down_w,
    slabs,
    taps,
    unit_one,
    slope_one,
    unit_two,
    scale_two,
    mixed_grads,
    given,
    ffn_grads,
    results,
    mask_columns,
    partial,
    arrived,
    sums,
    sums_sent,
    sums_arrived,
    load_sem,
    row_load_sem,
    token_edge_send,
    token_edge_recv,
    pass_send,
    pass_recv,
    back_send,
    back_recv,
    edge_send,
    edge_recv,
    act_sem,
    grads_sem,
    part_send,
    part_recv,
    sums_send,
    sums_recv,
):
    rows, length, width, chunks = geo.rows, geo.length, geo.width, geo.chunks
    section = lax.axis_index("section")
    dp = lax.axis_index("dp")
    seq = lax.axis_index("seq")
    mine = {"dp": dp, "seq": seq}
    in_first = section == 0
    in_second = section == 1
    has_left = (seq + geo.seq - 1) // geo.seq
    has_right = 1 - (seq + 1) // geo.seq
    own = slice(HALO, HALO + length)

    def bit_of(bit):
        axis, size = bit
        return (mine[axis] // size) % 2

    def partner(bit):
        axis, size = bit
        other = mine[axis] + (1 - 2 * bit_of(bit)) * size
        return (section, other, seq) if axis == "dp" else (section, dp, other)

    core = (1 - section, dp, seq)
    left, right = (section, dp, seq - 1), (section, dp, seq + 1)

    loads = [
        pltpu.make_async_copy(conv_hbm, conv_w, load_sem.at[0]),
        pltpu.make_async_copy(up_hbm, up_w, load_sem.at[1]),
        pltpu.make_async_copy(down_hbm, down_w, load_sem.at[2]),
    ]
    token_load = pltpu.make_async_copy(tokens_hbm, fields.at[:, own], row_load_sem.at[0])
    given_load = pltpu.make_async_copy(cotangent_hbm, given, row_load_sem.at[1])

    @pl.when(in_first)
    def _():
        token_load.start()

    for load in loads:
        load.start()

    @pl.when(in_second)
    def _():
        given_load.start()

    @pl.when(has_left == 0)
    def _():
        fields[:, :HALO] = jnp.zeros((rows, HALO, width), BF16)
        conv_grads[:, :HALO] = jnp.zeros((rows, HALO, width), BF16)

    @pl.when(has_right == 0)
    def _():
        fields[:, HALO + length :] = jnp.zeros((rows, HALO, width), BF16)
        conv_grads[:, HALO + length :] = jnp.zeros((rows, HALO, width), BF16)

    sums[...] = jnp.zeros(sums.shape, F32)

    barrier = pltpu.get_barrier_semaphore()
    for bit in geo.all_bits:
        pl.semaphore_signal(barrier, inc=1, device_id=partner(bit), device_id_type=MESH)
    pl.semaphore_signal(barrier, inc=1, device_id=core, device_id_type=MESH)

    @pl.when(has_left == 1)
    def _():
        for who in (section, 1 - section):
            pl.semaphore_signal(barrier, inc=1, device_id=(who, dp, seq - 1), device_id_type=MESH)

    @pl.when(has_right == 1)
    def _():
        for who in (section, 1 - section):
            pl.semaphore_signal(barrier, inc=1, device_id=(who, dp, seq + 1), device_id_type=MESH)

    pl.semaphore_wait(barrier, len(geo.all_bits) + 1 + 2 * has_left + 2 * has_right)

    tokens_right = pltpu.make_async_remote_copy(
        src_ref=tokens_hbm.at[:, length - EDGE : length],
        dst_ref=fields.at[:, HALO - EDGE : HALO],
        send_sem=token_edge_send.at[0],
        recv_sem=token_edge_recv.at[0],
        device_id=right,
        device_id_type=MESH,
    )
    tokens_left = pltpu.make_async_remote_copy(
        src_ref=tokens_hbm.at[:, 0:EDGE],
        dst_ref=fields.at[:, HALO + length : HALO + length + EDGE],
        send_sem=token_edge_send.at[1],
        recv_sem=token_edge_recv.at[1],
        device_id=left,
        device_id_type=MESH,
    )

    @pl.when(in_first)
    def _():
        pl.when(has_right == 1)(tokens_right.start)
        pl.when(has_left == 1)(tokens_left.start)

    for r in range(rows):
        plane = masks[:, r, :].astype(F32)
        padded = jnp.concatenate([plane, jnp.zeros((128 - TAPS, length), F32)], axis=0)
        mask_columns[r * length : (r + 1) * length, :] = jnp.transpose(padded)

    def span(m):
        return pl.ds(pl.multiple_of(m * length, length), length)

    def tap_list(source, m, dilation):
        mask_rows = mask_columns[span(m), :]
        for k in range(TAPS):
            values = source[m, pl.ds(HALO + (k - CENTRE) * dilation, length), :]
            if k != CENTRE:
                lane = jnp.broadcast_to(mask_rows[:, k : k + 1], (length, 128)).astype(BF16)
                values = values * jnp.concatenate([lane] * (width // 128), axis=1)
            yield k, values

    def pass_copies(m):
        return (
            pltpu.make_async_remote_copy(
                src_ref=results.at[m],
                dst_ref=fields.at[m, own],
                send_sem=pass_send.at[m, 0],
                recv_sem=pass_recv.at[m, 0],
                device_id=(1, dp, seq),
                device_id_type=MESH,
            ),
            pltpu.make_async_remote_copy(
                src_ref=results.at[m, length - HALO : length],
                dst_ref=fields.at[m, 0:HALO],
                send_sem=pass_send.at[m, 1],
                recv_sem=pass_recv.at[m, 1],
                device_id=(1, dp, seq + 1),
                device_id_type=MESH,
            ),
            pltpu.make_async_remote_copy(
                src_ref=results.at[m, 0:HALO],
                dst_ref=fields.at[m, HALO + length : HALO + length + HALO],
                send_sem=pass_send.at[m, 2],
                recv_sem=pass_recv.at[m, 2],
                device_id=(1, dp, seq - 1),
                device_id_type=MESH,
            ),
        )

    def back_copy(m):
        return pltpu.make_async_remote_copy(
            src_ref=results.at[m],
            dst_ref=given.at[m],
            send_sem=back_send.at[m],
            recv_sem=back_recv.at[m],
            device_id=(0, dp, seq),
            device_id_type=MESH,
        )

    def edge_copies(m, reach):
        return (
            pltpu.make_async_remote_copy(
                src_ref=conv_grads.at[m, HALO + length - reach : HALO + length],
                dst_ref=conv_grads.at[m, HALO - reach : HALO],
                send_sem=edge_send.at[m, 0],
                recv_sem=edge_recv.at[m, 0],
                device_id=right,
                device_id_type=MESH,
            ),
            pltpu.make_async_remote_copy(
                src_ref=conv_grads.at[m, HALO : HALO + reach],
                dst_ref=conv_grads.at[m, HALO + length : HALO + length + reach],
                send_sem=edge_send.at[m, 1],
                recv_sem=edge_recv.at[m, 1],
                device_id=left,
                device_id_type=MESH,
            ),
        )

    def act_copy(m):
        return pltpu.make_async_copy(results.at[m], act_hbm.at[m], act_sem.at[m])

    def grads_copy(m):
        return pltpu.make_async_copy(mixed_grads.at[m], grads_hbm.at[m], grads_sem.at[m])

    loads[0].wait()
    loads[1].wait()
    loads[2].wait()

    @pl.when(in_first)
    def _():
        token_load.wait()
        pl.when(has_left == 1)(tokens_right.wait_recv)
        pl.when(has_right == 1)(tokens_left.wait_recv)

    gain_one, gain_two = gains[0:1, :], gains[1:2, :]
    shift_conv, shift_one = shifts[0:1, :], shifts[1:2, :]
    shift_ffn, shift_two = shifts[2:3, :], shifts[3:4, :]

    def forward(m, carry):
        here = span(m)

        @pl.when(in_second)
        def _():
            whole, low, high = pass_copies(m)
            whole.wait_recv()
            pl.when(has_left == 1)(low.wait_recv)
            pl.when(has_right == 1)(high.wait_recv)

        for flag, dilation in ((in_first, TIGHT), (in_second, WIDE)):

            @pl.when(flag)
            def _(dilation=dilation):
                for k, values in tap_list(fields, m, dilation):
                    taps[:, k * width : (k + 1) * width] = values

        value, slope = gelu_pair(dot(taps[...], conv_w[...]) + shift_conv)
        unit, scale = normalise(value)
        unit_one[here, :] = unit.astype(BF16)
        slope_one[here, :] = (slope * scale).astype(BF16)
        mixed = fields[m, own, :].astype(F32) + unit * gain_one + shift_one
        mixed_low = mixed.astype(BF16)
        slabs[2 * chunks, here, :] = mixed_low
        ffn = None
        for c in range(chunks):
            part = slice(c * width, (c + 1) * width)
            value, slope = gelu_pair(dot(mixed_low, up_w[:, part]) + bias[:, part])
            low = value.astype(BF16)
            slabs[c, here, :] = low
            slabs[chunks + c, here, :] = slope.astype(BF16)
            term = dot(low, down_w[part, :])
            ffn = term if ffn is None else ffn + term
        unit, scale = normalise(ffn + shift_ffn)
        unit_two[here, :] = unit.astype(BF16)
        scale_two[here, :] = jnp.broadcast_to(scale, (length, 128))
        results[m] = (mixed + unit * gain_two + shift_two).astype(BF16)
        act_copy(m).start()

        @pl.when(in_first)
        def _():
            whole, low, high = pass_copies(m)
            pl.when(has_right == 1)(low.start)
            pl.when(has_left == 1)(high.start)
            whole.start()

        return carry

    lax.fori_loop(0, rows, forward, 0)

    @pl.when(in_second)
    def _():
        given_load.wait()

    def backward_ffn(m, carry):
        here = span(m)

        @pl.when(in_first)
        def _():
            back_copy(m).wait_recv()

        grad = given[m].astype(F32)
        unit = unit_two[here, :].astype(F32)
        grad_ffn = norm_backward(grad * gain_two, unit) * scale_two[here, 0:1]
        sums[1:2, :] += column_sum(grad * unit)
        sums[5:6, :] += column_sum(grad)
        sums[4:5, :] += column_sum(grad_ffn)
        grad_ffn_low = grad_ffn.astype(BF16)
        ffn_grads[here, :] = grad_ffn_low
        mixed = grad
        for c in range(chunks):
            part = slice(c * width, (c + 1) * width)
            grad_hidden = dot_nt(grad_ffn_low, down_w[part, :]) * slabs[chunks + c, here, :].astype(F32)
            sums[8 + c : 9 + c, :] += column_sum(grad_hidden)
            low = grad_hidden.astype(BF16)
            slabs[chunks + c, here, :] = low
            mixed = mixed + dot_nt(low, up_w[:, part])
        mixed_grads[m] = mixed
        unit = unit_one[here, :].astype(F32)
        grad_conv = norm_backward(mixed * gain_one, unit) * slope_one[here, :].astype(F32)
        sums[0:1, :] += column_sum(mixed * unit)
        sums[3:4, :] += column_sum(mixed)
        sums[2:3, :] += column_sum(grad_conv)
        conv_grads[m, own, :] = grad_conv.astype(BF16)
        for flag, reach in ((in_first, EDGE), (in_second, HALO)):

            @pl.when(flag)
            def _(reach=reach):
                low, high = edge_copies(m, reach)
                pl.when(has_right == 1)(low.start)
                pl.when(has_left == 1)(high.start)

        return carry

    lax.fori_loop(0, rows, backward_ffn, 0)

    def sums_copy(i):
        return pltpu.make_async_remote_copy(
            src_ref=sums_sent.at[i],
            dst_ref=sums_arrived.at[i],
            send_sem=sums_send.at[i],
            recv_sem=sums_recv.at[i],
            device_id=partner(geo.all_bits[i]),
            device_id_type=MESH,
        )

    def sums_begin(i):
        sums_sent[i] = sums[...]
        sums_copy(i).start()

    def sums_end(i):
        sums_copy(i).wait_recv()
        sums[...] += sums_arrived[i]

    my_bits = [bit_of(bit) for bit in geo.bits]
    owners, share = geo.owners, geo.share

    def is_order(j, t):
        off = j % 6 - t
        return 1 - (off * off + 35) // 36

    def bit_weights(j):
        picked = [is_order(j, t) for t in range(6)]
        return [
            sum(picked[t] * (owners >> (1 + geo.orders[t].index(b))) for t in range(6))
            for b in range(geo.stages)
        ]

    def place(weights, owner_dp, owner_seq):
        where = 0
        for b, (axis, size) in enumerate(geo.bits):
            index = owner_dp if axis == "dp" else owner_seq * geo.low
            where = where + ((index // size) % 2 + my_bits[b]) % 2 * weights[b]
        return where

    def part_copy(j, i):
        half = owners >> (i + 1)
        picked = [is_order(j, t) for t in range(6)]
        to = {"dp": dp, "seq": seq}
        for b, (axis, size) in enumerate(geo.bits):
            chosen = sum(picked[t] for t in range(6) if geo.orders[t][i] == b)
            to[axis] = to[axis] + chosen * (1 - 2 * my_bits[b]) * size
        return pltpu.make_async_remote_copy(
            src_ref=partial.at[j, half : 2 * half],
            dst_ref=arrived.at[j, half : 2 * half],
            send_sem=part_send.at[j, i],
            recv_sem=part_recv.at[j, i],
            device_id=(section, to["dp"], to["seq"]),
            device_id_type=MESH,
        )

    def take(j, i):
        half = owners >> (i + 1)
        part_copy(j, i).wait_recv()
        return partial[j, 0:half].astype(F32) + arrived[j, half : 2 * half].astype(F32)

    def advance(j, i):
        half = owners >> i
        partial[j, 0:half] = take(j, i - 1).astype(BF16)
        part_copy(j, i).start()

    def finish(j):
        total = take(j, geo.stages - 1)[0]

        @pl.when(j < chunks)
        def _():
            up_out[:, pl.ds(pl.multiple_of(j * width, width), width)] = total

        @pl.when((j >= chunks) & (j < 2 * chunks))
        def _():
            down_out[pl.ds(pl.multiple_of((j - chunks) * share, share), share), :] = total

        @pl.when(j >= 2 * chunks)
        def _():
            conv_out[j - 2 * chunks] = total

    down_turn = 2 * chunks - 1
    conv_turn = 2 * chunks + rows
    end_turn = conv_turn + TAPS

    def at_turn(turn, act):
        pl.when((turn >= 0) & (turn < chunks))(lambda: act(turn))
        pl.when((turn >= down_turn) & (turn < down_turn + chunks))(lambda: act(turn - down_turn + chunks))
        pl.when((turn >= conv_turn) & (turn < end_turn))(lambda: act(turn - conv_turn + 2 * chunks))

    def events(turn):
        at_turn(turn - geo.last_lag, finish)
        for i in range(geo.stages - 1, 0, -1):
            at_turn(turn - geo.lags[i], lambda j, i=i: advance(j, i))

    def row_slice(j, grad):
        weights = bit_weights(j)
        for owner in range(owners):
            where = place(weights, owner // (geo.seq // geo.low), owner % (geo.seq // geo.low))
            partial[j, where] = grad[owner * share : (owner + 1) * share].astype(BF16)
        part_copy(j, 0).start()

    def up_slice(j, carry):
        row_slice(j, dot_tn(slabs[2 * chunks], slabs[chunks + j]))
        events(j)
        return carry

    def down_slab(c, carry):
        grad = dot_tn(slabs[c], ffn_grads[...])
        each = owners // chunks
        per_dp = geo.seq // geo.low
        for jj in range(chunks):
            weights = bit_weights(chunks + jj)
            for w in range(each):
                owner = c * each + w
                where = place(weights, owner // per_dp, owner % per_dp)
                at = (w * chunks + jj) * share
                partial[chunks + jj, where] = grad[at : at + share].astype(BF16)

        @pl.when(c == chunks - 1)
        def _():
            for jj in range(chunks):
                part_copy(chunks + jj, 0).start()

        events(chunks + c)
        return carry

    sums_begin(0)
    lax.fori_loop(0, chunks, up_slice, 0)
    sums_end(0)
    sums_begin(1)
    lax.fori_loop(0, chunks, down_slab, 0)
    sums_end(1)
    sums_begin(2)

    def settle_forward(m, carry):
        act_copy(m).wait()

        @pl.when(in_first)
        def _():
            whole, low, high = pass_copies(m)
            pl.when(has_right == 1)(low.wait_send)
            pl.when(has_left == 1)(high.wait_send)
            whole.wait_send()

        return carry

    lax.fori_loop(0, rows, settle_forward, 0)

    def backward_conv(m, carry):
        here = span(m)
        for flag, dilation, reach in ((in_first, TIGHT, EDGE), (in_second, WIDE, HALO)):

            @pl.when(flag)
            def _(dilation=dilation, reach=reach):
                low, high = edge_copies(m, reach)
                pl.when(has_left == 1)(low.wait_recv)
                pl.when(has_right == 1)(high.wait_recv)
                for k, values in tap_list(conv_grads, m, dilation):
                    slabs[TAPS - 1 - k, here, :] = values

        grad = mixed_grads[m]
        for k in range(TAPS):
            grad = grad + dot_nt(slabs[k, here, :], conv_w[k * width : (k + 1) * width, :])
        mixed_grads[m] = grad

        @pl.when(in_second)
        def _():
            low = grad.astype(BF16)
            results[m] = low
            back_copy(m).start()
            mixed_grads[m] = low.astype(F32)

        grads_copy(m).start()
        events(2 * chunks + m)
        return carry

    lax.fori_loop(0, rows, backward_conv, 0)
    sums_end(2)
    if len(geo.all_bits) > 3:
        sums_begin(3)

    def gather_fields(m, carry):
        ffn_grads[span(m), :] = fields[m, own, :]
        return carry

    lax.fori_loop(0, rows, gather_fields, 0)

    def conv_slice(k, carry):
        j = 2 * chunks + k
        row_slice(j, dot_tn(ffn_grads[...], slabs[k]))
        events(conv_turn + k)
        return carry

    lax.fori_loop(0, TAPS, conv_slice, 0)
    for i in range(3, len(geo.all_bits)):
        sums_end(i)
        if i + 1 < len(geo.all_bits):
            sums_begin(i + 1)

    index = dp * geo.seq + seq
    lane = lax.broadcasted_iota(jnp.int32, (128, width), 1)
    line = lax.broadcasted_iota(jnp.int32, (128, width), 0)
    exact = functools.partial(
        lax.dot_general,
        dimension_numbers=(((1,), (1,)), ((), ())),
        precision=lax.Precision.HIGHEST,
        preferred_element_type=F32,
    )
    picked = exact(sums[...], (lane == line + index * geo.final_share).astype(F32))
    gain_out[...] = picked[0:2, : geo.final_share]
    shift_out[...] = picked[2:6, : geo.final_share]
    start = index * geo.bias_share
    picked = exact(sums[...], (lane == line + start % width).astype(F32))
    wanted = lax.broadcasted_iota(jnp.int32, picked.shape, 0) == 8 + start // width
    bias_out[...] = column_sum(jnp.where(wanted, picked, 0.0))[:, : geo.bias_share]

    def drain(turn, carry):
        events(turn)
        return carry

    lax.fori_loop(end_turn, end_turn + geo.last_lag, drain, 0)

    def settle_slice(j, carry):
        for i in range(geo.stages):
            part_copy(j, i).wait_send()
        return carry

    lax.fori_loop(0, geo.slices, settle_slice, 0)
    for i in range(len(geo.all_bits)):
        sums_copy(i).wait_send()

    def settle_row(m, carry):
        grads_copy(m).wait()
        for flag, reach in ((in_first, EDGE), (in_second, HALO)):

            @pl.when(flag)
            def _(reach=reach):
                low, high = edge_copies(m, reach)
                pl.when(has_right == 1)(low.wait_send)
                pl.when(has_left == 1)(high.wait_send)

        pl.when(in_second)(back_copy(m).wait_send)
        return carry

    lax.fori_loop(0, rows, settle_row, 0)

    @pl.when(in_first)
    def _():
        pl.when(has_right == 1)(tokens_right.wait_send)
        pl.when(has_left == 1)(tokens_left.wait_send)


def per_device(
    dp,
    seq,
    tokens,
    cotangent,
    tap_masks,
    conv_weight,
    up_weight,
    up_bias,
    down_weight,
    norm_gains,
    shift_terms,
):
    rows, length, width = tokens.shape
    hidden = up_weight.shape[2]
    geo = Geometry(dp, seq, rows, length, width, hidden)
    reach = length + 2 * HALO
    vmem = pl.BlockSpec(memory_space=pltpu.VMEM)
    hbm = pl.BlockSpec(memory_space=pl.ANY)
    dma = pltpu.SemaphoreType.DMA
    stages = len(geo.all_bits)
    slices = (geo.slices, geo.owners, geo.share, width)
    act, grads, conv_grad, up_grad, down_grad, bias_grad, gain_grad, shift_grad = pl.pallas_call(
        functools.partial(body, geo),
        out_shape=[
            jax.ShapeDtypeStruct((rows, length, width), BF16),
            jax.ShapeDtypeStruct((rows, length, width), F32),
            jax.ShapeDtypeStruct((TAPS, geo.share, width), F32),
            jax.ShapeDtypeStruct((geo.share, hidden), F32),
            jax.ShapeDtypeStruct((geo.chunks * geo.share, width), F32),
            jax.ShapeDtypeStruct((1, geo.bias_share), F32),
            jax.ShapeDtypeStruct((2, geo.final_share), F32),
            jax.ShapeDtypeStruct((4, geo.final_share), F32),
        ],
        in_specs=[hbm] * 5 + [vmem] * 4,
        out_specs=[hbm] * 2 + [vmem] * 6,
        scratch_shapes=[
            pltpu.VMEM((rows, reach, width), BF16),
            pltpu.VMEM((rows, reach, width), BF16),
            pltpu.VMEM((TAPS * width, width), BF16),
            pltpu.VMEM((width, hidden), BF16),
            pltpu.VMEM((hidden, width), BF16),
            pltpu.VMEM((TAPS, geo.tokens, width), BF16),
            pltpu.VMEM((length, TAPS * width), BF16),
            pltpu.VMEM((geo.tokens, width), BF16),
            pltpu.VMEM((geo.tokens, width), BF16),
            pltpu.VMEM((geo.tokens, width), BF16),
            pltpu.VMEM((geo.tokens, 128), F32),
            pltpu.VMEM((rows, length, width), F32),
            pltpu.VMEM((rows, length, width), BF16),
            pltpu.VMEM((geo.tokens, width), BF16),
            pltpu.VMEM((rows, length, width), BF16),
            pltpu.VMEM((geo.tokens, 128), F32),
            pltpu.VMEM(slices, BF16),
            pltpu.VMEM(slices, BF16),
            pltpu.VMEM((16, width), F32),
            pltpu.VMEM((stages, 16, width), F32),
            pltpu.VMEM((stages, 16, width), F32),
            dma((3,)),
            dma((2,)),
            dma((2,)),
            dma((2,)),
            dma((rows, 3)),
            dma((rows, 3)),
            dma((rows,)),
            dma((rows,)),
            dma((rows, 2)),
            dma((rows, 2)),
            dma((rows,)),
            dma((rows,)),
            dma((geo.slices, geo.stages)),
            dma((geo.slices, geo.stages)),
            dma((stages,)),
            dma((stages,)),
        ],
        compiler_params=pltpu.CompilerParams(
            collective_id=0, has_side_effects=True, vmem_limit_bytes=63 * 2**20
        ),
    )(
        tokens,
        cotangent,
        jnp.transpose(conv_weight[0], (1, 0, 2)).reshape(TAPS * width, width),
        up_weight[0],
        down_weight[0],
        tap_masks[0],
        up_bias,
        jnp.transpose(norm_gains[0]),
        jnp.transpose(shift_terms[0]),
    )
    conv_grad = jnp.transpose(conv_grad, (1, 0, 2))
    if geo.low > 1:
        groups = [list(range(at, at + geo.low)) for at in range(0, seq, geo.low)]
        conv_grad, up_grad, down_grad = (
            lax.psum_scatter(
                grad, "seq", scatter_dimension=0, axis_index_groups=groups, tiled=True
            )
            for grad in (conv_grad, up_grad, down_grad)
        )
    return (
        act[None],
        grads[None],
        conv_grad[None],
        up_grad[None],
        bias_grad,
        down_grad[None],
        jnp.transpose(gain_grad)[None],
        jnp.transpose(shift_grad)[None],
    )


def solution(mesh):
    placed = (
        P("dp", "seq", None),
        P("dp", "seq", None),
        P("section", None, "dp", "seq"),
        P("section", None, None, None),
        P("section", None, None),
        P("section", None),
        P("section", None, None),
        P("section", None, None),
        P("section", None, None),
    )
    return jax.shard_map(
        functools.partial(per_device, mesh.shape["dp"], mesh.shape["seq"]),
        mesh=mesh,
        in_specs=placed,
        out_specs=(
            P("section", "dp", "seq", None),
            P("section", "dp", "seq", None),
            P("section", ("dp", "seq"), None, None),
            P("section", ("dp", "seq"), None),
            P("section", ("dp", "seq")),
            P("section", ("dp", "seq"), None),
            P("section", ("dp", "seq"), None),
            P("section", ("dp", "seq"), None),
        ),
        check_vma=False,
    )
```

```python
import functools

import jax
import jax.numpy as jnp
from jax import lax
from jax.experimental import pallas as pl
from jax.experimental.pallas import tpu as pltpu
from jax.sharding import PartitionSpec as P

TAPS = 9
CENTRE = TAPS // 2
TIGHT = 2
WIDE = 32
HALO = CENTRE * WIDE
EDGE = 16
EPS = 1e-05
MESH = pl.DeviceIdType.MESH
BF16 = jnp.bfloat16
F32 = jnp.float32
LAG = 4
CONV_DELAY = 0
TANH_SCALE = 0.7978845608028654
TANH_CUBE = TANH_SCALE * 0.044715


def gelu_pair(z):
    square = z * z
    half = 0.5 + 0.5 * jnp.tanh(z * (TANH_SCALE + TANH_CUBE * square))
    value = z * half
    return value, half + value * (1.0 - half) * (2.0 * TANH_SCALE + 6.0 * TANH_CUBE * square)


def normalise(values):
    centred = values - jnp.mean(values, axis=-1, keepdims=True)
    scale = lax.rsqrt(jnp.mean(centred * centred, axis=-1, keepdims=True) + EPS)
    return centred * scale, scale


def norm_backward(weighted, unit):
    return (
        weighted
        - jnp.mean(weighted, axis=-1, keepdims=True)
        - unit * jnp.mean(weighted * unit, axis=-1, keepdims=True)
    )


def column_sum(values):
    return jnp.sum(values, axis=0, keepdims=True)


def dot(a, b):
    return jnp.dot(a, b, preferred_element_type=F32)


def dot_nt(a, b):
    return lax.dot_general(a, b, (((1,), (1,)), ((), ())), preferred_element_type=F32)


def dot_tn(a, b):
    return lax.dot_general(a, b, (((0,), (0,)), ((), ())), preferred_element_type=F32)


class Geometry:
    def __init__(self, dp, seq, rows, length, width, hidden):
        self.dp, self.seq = dp, seq
        self.rows, self.length, self.width = rows, length, width
        self.tokens = rows * length
        self.chunks = hidden // width
        self.low = max(1, 16 * dp * seq // width)
        self.owners = dp * seq // self.low
        self.share = width // self.owners
        self.final_share = width // (dp * seq)
        self.bias_share = hidden // (dp * seq)
        dp_bits = [("dp", 1 << i) for i in range(dp.bit_length() - 1)]
        seq_all = [("seq", 1 << i) for i in range(seq.bit_length() - 1)]
        seq_bits = [bit for bit in seq_all if bit[1] >= self.low]
        self.bits = dp_bits + seq_bits
        self.all_bits = dp_bits + seq_all
        self.pairs = (TAPS + 1) // 2
        self.slices = 2 * self.chunks + self.pairs
        halvings = [(bit,) for bit in dp_bits]
        lines = [tuple(seq_bits[i : i + 2]) for i in range(0, len(seq_bits), 2)]
        across = halvings + lines
        back = halvings[::-1] + lines
        rest = halvings[1:] + lines + halvings[:1]
        rest_along = lines + halvings[1:] + halvings[:1]
        ffn = [across, back, across, back, across, across, back, across]
        conv = [rest, rest_along]
        self.orders = [ffn[j % len(ffn)] for j in range(2 * self.chunks)]
        self.orders += [conv[k % 2] for k in range(self.pairs)]
        self.stages = len(across)
        self.flips = [(bit,) for bit in self.all_bits] + [line for line in lines if len(line) > 1]


def body(
    geo,
    tokens_hbm,
    cotangent_hbm,
    conv_hbm,
    up_hbm,
    down_hbm,
    masks,
    bias,
    gains,
    shifts,
    act_hbm,
    grads_hbm,
    conv_out,
    up_out,
    down_out,
    bias_out,
    gain_out,
    shift_out,
    fields,
    fields_other,
    conv_grads,
    near_edges,
    conv_w,
    up_w,
    down_w,
    slabs,
    taps,
    halves,
    unit_one,
    slope_one,
    unit_two,
    scale_two,
    mixed_grads,
    given,
    ffn_grads,
    results,
    masks_other,
    masks_second,
    columns,
    columns_other,
    columns_second,
    partial,
    arrived,
    sums,
    sums_sent,
    sums_arrived,
    load_sem,
    row_load_sem,
    token_edge_send,
    token_edge_recv,
    masks_send,
    masks_recv,
    pass_send,
    pass_recv,
    field_send,
    field_recv,
    weight_send,
    weight_recv,
    back_send,
    back_recv,
    half_send,
    half_recv,
    near_send,
    near_recv,
    act_sem,
    grads_sem,
    grads_send,
    grads_recv,
    part_send,
    part_recv,
    sums_send,
    sums_recv,
):
    rows, length, width, chunks = geo.rows, geo.length, geo.width, geo.chunks
    tokens, half_width = geo.tokens, geo.width // 2
    section = lax.axis_index("section")
    dp = lax.axis_index("dp")
    seq = lax.axis_index("seq")
    mine = {"dp": dp, "seq": seq}
    in_first = section == 0
    in_second = section == 1
    has_left = (seq + geo.seq - 1) // geo.seq
    has_right = 1 - (seq + 1) // geo.seq
    on_left, on_right = has_left == 1, has_right == 1
    own = slice(HALO, HALO + length)
    near = slice(HALO - EDGE, HALO + length + EDGE)

    def bit_of(bit):
        axis, size = bit
        return (mine[axis] // size) % 2

    def partner(*flips):
        to = dict(mine)
        for axis, size in flips:
            to[axis] = to[axis] + (1 - 2 * bit_of((axis, size))) * size
        return (section, to["dp"], to["seq"])

    def remote(source, target, sends, receives, device):
        return pltpu.make_async_remote_copy(
            src_ref=source,
            dst_ref=target,
            send_sem=sends,
            recv_sem=receives,
            device_id=device,
            device_id_type=MESH,
        )

    core = (1 - section, dp, seq)
    left, right = (section, dp, seq - 1), (section, dp, seq + 1)
    first_core, second_core = (0, dp, seq), (1, dp, seq)
    pair_bit = geo.bits[0]
    pair = partner(pair_bit)
    my_half = bit_of(pair_bit)
    mine_at = pl.ds(pl.multiple_of(my_half * half_width, half_width), half_width)
    other_at = pl.ds(pl.multiple_of((1 - my_half) * half_width, half_width), half_width)

    loads = [
        pltpu.make_async_copy(conv_hbm, conv_w, load_sem.at[0]),
        pltpu.make_async_copy(up_hbm, up_w, load_sem.at[1]),
        pltpu.make_async_copy(down_hbm, down_w, load_sem.at[2]),
    ]
    token_load = pltpu.make_async_copy(tokens_hbm, fields.at[:, own], row_load_sem.at[0])
    given_load = pltpu.make_async_copy(cotangent_hbm, given, row_load_sem.at[1])
    pl.when(in_first)(token_load.start)
    for load in loads:
        load.start()
    pl.when(in_second)(given_load.start)

    @pl.when(has_left == 0)
    def _():
        fields[:, :HALO] = jnp.zeros((rows, HALO, width), BF16)
        conv_grads[:, :HALO] = jnp.zeros((rows, HALO, width), BF16)

    @pl.when(has_right == 0)
    def _():
        fields[:, HALO + length :] = jnp.zeros((rows, HALO, width), BF16)
        conv_grads[:, HALO + length :] = jnp.zeros((rows, HALO, width), BF16)

    sums[...] = jnp.zeros(sums.shape, F32)

    barrier = pltpu.get_barrier_semaphore()

    def greet(device):
        pl.semaphore_signal(barrier, inc=1, device_id=device, device_id_type=MESH)

    for flips in geo.flips:
        greet(partner(*flips))
    greet(core)
    for flag, at in ((on_left, seq - 1), (on_right, seq + 1)):

        @pl.when(flag)
        def _(at=at):
            greet((section, dp, at))
            greet((1 - section, dp, at))

    pl.semaphore_wait(barrier, len(geo.flips) + 1 + 2 * has_left + 2 * has_right)

    tokens_right = remote(
        tokens_hbm.at[:, length - EDGE : length],
        fields.at[:, HALO - EDGE : HALO],
        token_edge_send.at[0],
        token_edge_recv.at[0],
        right,
    )
    tokens_left = remote(
        tokens_hbm.at[:, 0:EDGE],
        fields.at[:, HALO + length : HALO + length + EDGE],
        token_edge_send.at[1],
        token_edge_recv.at[1],
        left,
    )

    @pl.when(in_first)
    def _():
        pl.when(on_right)(tokens_right.start)
        pl.when(on_left)(tokens_left.start)

    masks_across = remote(masks, masks_other, masks_send.at[0], masks_recv.at[0], pair)
    masks_back = remote(masks, masks_second, masks_send.at[1], masks_recv.at[1], first_core)
    masks_across.start()
    pl.when(in_second)(masks_back.start)

    def to_columns(source, target):
        for r in range(rows):
            plane = source[:, r, :].astype(F32)
            padded = jnp.concatenate([plane, jnp.zeros((128 - TAPS, length), F32)], axis=0)
            target[r * length : (r + 1) * length, :] = jnp.transpose(padded)

    to_columns(masks, columns)

    def span(m):
        return pl.ds(pl.multiple_of(m * length, length), length)

    def one_tap(source, mask_columns, m, k, dilation):
        values = source[m, pl.ds(HALO + (k - CENTRE) * dilation, length), :]
        if k == CENTRE:
            return values
        lane = jnp.broadcast_to(mask_columns[span(m), k : k + 1], (length, 128)).astype(BF16)
        return values * jnp.concatenate([lane] * (width // 128), axis=1)

    def pass_copies(m):
        return (
            remote(results.at[m], fields.at[m, own], pass_send.at[m, 0], pass_recv.at[m, 0], second_core),
            remote(
                results.at[m, length - HALO : length],
                fields.at[m, 0:HALO],
                pass_send.at[m, 1],
                pass_recv.at[m, 1],
                (1, dp, seq + 1),
            ),
            remote(
                results.at[m, 0:HALO],
                fields.at[m, HALO + length : HALO + length + HALO],
                pass_send.at[m, 2],
                pass_recv.at[m, 2],
                (1, dp, seq - 1),
            ),
        )

    def back_copies(m):
        return (
            remote(conv_grads.at[m, own], conv_grads.at[m, own], back_send.at[m, 0], back_recv.at[m, 0], first_core),
            remote(mixed_grads.at[m], mixed_grads.at[m], back_send.at[m, 1], back_recv.at[m, 1], first_core),
            remote(
                conv_grads.at[m, HALO + length - HALO : HALO + length],
                conv_grads.at[m, 0:HALO],
                back_send.at[m, 2],
                back_recv.at[m, 2],
                (0, dp, seq + 1),
            ),
            remote(
                conv_grads.at[m, HALO : HALO + HALO],
                conv_grads.at[m, HALO + length : HALO + length + HALO],
                back_send.at[m, 3],
                back_recv.at[m, 3],
                (0, dp, seq - 1),
            ),
        )

    def near_copies(m):
        return (
            remote(
                conv_grads.at[m, HALO + length - EDGE : HALO + length],
                near_edges.at[m, 0],
                near_send.at[m, 0],
                near_recv.at[m, 0],
                right,
            ),
            remote(
                conv_grads.at[m, HALO : HALO + EDGE],
                near_edges.at[m, 1],
                near_send.at[m, 1],
                near_recv.at[m, 1],
                left,
            ),
        )

    def field_copy(m):
        return remote(fields.at[m], fields_other.at[m], field_send.at[m], field_recv.at[m], pair)

    near_fields = remote(
        fields.at[:, near], fields_other.at[:, near], field_send.at[0], field_recv.at[0], pair
    )

    def half_copy(m):
        return remote(
            conv_grads.at[m, own, other_at],
            halves.at[pl.ds(pl.multiple_of(tokens + m * length, length), length)],
            half_send.at[m],
            half_recv.at[m],
            pair,
        )

    weight_copy = remote(conv_w, conv_w, weight_send, weight_recv, first_core)

    def act_copy(m):
        return pltpu.make_async_copy(results.at[m], act_hbm.at[m], act_sem.at[m])

    def grads_copy(m):
        return pltpu.make_async_copy(mixed_grads.at[m], grads_hbm.at[m], grads_sem.at[m])

    def grads_across(m):
        return remote(mixed_grads.at[m], grads_hbm.at[m], grads_send.at[m], grads_recv.at[m], second_core)

    for load in loads:
        load.wait()

    @pl.when(in_first)
    def _():
        token_load.wait()
        pl.when(on_left)(tokens_right.wait_recv)
        pl.when(on_right)(tokens_left.wait_recv)
        near_fields.start()

    gain_one, gain_two = gains[0:1, :], gains[1:2, :]
    shift_conv, shift_one = shifts[0:1, :], shifts[1:2, :]
    shift_ffn, shift_two = shifts[2:3, :], shifts[3:4, :]

    def forward(m, carry):
        here = span(m)

        @pl.when(in_second)
        def _():
            whole, low, high = pass_copies(m)
            whole.wait_recv()
            pl.when(on_left)(low.wait_recv)
            pl.when(on_right)(high.wait_recv)
            field_copy(m).start()
            pl.when(m == rows - 1)(weight_copy.start)

        for flag, dilation in ((in_first, TIGHT), (in_second, WIDE)):

            @pl.when(flag)
            def _(dilation=dilation):
                for k in range(TAPS):
                    taps[:, k * width : (k + 1) * width] = one_tap(fields, columns, m, k, dilation)

        value, slope = gelu_pair(dot(taps[...], conv_w[...]) + shift_conv)
        unit, scale = normalise(value)
        unit_one[here, :] = unit.astype(BF16)
        slope_one[here, :] = (slope * scale).astype(BF16)
        mixed = fields[m, own, :].astype(F32) + unit * gain_one + shift_one
        mixed_low = mixed.astype(BF16)
        slabs[2 * chunks, here, :] = mixed_low
        ffn = None
        for c in range(chunks):
            part = slice(c * width, (c + 1) * width)
            value, slope = gelu_pair(dot(mixed_low, up_w[:, part]) + bias[:, part])
            low = value.astype(BF16)
            slabs[c, here, :] = low
            slabs[chunks + c, here, :] = slope.astype(BF16)
            term = dot(low, down_w[part, :])
            ffn = term if ffn is None else ffn + term
        unit, scale = normalise(ffn + shift_ffn)
        unit_two[here, :] = unit.astype(BF16)
        scale_two[here, :] = jnp.broadcast_to(scale, (length, 128))
        results[m] = (mixed + unit * gain_two + shift_two).astype(BF16)
        act_copy(m).start()

        @pl.when(in_first)
        def _():
            whole, low, high = pass_copies(m)
            pl.when(on_right)(low.start)
            pl.when(on_left)(high.start)
            whole.start()

        return carry

    lax.fori_loop(0, rows, forward, 0)

    masks_across.wait_recv()
    to_columns(masks_other, columns_other)

    @pl.when(in_first)
    def _():
        masks_back.wait_recv()
        to_columns(masks_second, columns_second)

    def conv_back(m, mask_columns, dilation):
        grad = mixed_grads[m]
        for k in range(TAPS):
            at = (TAPS - 1 - k) * width
            grad = grad + dot_nt(one_tap(conv_grads, mask_columns, m, k, dilation), conv_w[at : at + width, :])
        return grad

    def second_input(m, carry):
        whole, sides, low, high = back_copies(m)
        whole.wait_recv()
        sides.wait_recv()
        pl.when(on_left)(low.wait_recv)
        pl.when(on_right)(high.wait_recv)
        low = conv_back(m, columns_second, WIDE).astype(BF16)
        given[m] = low
        mixed_grads[m] = low.astype(F32)
        grads_across(m).start()
        return carry

    @pl.when(in_first)
    def _():
        weight_copy.wait_recv()
        lax.fori_loop(0, rows, second_input, 0)
        loads[0].start()

    pl.when(in_second)(given_load.wait)

    def backward_ffn(m, carry):
        here = span(m)
        grad = given[m].astype(F32)
        unit = unit_two[here, :].astype(F32)
        grad_ffn = norm_backward(grad * gain_two, unit) * scale_two[here, 0:1]
        sums[1:2, :] += column_sum(grad * unit)
        sums[5:6, :] += column_sum(grad)
        sums[4:5, :] += column_sum(grad_ffn)
        grad_ffn_low = grad_ffn.astype(BF16)
        ffn_grads[here, :] = grad_ffn_low
        mixed = grad
        for c in range(chunks):
            part = slice(c * width, (c + 1) * width)
            grad_hidden = dot_nt(grad_ffn_low, down_w[part, :]) * slabs[chunks + c, here, :].astype(F32)
            sums[8 + c : 9 + c, :] += column_sum(grad_hidden)
            low = grad_hidden.astype(BF16)
            slabs[chunks + c, here, :] = low
            mixed = mixed + dot_nt(low, up_w[:, part])
        pl.when(in_first)(grads_across(m).wait_send)
        mixed_grads[m] = mixed
        unit = unit_one[here, :].astype(F32)
        grad_conv = norm_backward(mixed * gain_one, unit) * slope_one[here, :].astype(F32)
        sums[0:1, :] += column_sum(mixed * unit)
        sums[3:4, :] += column_sum(mixed)
        sums[2:3, :] += column_sum(grad_conv)
        conv_grads[m, own, :] = grad_conv.astype(BF16)

        @pl.when(in_second)
        def _():
            whole, sides, low, high = back_copies(m)
            pl.when(on_right)(low.start)
            pl.when(on_left)(high.start)
            whole.start()
            sides.start()

        @pl.when(in_first)
        def _():
            low, high = near_copies(m)
            pl.when(on_right)(low.start)
            pl.when(on_left)(high.start)

        half_copy(m).start()
        halves[here, :] = conv_grads[m, own, mine_at]
        return carry

    lax.fori_loop(0, rows, backward_ffn, 0)

    def sums_copy(i):
        return remote(
            sums_sent.at[i], sums_arrived.at[i], sums_send.at[i], sums_recv.at[i], partner(geo.all_bits[i])
        )

    def sums_begin(i):
        sums_sent[i] = sums[...]
        sums_copy(i).start()

    def sums_end(i):
        sums_copy(i).wait_recv()
        sums[...] += sums_arrived[i]

    owners, share, stages = geo.owners, geo.share, geo.stages
    my_bits = {bit: bit_of(bit) for bit in geo.bits}
    peers = {}

    def columns_of(j):
        single = j == geo.slices - 1 and TAPS % 2 == 1
        return slice(0, half_width) if single else slice(0, width)

    def is_conv(j):
        return j >= 2 * chunks

    def place(j, owner_dp, owner_seq):
        where = 0
        weight = owners
        for axis, size in sum(geo.orders[j], ()):
            weight //= 2
            index = owner_dp if axis == "dp" else owner_seq * geo.low
            where = where + ((index // size) % 2 + my_bits[axis, size]) % 2 * weight
        return where

    def left_after(j, i):
        return owners >> len(sum(geo.orders[j][: i + 1], ()))

    def part_copies(j, i):
        bits, piece = geo.orders[j][i], left_after(j, i)
        copies = []
        for q in range(1, 1 << len(bits)):
            flips = tuple(bit for n, bit in enumerate(bits) if (q >> (len(bits) - 1 - n)) % 2)
            if flips not in peers:
                peers[flips] = partner(*flips)
            at = q * piece
            copies.append(
                remote(
                    partial.at[j, at : at + piece, :, columns_of(j)],
                    arrived.at[j, at : at + piece, :, columns_of(j)],
                    part_send.at[j, at],
                    part_recv.at[j, at],
                    peers[flips],
                )
            )
        return copies

    def send(j, i):
        for copy in part_copies(j, i):
            copy.start()

    def receive(j, i):
        for copy in part_copies(j, i):
            copy.wait_recv()

    def total_of(j, i):
        piece, at = left_after(j, i), columns_of(j)
        total = partial[j, 0:piece, :, at].astype(F32)
        for q in range(1, 1 << len(geo.orders[j][i])):
            total = total + arrived[j, q * piece : (q + 1) * piece, :, at].astype(F32)
        return total

    def advance(j, i):
        receive(j, i - 1)
        partial[j, 0 : left_after(j, i - 1), :, columns_of(j)] = total_of(j, i - 1).astype(BF16)
        send(j, i)

    def finish(j):
        receive(j, stages - 1)
        if not is_conv(j):
            total = total_of(j, stages - 1)[0]
            if j < chunks:
                up_out[:, j * width : (j + 1) * width] = total
            else:
                down_out[(j - chunks) * share : (j - chunks + 1) * share, :] = total
            return
        for q in range(2):
            k = 2 * (j - 2 * chunks) + q
            if k < TAPS:
                at = slice(q * half_width, (q + 1) * half_width)
                conv_out[k, :, mine_at] = partial[j, 0, :, at].astype(F32)
                conv_out[k, :, other_at] = arrived[j, 1, :, at].astype(F32)

    per_dp = geo.seq // geo.low

    def up_slice(j):
        grad = dot_tn(slabs[2 * chunks], slabs[chunks + j])
        for owner in range(owners):
            where = place(j, owner // per_dp, owner % per_dp)
            partial[j, where] = grad[owner * share : (owner + 1) * share].astype(BF16)
        send(j, 0)

    def down_slab(c):
        grad = dot_tn(slabs[c], ffn_grads[...])
        each = owners // chunks
        for jj in range(chunks):
            for w in range(each):
                owner = c * each + w
                where = place(chunks + jj, owner // per_dp, owner % per_dp)
                at = (w * chunks + jj) * share
                partial[chunks + jj, where] = grad[at : at + share].astype(BF16)
        if c == chunks - 1:
            for jj in range(chunks):
                send(chunks + jj, 0)

    def conv_slice(p):
        j = 2 * chunks + p
        if p == 0:
            for m in range(rows):
                half_copy(m).wait_recv()
            pl.when(in_first)(near_fields.wait_recv)

            @pl.when(in_second)
            def _():
                for m in range(rows):
                    field_copy(m).wait_recv()

        for q in range(2):
            k = 2 * p + q
            if k >= TAPS:
                continue
            at = slice(q * half_width, (q + 1) * half_width)
            places = [place(j, owner // per_dp, owner % per_dp) for owner in range(owners)]
            for flag, dilation in ((in_first, TIGHT), (in_second, WIDE)):

                @pl.when(flag)
                def _(dilation=dilation):
                    grad = None
                    for source, mask_columns, base in ((fields, columns, 0), (fields_other, columns_other, tokens)):
                        for m in range(rows):
                            low = base + m * length
                            values = one_tap(source, mask_columns, m, k, dilation)
                            term = dot_tn(values, halves[low : low + length, :])
                            grad = term if grad is None else grad + term
                    for owner in range(owners):
                        partial[j, places[owner], :, at] = grad[owner * share : (owner + 1) * share].astype(BF16)
        send(j, 0)

    def first_input(m):
        low, high = near_copies(m)

        @pl.when(on_left)
        def _():
            low.wait_recv()
            conv_grads[m, HALO - EDGE : HALO, :] = near_edges[m, 0]

        @pl.when(on_right)
        def _():
            high.wait_recv()
            conv_grads[m, HALO + length : HALO + length + EDGE, :] = near_edges[m, 1]

        if m == 0:
            loads[0].wait()
        mixed_grads[m] = conv_back(m, columns, TIGHT)
        grads_copy(m).start()

    def share_sums():
        index = dp * geo.seq + seq
        lane = lax.broadcasted_iota(jnp.int32, (128, width), 1)
        line = lax.broadcasted_iota(jnp.int32, (128, width), 0)
        exact = functools.partial(
            lax.dot_general,
            dimension_numbers=(((1,), (1,)), ((), ())),
            precision=lax.Precision.HIGHEST,
            preferred_element_type=F32,
        )
        picked = exact(sums[...], (lane == line + index * geo.final_share).astype(F32))
        gain_out[...] = picked[0:2, : geo.final_share]
        shift_out[...] = picked[2:6, : geo.final_share]
        start = index * geo.bias_share
        picked = exact(sums[...], (lane == line + start % width).astype(F32))
        wanted = lax.broadcasted_iota(jnp.int32, picked.shape, 0) == 8 + start // width
        bias_out[...] = column_sum(jnp.where(wanted, picked, 0.0))[:, : geo.bias_share]

    work = [functools.partial(up_slice, j) for j in range(chunks)]
    work += [functools.partial(down_slab, c) for c in range(chunks)]
    work += [functools.partial(conv_slice, p) for p in range(geo.pairs)]
    work += [lambda m=m: pl.when(in_first)(lambda: first_input(m)) for m in range(rows)]
    starts = list(range(chunks)) + [2 * chunks - 1 + jj for jj in range(chunks)]
    starts += [2 * chunks + CONV_DELAY + p for p in range(geo.pairs)]
    due = {}
    for j, start in enumerate(starts):
        for i in range(1, stages + 1):
            due.setdefault(start + LAG * i, []).append((j, i))
    sum_turns = {4 + 2 * i: i for i in range(len(geo.all_bits))}
    sums_begin(0)
    for turn in range(max(max(due), max(sum_turns), len(work) - 1) + 1):
        if turn < len(work):
            work[turn]()
        for j, i in due.get(turn, ()):
            if i < stages:
                advance(j, i)
            else:
                finish(j)
        if turn in sum_turns:
            i = sum_turns[turn]
            sums_end(i)
            if i + 1 < len(geo.all_bits):
                sums_begin(i + 1)
            else:
                share_sums()

    for j in range(geo.slices):
        for i in range(stages):
            for copy in part_copies(j, i):
                copy.wait_send()
    for i in range(len(geo.all_bits)):
        sums_copy(i).wait_send()
    masks_across.wait_send()

    def settle_row(m, carry):
        act_copy(m).wait()
        half_copy(m).wait_send()

        @pl.when(in_first)
        def _():
            grads_copy(m).wait()
            whole, low, high = pass_copies(m)
            pl.when(on_right)(low.wait_send)
            pl.when(on_left)(high.wait_send)
            whole.wait_send()
            low, high = near_copies(m)
            pl.when(on_right)(low.wait_send)
            pl.when(on_left)(high.wait_send)

        @pl.when(in_second)
        def _():
            field_copy(m).wait_send()
            whole, sides, low, high = back_copies(m)
            pl.when(on_right)(low.wait_send)
            pl.when(on_left)(high.wait_send)
            whole.wait_send()
            sides.wait_send()
            grads_across(m).wait_recv()

        return carry

    lax.fori_loop(0, rows, settle_row, 0)

    @pl.when(in_first)
    def _():
        pl.when(on_right)(tokens_right.wait_send)
        pl.when(on_left)(tokens_left.wait_send)
        near_fields.wait_send()

    @pl.when(in_second)
    def _():
        masks_back.wait_send()
        weight_copy.wait_send()


def hand_over(*refs):
    sems_in, sems_out = refs[-2:]
    count = len(refs) // 3
    sources, targets, held = refs[:count], refs[count : 2 * count], refs[2 * count : 3 * count]
    copies_in = [pltpu.make_async_copy(sources[i], held[i], sems_in.at[i]) for i in range(count)]
    copies_out = [pltpu.make_async_copy(held[i], targets[i], sems_out.at[i]) for i in range(count)]
    for copy in copies_in:
        copy.start()
    for i in range(count):
        copies_in[i].wait()
        copies_out[i].start()
    for copy in copies_out:
        copy.wait()


def per_device(
    dp,
    seq,
    tokens,
    cotangent,
    tap_masks,
    conv_weight,
    up_weight,
    up_bias,
    down_weight,
    norm_gains,
    shift_terms,
):
    rows, length, width = tokens.shape
    hidden = up_weight.shape[2]
    geo = Geometry(dp, seq, rows, length, width, hidden)
    reach = length + 2 * HALO
    vmem = pl.BlockSpec(memory_space=pltpu.VMEM)
    hbm = pl.BlockSpec(memory_space=pl.ANY)
    dma = pltpu.SemaphoreType.DMA
    stages = len(geo.all_bits)
    slices = (geo.slices, geo.owners, geo.share, width)
    made = pl.pallas_call(
        functools.partial(body, geo),
        out_shape=[
            jax.ShapeDtypeStruct((rows, length, width), BF16),
            jax.ShapeDtypeStruct((rows, length, width), F32),
            jax.ShapeDtypeStruct((TAPS, geo.share, width), F32),
            jax.ShapeDtypeStruct((geo.share, hidden), F32),
            jax.ShapeDtypeStruct((geo.chunks * geo.share, width), F32),
            jax.ShapeDtypeStruct((1, geo.bias_share), F32),
            jax.ShapeDtypeStruct((2, geo.final_share), F32),
            jax.ShapeDtypeStruct((4, geo.final_share), F32),
        ],
        in_specs=[hbm] * 5 + [vmem] * 4,
        out_specs=[hbm] * 2 + [vmem] * 6,
        scratch_shapes=[
            pltpu.VMEM((rows, reach, width), BF16),
            pltpu.VMEM((rows, reach, width), BF16),
            pltpu.VMEM((rows, reach, width), BF16),
            pltpu.VMEM((rows, 2, EDGE, width), BF16),
            pltpu.VMEM((TAPS * width, width), BF16),
            pltpu.VMEM((width, hidden), BF16),
            pltpu.VMEM((hidden, width), BF16),
            pltpu.VMEM((2 * geo.chunks + 1, geo.tokens, width), BF16),
            pltpu.VMEM((length, TAPS * width), BF16),
            pltpu.VMEM((2 * geo.tokens, width // 2), BF16),
            pltpu.VMEM((geo.tokens, width), BF16),
            pltpu.VMEM((geo.tokens, width), BF16),
            pltpu.VMEM((geo.tokens, width), BF16),
            pltpu.VMEM((geo.tokens, 128), F32),
            pltpu.VMEM((rows, length, width), F32),
            pltpu.VMEM((rows, length, width), BF16),
            pltpu.VMEM((geo.tokens, width), BF16),
            pltpu.VMEM((rows, length, width), BF16),
            pltpu.VMEM((TAPS, rows, length), jnp.int32),
            pltpu.VMEM((TAPS, rows, length), jnp.int32),
            pltpu.VMEM((geo.tokens, 128), F32),
            pltpu.VMEM((geo.tokens, 128), F32),
            pltpu.VMEM((geo.tokens, 128), F32),
            pltpu.VMEM(slices, BF16),
            pltpu.VMEM(slices, BF16),
            pltpu.VMEM((16, width), F32),
            pltpu.VMEM((stages, 16, width), F32),
            pltpu.VMEM((stages, 16, width), F32),
            dma((3,)),
            dma((2,)),
            dma((2,)),
            dma((2,)),
            dma((2,)),
            dma((2,)),
            dma((rows, 3)),
            dma((rows, 3)),
            dma((rows,)),
            dma((rows,)),
            dma,
            dma,
            dma((rows, 4)),
            dma((rows, 4)),
            dma((rows,)),
            dma((rows,)),
            dma((rows, 2)),
            dma((rows, 2)),
            dma((rows,)),
            dma((rows,)),
            dma((rows,)),
            dma((rows,)),
            dma((geo.slices, geo.owners)),
            dma((geo.slices, geo.owners)),
            dma((stages,)),
            dma((stages,)),
        ],
        compiler_params=pltpu.CompilerParams(
            collective_id=0, has_side_effects=True, vmem_limit_bytes=63 * 2**20
        ),
    )(
        tokens,
        cotangent,
        jnp.transpose(conv_weight[0], (1, 0, 2)).reshape(TAPS * width, width),
        up_weight[0],
        down_weight[0],
        tap_masks[0],
        up_bias,
        jnp.transpose(norm_gains[0]),
        jnp.transpose(shift_terms[0]),
    )
    made = pl.pallas_call(
        hand_over,
        out_shape=[jax.ShapeDtypeStruct(array.shape, array.dtype) for array in made],
        in_specs=[hbm] * len(made),
        out_specs=[hbm] * len(made),
        scratch_shapes=[pltpu.VMEM(array.shape, array.dtype) for array in made] + [dma((len(made),))] * 2,
    )(*made)
    act, grads, conv_grad, up_grad, down_grad, bias_grad, gain_grad, shift_grad = made
    conv_grad = jnp.transpose(conv_grad, (1, 0, 2))
    if geo.low > 1:
        groups = [list(range(at, at + geo.low)) for at in range(0, seq, geo.low)]
        conv_grad, up_grad, down_grad = (
            lax.psum_scatter(
                grad, "seq", scatter_dimension=0, axis_index_groups=groups, tiled=True
            )
            for grad in (conv_grad, up_grad, down_grad)
        )
    return (
        act[None],
        grads[None],
        conv_grad[None],
        up_grad[None],
        bias_grad,
        down_grad[None],
        jnp.transpose(gain_grad)[None],
        jnp.transpose(shift_grad)[None],
    )


def solution(mesh):
    placed = (
        P("dp", "seq", None),
        P("dp", "seq", None),
        P("section", None, "dp", "seq"),
        P("section", None, None, None),
        P("section", None, None),
        P("section", None),
        P("section", None, None),
        P("section", None, None),
        P("section", None, None),
    )
    return jax.shard_map(
        functools.partial(per_device, mesh.shape["dp"], mesh.shape["seq"]),
        mesh=mesh,
        in_specs=placed,
        out_specs=(
            P("section", "dp", "seq", None),
            P("section", "dp", "seq", None),
            P("section", ("dp", "seq"), None, None),
            P("section", ("dp", "seq"), None),
            P("section", ("dp", "seq")),
            P("section", ("dp", "seq"), None),
            P("section", ("dp", "seq"), None),
            P("section", ("dp", "seq"), None),
        ),
        check_vma=False,
    )
```

```python
import functools

import jax
import jax.numpy as jnp
from jax import lax
from jax.experimental import pallas as pl
from jax.experimental.pallas import tpu as pltpu
from jax.sharding import PartitionSpec as P

TAPS = 9
CENTRE = TAPS // 2
TIGHT = 2
WIDE = 32
HALO = CENTRE * WIDE
EDGE = 16
EPS = 1e-05
MESH = pl.DeviceIdType.MESH
BF16 = jnp.bfloat16
F32 = jnp.float32
LAG = 3
PLAN = (
    ("conv", 4), ("conv", 3), ("conv", 1), ("first", 3), (8, 0), ("other", 0), ("up", 1), (7, 0), (8, 1),
    ("conv", 0), (5, 0), ("first", 0), ("conv", 2), ("down", 0), (8, 2), ("up", 0), ("first", 2), (4, 0), (7, 1),
    ("down", 1), (1, 0), (0, 0), (4, 1), (6, 0), (7, 2), (5, 1), (2, 0), (1, 1), (3, 0), (6, 1), (5, 2), (0, 1),
    ("first", 1), (5, 3), (7, 3), (4, 2), (3, 1), (2, 1), (6, 2), (1, 2), (8, 3), (0, 2), (3, 2), (6, 3), (4, 3),
    (1, 3), (0, 3), (2, 2),
)
ALONG = (5, 7, 8)
TANH_SCALE = 0.7978845608028654
TANH_CUBE = TANH_SCALE * 0.044715


def gelu_pair(z):
    square = z * z
    half = 0.5 + 0.5 * jnp.tanh(z * (TANH_SCALE + TANH_CUBE * square))
    value = z * half
    return value, half + value * (1.0 - half) * (2.0 * TANH_SCALE + 6.0 * TANH_CUBE * square)


def normalise(values):
    centred = values - jnp.mean(values, axis=-1, keepdims=True)
    scale = lax.rsqrt(jnp.mean(centred * centred, axis=-1, keepdims=True) + EPS)
    return centred * scale, scale


def norm_backward(weighted, unit):
    return (
        weighted
        - jnp.mean(weighted, axis=-1, keepdims=True)
        - unit * jnp.mean(weighted * unit, axis=-1, keepdims=True)
    )


def column_sum(values):
    return jnp.sum(values, axis=0, keepdims=True)


def dot(a, b):
    return jnp.dot(a, b, preferred_element_type=F32)


def dot_nt(a, b):
    return lax.dot_general(a, b, (((1,), (1,)), ((), ())), preferred_element_type=F32)


def dot_tn(a, b):
    return lax.dot_general(a, b, (((0,), (0,)), ((), ())), preferred_element_type=F32)


class Geometry:
    def __init__(self, dp, seq, rows, length, width, hidden):
        self.dp, self.seq = dp, seq
        self.rows, self.length, self.width = rows, length, width
        self.tokens = rows * length
        self.chunks = hidden // width
        self.low = max(1, 16 * dp * seq // width)
        self.owners = dp * seq // self.low
        self.share = width // self.owners
        self.final_share = width // (dp * seq)
        self.bias_share = hidden // (dp * seq)
        dp_bits = [("dp", 1 << i) for i in range(dp.bit_length() - 1)]
        seq_all = [("seq", 1 << i) for i in range(seq.bit_length() - 1)]
        seq_bits = [bit for bit in seq_all if bit[1] >= self.low]
        self.bits = dp_bits + seq_bits
        self.all_bits = dp_bits + seq_all
        self.dp_bits = dp_bits
        self.pairs = (TAPS + 1) // 2
        self.part_chunks = self.chunks // 2
        self.slices = 2 * self.part_chunks + self.pairs
        low_bit, high_bit, lines = dp_bits[:1], dp_bits[-1:], seq_bits
        self.orders = [low_bit + lines + high_bit] * self.part_chunks + [low_bit + lines] * self.part_chunks
        self.orders += [high_bit + lines + low_bit] * self.pairs
        for j in range(self.slices):
            if j in ALONG:
                self.orders[j] = lines[:1] + self.orders[j][:1] + self.orders[j][2:]
        planned = len(self.bits) == 4 and rows == 4 and self.chunks == 4
        self.plan = PLAN if planned else self.plain_plan()

    def plain_plan(self):
        first_down, first_conv = self.part_chunks, 2 * self.part_chunks
        work = [("other", 0)]
        work += [("down", i) for i in range(self.part_chunks)]
        work += [("up", i) for i in range(self.part_chunks)]
        work += [("conv", p) for p in range(self.pairs)]
        work += [("first", m) for m in range(self.rows)]
        due = {}
        for turn, (kind, at) in enumerate(work):
            begun = {"up": [at], "conv": [first_conv + at]}.get(kind, [])
            if kind == "down" and at == self.part_chunks - 1:
                begun = range(first_down, first_conv)
            for j in begun:
                for i in range(len(self.orders[j])):
                    due.setdefault(turn + LAG * (i + 1), []).append((j, i))
        plan = []
        for turn in range(max(max(due) + 1, len(work))):
            plan += work[turn : turn + 1] + due.get(turn, [])
        return plan


def body(
    geo,
    tokens_hbm,
    cotangent_hbm,
    conv_hbm,
    up_hbm,
    down_hbm,
    masks,
    bias,
    gains,
    shifts,
    act_hbm,
    grads_hbm,
    conv_out,
    up_out,
    down_out,
    bias_out,
    gain_out,
    shift_out,
    fields,
    fields_other,
    conv_grads,
    near_edges,
    conv_w,
    up_w,
    down_w,
    slabs,
    taps,
    halves,
    unit_one,
    slope_one,
    unit_two,
    scale_two,
    mixed_grads,
    given,
    ffn_grads,
    mixed_other,
    ffn_grads_other,
    upper_other,
    hidden_other,
    results,
    masks_other,
    masks_second,
    columns,
    columns_other,
    columns_second,
    partial,
    arrived,
    sums,
    sums_sent,
    sums_arrived,
    load_sem,
    row_load_sem,
    token_edge_send,
    token_edge_recv,
    masks_send,
    masks_recv,
    pass_send,
    pass_recv,
    field_send,
    field_recv,
    weight_send,
    weight_recv,
    back_send,
    back_recv,
    half_send,
    half_recv,
    mixed_send,
    mixed_recv,
    ffn_send,
    ffn_recv,
    near_send,
    near_recv,
    act_sem,
    grads_sem,
    grads_send,
    grads_recv,
    part_send,
    part_recv,
    sums_send,
    sums_recv,
):
    rows, length, width, chunks = geo.rows, geo.length, geo.width, geo.chunks
    tokens, half_width = geo.tokens, geo.width // 2
    section = lax.axis_index("section")
    dp = lax.axis_index("dp")
    seq = lax.axis_index("seq")
    mine = {"dp": dp, "seq": seq}
    in_first = section == 0
    in_second = section == 1
    has_left = (seq + geo.seq - 1) // geo.seq
    has_right = 1 - (seq + 1) // geo.seq
    on_left, on_right = has_left == 1, has_right == 1
    own = slice(HALO, HALO + length)
    near = slice(HALO - EDGE, HALO + length + EDGE)

    def bit_of(bit):
        axis, size = bit
        return (mine[axis] // size) % 2

    def partner(bit):
        axis, size = bit
        other = mine[axis] + (1 - 2 * bit_of(bit)) * size
        return (section, other, seq) if axis == "dp" else (section, dp, other)

    def remote(source, target, sends, receives, device):
        return pltpu.make_async_remote_copy(
            src_ref=source,
            dst_ref=target,
            send_sem=sends,
            recv_sem=receives,
            device_id=device,
            device_id_type=MESH,
        )

    core = (1 - section, dp, seq)
    left, right = (section, dp, seq - 1), (section, dp, seq + 1)
    first_core, second_core = (0, dp, seq), (1, dp, seq)
    conv_bit, ffn_bit = geo.dp_bits[0], geo.dp_bits[-1]
    pair, ffn_pair = partner(conv_bit), partner(ffn_bit)
    my_half, my_part = bit_of(conv_bit), bit_of(ffn_bit)
    part_chunks = geo.part_chunks
    mine_at = pl.ds(pl.multiple_of(my_half * half_width, half_width), half_width)
    other_at = pl.ds(pl.multiple_of((1 - my_half) * half_width, half_width), half_width)

    loads = [
        pltpu.make_async_copy(conv_hbm, conv_w, load_sem.at[0]),
        pltpu.make_async_copy(up_hbm, up_w, load_sem.at[1]),
        pltpu.make_async_copy(down_hbm, down_w, load_sem.at[2]),
    ]
    token_load = pltpu.make_async_copy(tokens_hbm, fields.at[:, own], row_load_sem.at[0])
    given_load = pltpu.make_async_copy(cotangent_hbm, given, row_load_sem.at[1])
    pl.when(in_first)(token_load.start)
    for load in loads:
        load.start()
    pl.when(in_second)(given_load.start)

    @pl.when(has_left == 0)
    def _():
        fields[:, :HALO] = jnp.zeros((rows, HALO, width), BF16)
        conv_grads[:, :HALO] = jnp.zeros((rows, HALO, width), BF16)

    @pl.when(has_right == 0)
    def _():
        fields[:, HALO + length :] = jnp.zeros((rows, HALO, width), BF16)
        conv_grads[:, HALO + length :] = jnp.zeros((rows, HALO, width), BF16)

    sums[...] = jnp.zeros(sums.shape, F32)

    barrier = pltpu.get_barrier_semaphore()

    def greet(device):
        pl.semaphore_signal(barrier, inc=1, device_id=device, device_id_type=MESH)

    for bit in geo.all_bits:
        greet(partner(bit))
    greet(core)
    for flag, at in ((on_left, seq - 1), (on_right, seq + 1)):

        @pl.when(flag)
        def _(at=at):
            greet((section, dp, at))
            greet((1 - section, dp, at))

    pl.semaphore_wait(barrier, len(geo.all_bits) + 1 + 2 * has_left + 2 * has_right)

    tokens_right = remote(
        tokens_hbm.at[:, length - EDGE : length],
        fields.at[:, HALO - EDGE : HALO],
        token_edge_send.at[0],
        token_edge_recv.at[0],
        right,
    )
    tokens_left = remote(
        tokens_hbm.at[:, 0:EDGE],
        fields.at[:, HALO + length : HALO + length + EDGE],
        token_edge_send.at[1],
        token_edge_recv.at[1],
        left,
    )

    @pl.when(in_first)
    def _():
        pl.when(on_right)(tokens_right.start)
        pl.when(on_left)(tokens_left.start)

    masks_across = remote(masks, masks_other, masks_send.at[0], masks_recv.at[0], pair)
    masks_back = remote(masks, masks_second, masks_send.at[1], masks_recv.at[1], first_core)
    masks_across.start()
    pl.when(in_second)(masks_back.start)

    def to_columns(source, target):
        for r in range(rows):
            plane = source[:, r, :].astype(F32)
            padded = jnp.concatenate([plane, jnp.zeros((128 - TAPS, length), F32)], axis=0)
            target[r * length : (r + 1) * length, :] = jnp.transpose(padded)

    to_columns(masks, columns)

    def span(m):
        return pl.ds(pl.multiple_of(m * length, length), length)

    def one_tap(source, mask_columns, m, k, dilation):
        values = source[m, pl.ds(HALO + (k - CENTRE) * dilation, length), :]
        if k == CENTRE:
            return values
        lane = jnp.broadcast_to(mask_columns[span(m), k : k + 1], (length, 128)).astype(BF16)
        return values * jnp.concatenate([lane] * (width // 128), axis=1)

    def pass_copies(m):
        return (
            remote(results.at[m], fields.at[m, own], pass_send.at[m, 0], pass_recv.at[m, 0], second_core),
            remote(
                results.at[m, length - HALO : length],
                fields.at[m, 0:HALO],
                pass_send.at[m, 1],
                pass_recv.at[m, 1],
                (1, dp, seq + 1),
            ),
            remote(
                results.at[m, 0:HALO],
                fields.at[m, HALO + length : HALO + length + HALO],
                pass_send.at[m, 2],
                pass_recv.at[m, 2],
                (1, dp, seq - 1),
            ),
        )

    def back_copies(m):
        return (
            remote(conv_grads.at[m, own], conv_grads.at[m, own], back_send.at[m, 0], back_recv.at[m, 0], first_core),
            remote(mixed_grads.at[m], mixed_grads.at[m], back_send.at[m, 1], back_recv.at[m, 1], first_core),
            remote(
                conv_grads.at[m, HALO + length - HALO : HALO + length],
                conv_grads.at[m, 0:HALO],
                back_send.at[m, 2],
                back_recv.at[m, 2],
                (0, dp, seq + 1),
            ),
            remote(
                conv_grads.at[m, HALO : HALO + HALO],
                conv_grads.at[m, HALO + length : HALO + length + HALO],
                back_send.at[m, 3],
                back_recv.at[m, 3],
                (0, dp, seq - 1),
            ),
        )

    def near_copies(m):
        return (
            remote(
                conv_grads.at[m, HALO + length - EDGE : HALO + length],
                near_edges.at[m, 0],
                near_send.at[m, 0],
                near_recv.at[m, 0],
                right,
            ),
            remote(
                conv_grads.at[m, HALO : HALO + EDGE],
                near_edges.at[m, 1],
                near_send.at[m, 1],
                near_recv.at[m, 1],
                left,
            ),
        )

    def field_copy(m):
        return remote(fields.at[m], fields_other.at[m], field_send.at[m], field_recv.at[m], pair)

    near_fields = remote(
        fields.at[:, near], fields_other.at[:, near], field_send.at[0], field_recv.at[0], pair
    )

    def half_copy(m):
        return remote(
            conv_grads.at[m, own, other_at],
            halves.at[pl.ds(pl.multiple_of(tokens + m * length, length), length)],
            half_send.at[m],
            half_recv.at[m],
            pair,
        )

    def mixed_copy(m):
        here = span(m)
        return remote(
            slabs.at[2 * chunks, here], mixed_other.at[here], mixed_send.at[m], mixed_recv.at[m], ffn_pair
        )

    def ffn_copy(m):
        here = span(m)
        return remote(ffn_grads.at[here], ffn_grads_other.at[here], ffn_send.at[m], ffn_recv.at[m], ffn_pair)

    weight_copy = remote(conv_w, conv_w, weight_send, weight_recv, first_core)

    def act_copy(m):
        return pltpu.make_async_copy(results.at[m], act_hbm.at[m], act_sem.at[m])

    def grads_copy(m):
        return pltpu.make_async_copy(mixed_grads.at[m], grads_hbm.at[m], grads_sem.at[m])

    def grads_across(m):
        return remote(mixed_grads.at[m], grads_hbm.at[m], grads_send.at[m], grads_recv.at[m], second_core)

    for load in loads:
        load.wait()

    @pl.when(in_first)
    def _():
        token_load.wait()
        pl.when(on_left)(tokens_right.wait_recv)
        pl.when(on_right)(tokens_left.wait_recv)
        near_fields.start()

    gain_one, gain_two = gains[0:1, :], gains[1:2, :]
    shift_conv, shift_one = shifts[0:1, :], shifts[1:2, :]
    shift_ffn, shift_two = shifts[2:3, :], shifts[3:4, :]

    def forward(m, carry):
        here = span(m)

        @pl.when(in_second)
        def _():
            whole, low, high = pass_copies(m)
            whole.wait_recv()
            pl.when(on_left)(low.wait_recv)
            pl.when(on_right)(high.wait_recv)
            field_copy(m).start()
            pl.when(m == rows - 1)(weight_copy.start)

        for flag, dilation in ((in_first, TIGHT), (in_second, WIDE)):

            @pl.when(flag)
            def _(dilation=dilation):
                for k in range(TAPS):
                    taps[:, k * width : (k + 1) * width] = one_tap(fields, columns, m, k, dilation)

        value, slope = gelu_pair(dot(taps[...], conv_w[...]) + shift_conv)
        unit, scale = normalise(value)
        unit_one[here, :] = unit.astype(BF16)
        slope_one[here, :] = (slope * scale).astype(BF16)
        mixed = fields[m, own, :].astype(F32) + unit * gain_one + shift_one
        mixed_low = mixed.astype(BF16)
        slabs[2 * chunks, here, :] = mixed_low
        mixed_copy(m).start()
        ffn = None
        for c in range(chunks):
            part = slice(c * width, (c + 1) * width)
            value, slope = gelu_pair(dot(mixed_low, up_w[:, part]) + bias[:, part])
            low = value.astype(BF16)
            slabs[c, here, :] = low
            slabs[chunks + c, here, :] = slope.astype(BF16)
            term = dot(low, down_w[part, :])
            ffn = term if ffn is None else ffn + term
        unit, scale = normalise(ffn + shift_ffn)
        unit_two[here, :] = unit.astype(BF16)
        scale_two[here, :] = jnp.broadcast_to(scale, (length, 128))
        results[m] = (mixed + unit * gain_two + shift_two).astype(BF16)
        act_copy(m).start()

        @pl.when(in_first)
        def _():
            whole, low, high = pass_copies(m)
            pl.when(on_right)(low.start)
            pl.when(on_left)(high.start)
            whole.start()

        return carry

    lax.fori_loop(0, rows, forward, 0)

    masks_across.wait_recv()
    to_columns(masks_other, columns_other)

    @pl.when(in_first)
    def _():
        masks_back.wait_recv()
        to_columns(masks_second, columns_second)

    def conv_back(m, mask_columns, dilation):
        grad = mixed_grads[m]
        for k in range(TAPS):
            at = (TAPS - 1 - k) * width
            grad = grad + dot_nt(one_tap(conv_grads, mask_columns, m, k, dilation), conv_w[at : at + width, :])
        return grad

    def chunk_of(i):
        return my_part * part_chunks + i

    def chunk_span(i):
        return pl.ds(pl.multiple_of(chunk_of(i) * width, width), width)

    def other_forward(m, carry):
        here = span(m)
        mixed_copy(m).wait_recv()
        for i in range(part_chunks):
            at = chunk_span(i)
            value, slope = gelu_pair(dot(mixed_other[here, :], up_w[:, at]) + bias[:, at])
            upper_other[i, here, :] = value.astype(BF16)
            hidden_other[i, here, :] = slope.astype(BF16)
        return carry

    def other_backward(m, carry):
        here = span(m)
        ffn_copy(m).wait_recv()
        for i in range(part_chunks):
            grad = dot_nt(ffn_grads_other[here, :], down_w[chunk_span(i), :])
            hidden_other[i, here, :] = (grad * hidden_other[i, here, :].astype(F32)).astype(BF16)
        return carry

    def second_input(m, carry):
        whole, sides, low, high = back_copies(m)
        whole.wait_recv()
        sides.wait_recv()
        pl.when(on_left)(low.wait_recv)
        pl.when(on_right)(high.wait_recv)
        low = conv_back(m, columns_second, WIDE).astype(BF16)
        given[m] = low
        mixed_grads[m] = low.astype(F32)
        grads_across(m).start()
        return carry

    @pl.when(in_first)
    def _():
        lax.fori_loop(0, rows, other_forward, 0)
        weight_copy.wait_recv()
        lax.fori_loop(0, rows, second_input, 0)
        loads[0].start()

    pl.when(in_second)(given_load.wait)

    def backward_ffn(m, carry):
        here = span(m)
        grad = given[m].astype(F32)
        unit = unit_two[here, :].astype(F32)
        grad_ffn = norm_backward(grad * gain_two, unit) * scale_two[here, 0:1]
        sums[1:2, :] += column_sum(grad * unit)
        sums[5:6, :] += column_sum(grad)
        sums[4:5, :] += column_sum(grad_ffn)
        grad_ffn_low = grad_ffn.astype(BF16)
        ffn_grads[here, :] = grad_ffn_low
        ffn_copy(m).start()
        mixed = grad
        for c in range(chunks):
            part = slice(c * width, (c + 1) * width)
            grad_hidden = dot_nt(grad_ffn_low, down_w[part, :]) * slabs[chunks + c, here, :].astype(F32)
            sums[8 + c : 9 + c, :] += column_sum(grad_hidden)
            low = grad_hidden.astype(BF16)
            slabs[chunks + c, here, :] = low
            mixed = mixed + dot_nt(low, up_w[:, part])
        pl.when(in_first)(grads_across(m).wait_send)
        mixed_grads[m] = mixed
        unit = unit_one[here, :].astype(F32)
        grad_conv = norm_backward(mixed * gain_one, unit) * slope_one[here, :].astype(F32)
        sums[0:1, :] += column_sum(mixed * unit)
        sums[3:4, :] += column_sum(mixed)
        sums[2:3, :] += column_sum(grad_conv)
        conv_grads[m, own, :] = grad_conv.astype(BF16)

        @pl.when(in_second)
        def _():
            whole, sides, low, high = back_copies(m)
            pl.when(on_right)(low.start)
            pl.when(on_left)(high.start)
            whole.start()
            sides.start()

        @pl.when(in_first)
        def _():
            low, high = near_copies(m)
            pl.when(on_right)(low.start)
            pl.when(on_left)(high.start)

        half_copy(m).start()
        halves[here, :] = conv_grads[m, own, mine_at]
        return carry

    lax.fori_loop(0, rows, backward_ffn, 0)

    @pl.when(in_second)
    def _():
        lax.fori_loop(0, rows, other_forward, 0)

    def sums_copy(i):
        return remote(
            sums_sent.at[i], sums_arrived.at[i], sums_send.at[i], sums_recv.at[i], partner(geo.all_bits[i])
        )

    def sums_begin(i):
        sums_sent[i] = sums[...]
        sums_copy(i).start()

    def sums_end(i):
        sums_copy(i).wait_recv()
        sums[...] += sums_arrived[i]

    owners, share = geo.owners, geo.share
    my_bits = {bit: bit_of(bit) for bit in geo.bits}
    partners = {bit: partner(bit) for bit in geo.bits}
    per_dp = geo.seq // geo.low
    first_down, first_conv = part_chunks, 2 * part_chunks

    def columns_of(j):
        single = j == geo.slices - 1 and TAPS % 2 == 1
        return slice(0, half_width) if single else slice(0, width)

    def place(j, owner_dp, owner_seq):
        where = 0
        weight = owners
        for axis, size in geo.orders[j]:
            weight //= 2
            index = owner_dp if axis == "dp" else owner_seq * geo.low
            where = where + ((index // size) % 2 + my_bits[axis, size]) % 2 * weight
        return where

    def part_copy(j, i):
        half, at = owners >> (i + 1), columns_of(j)
        return remote(
            partial.at[j, half : 2 * half, :, at],
            arrived.at[j, half : 2 * half, :, at],
            part_send.at[j, i],
            part_recv.at[j, i],
            partners[geo.orders[j][i]],
        )

    def total_of(j, i):
        half, at = owners >> (i + 1), columns_of(j)
        return partial[j, 0:half, :, at].astype(F32) + arrived[j, half : 2 * half, :, at].astype(F32)

    def advance(j, i):
        part_copy(j, i - 1).wait_recv()
        partial[j, 0 : owners >> i, :, columns_of(j)] = total_of(j, i - 1).astype(BF16)
        part_copy(j, i).start()

    def finish(j):
        last = len(geo.orders[j]) - 1
        part_copy(j, last).wait_recv()
        if j < first_down:
            for part, total in ((my_part, partial[j, 0]), (1 - my_part, arrived[j, 1])):
                at = (part * part_chunks + j) * width
                up_out[:, pl.ds(pl.multiple_of(at, width), width)] = total.astype(F32)
        elif j < first_conv:
            total = total_of(j, last)
            for r in range(2):
                at = (2 * (j - first_down) + r) * share
                down_out[at : at + share, :] = total[r]
        else:
            for q in range(2):
                k = 2 * (j - first_conv) + q
                if k < TAPS:
                    at = slice(q * half_width, (q + 1) * half_width)
                    conv_out[k, :, mine_at] = partial[j, 0, :, at].astype(F32)
                    conv_out[k, :, other_at] = arrived[j, 1, :, at].astype(F32)

    def up_slice(j):
        grad = dot_tn(slabs[2 * chunks], slabs[chunks + chunk_of(j)]) + dot_tn(mixed_other[...], hidden_other[j])
        for owner in range(owners):
            where = place(j, owner // per_dp, owner % per_dp)
            partial[j, where] = grad[owner * share : (owner + 1) * share].astype(BF16)
        part_copy(j, 0).start()

    def down_slab(i):
        grad = dot_tn(slabs[chunk_of(i)], ffn_grads[...]) + dot_tn(upper_other[i], ffn_grads_other[...])
        each = owners // chunks
        for w in range(each):
            owner = chunk_of(i) * each + w
            for s in range(part_chunks):
                where = place(first_down + s, owner // per_dp, owner % per_dp)
                for r in range(2):
                    at = ((w * part_chunks + s) * 2 + r) * share
                    partial[first_down + s, where + r] = grad[at : at + share].astype(BF16)
        if i == part_chunks - 1:
            for s in range(part_chunks):
                part_copy(first_down + s, 0).start()

    conv_begun = []

    def conv_slice(p):
        j = first_conv + p
        if not conv_begun:
            conv_begun.append(p)
            for m in range(rows):
                half_copy(m).wait_recv()
            pl.when(in_first)(near_fields.wait_recv)

            @pl.when(in_second)
            def _():
                for m in range(rows):
                    field_copy(m).wait_recv()

        for q in range(2):
            k = 2 * p + q
            if k >= TAPS:
                continue
            at = slice(q * half_width, (q + 1) * half_width)
            places = [place(j, owner // per_dp, owner % per_dp) for owner in range(owners)]
            for flag, dilation in ((in_first, TIGHT), (in_second, WIDE)):

                @pl.when(flag)
                def _(dilation=dilation):
                    grad = None
                    for source, mask_columns, base in ((fields, columns, 0), (fields_other, columns_other, tokens)):
                        for m in range(rows):
                            low = base + m * length
                            values = one_tap(source, mask_columns, m, k, dilation)
                            term = dot_tn(values, halves[low : low + length, :])
                            grad = term if grad is None else grad + term
                    for owner in range(owners):
                        partial[j, places[owner], :, at] = grad[owner * share : (owner + 1) * share].astype(BF16)
        part_copy(j, 0).start()

    input_begun = []

    def first_input(m):
        low, high = near_copies(m)

        @pl.when(on_left)
        def _():
            low.wait_recv()
            conv_grads[m, HALO - EDGE : HALO, :] = near_edges[m, 0]

        @pl.when(on_right)
        def _():
            high.wait_recv()
            conv_grads[m, HALO + length : HALO + length + EDGE, :] = near_edges[m, 1]

        if not input_begun:
            input_begun.append(m)
            loads[0].wait()
        mixed_grads[m] = conv_back(m, columns, TIGHT)
        grads_copy(m).start()

    def share_sums():
        index = dp * geo.seq + seq
        lane = lax.broadcasted_iota(jnp.int32, (128, width), 1)
        line = lax.broadcasted_iota(jnp.int32, (128, width), 0)
        exact = functools.partial(
            lax.dot_general,
            dimension_numbers=(((1,), (1,)), ((), ())),
            precision=lax.Precision.HIGHEST,
            preferred_element_type=F32,
        )
        picked = exact(sums[...], (lane == line + index * geo.final_share).astype(F32))
        gain_out[...] = picked[0:2, : geo.final_share]
        shift_out[...] = picked[2:6, : geo.final_share]
        start = index * geo.bias_share
        picked = exact(sums[...], (lane == line + start % width).astype(F32))
        wanted = lax.broadcasted_iota(jnp.int32, picked.shape, 0) == 8 + start // width
        bias_out[...] = column_sum(jnp.where(wanted, picked, 0.0))[:, : geo.bias_share]

    def gradients_back():
        lax.fori_loop(0, rows, other_backward, 0)

    def work_of(kind, at):
        if kind == "first":
            return lambda: pl.when(in_first)(lambda: first_input(at))
        if kind == "other":
            return gradients_back
        return functools.partial({"up": up_slice, "down": down_slab, "conv": conv_slice}[kind], at)

    sums_begin(0)
    stride = 6
    sums_done = 0
    for at, (what, which) in enumerate(geo.plan):
        if isinstance(what, str):
            work_of(what, which)()
        elif which + 1 < len(geo.orders[what]):
            advance(what, which + 1)
        else:
            finish(what)
        if (at + 1) % stride == 0 and sums_done < len(geo.all_bits):
            sums_end(sums_done)
            sums_done += 1
            if sums_done < len(geo.all_bits):
                sums_begin(sums_done)
            else:
                share_sums()

    for j in range(geo.slices):
        for i in range(len(geo.orders[j])):
            part_copy(j, i).wait_send()
    for i in range(len(geo.all_bits)):
        sums_copy(i).wait_send()
    masks_across.wait_send()

    def settle_row(m, carry):
        act_copy(m).wait()
        half_copy(m).wait_send()
        mixed_copy(m).wait_send()
        ffn_copy(m).wait_send()

        @pl.when(in_first)
        def _():
            grads_copy(m).wait()
            whole, low, high = pass_copies(m)
            pl.when(on_right)(low.wait_send)
            pl.when(on_left)(high.wait_send)
            whole.wait_send()
            low, high = near_copies(m)
            pl.when(on_right)(low.wait_send)
            pl.when(on_left)(high.wait_send)

        @pl.when(in_second)
        def _():
            field_copy(m).wait_send()
            whole, sides, low, high = back_copies(m)
            pl.when(on_right)(low.wait_send)
            pl.when(on_left)(high.wait_send)
            whole.wait_send()
            sides.wait_send()
            grads_across(m).wait_recv()

        return carry

    lax.fori_loop(0, rows, settle_row, 0)

    @pl.when(in_first)
    def _():
        pl.when(on_right)(tokens_right.wait_send)
        pl.when(on_left)(tokens_left.wait_send)
        near_fields.wait_send()

    @pl.when(in_second)
    def _():
        masks_back.wait_send()
        weight_copy.wait_send()


def hand_over(*refs):
    sems_in, sems_out = refs[-2:]
    count = len(refs) // 3
    sources, targets, held = refs[:count], refs[count : 2 * count], refs[2 * count : 3 * count]
    copies_in = [pltpu.make_async_copy(sources[i], held[i], sems_in.at[i]) for i in range(count)]
    copies_out = [pltpu.make_async_copy(held[i], targets[i], sems_out.at[i]) for i in range(count)]
    for copy in copies_in:
        copy.start()
    for i in range(count):
        copies_in[i].wait()
        copies_out[i].start()
    for copy in copies_out:
        copy.wait()


def per_device(
    dp,
    seq,
    tokens,
    cotangent,
    tap_masks,
    conv_weight,
    up_weight,
    up_bias,
    down_weight,
    norm_gains,
    shift_terms,
):
    rows, length, width = tokens.shape
    hidden = up_weight.shape[2]
    geo = Geometry(dp, seq, rows, length, width, hidden)
    reach = length + 2 * HALO
    vmem = pl.BlockSpec(memory_space=pltpu.VMEM)
    hbm = pl.BlockSpec(memory_space=pl.ANY)
    dma = pltpu.SemaphoreType.DMA
    stages = len(geo.all_bits)
    slices = (geo.slices, geo.owners, geo.share, width)
    made = pl.pallas_call(
        functools.partial(body, geo),
        out_shape=[
            jax.ShapeDtypeStruct((rows, length, width), BF16),
            jax.ShapeDtypeStruct((rows, length, width), F32),
            jax.ShapeDtypeStruct((TAPS, geo.share, width), F32),
            jax.ShapeDtypeStruct((geo.share, hidden), F32),
            jax.ShapeDtypeStruct((geo.chunks * geo.share, width), F32),
            jax.ShapeDtypeStruct((1, geo.bias_share), F32),
            jax.ShapeDtypeStruct((2, geo.final_share), F32),
            jax.ShapeDtypeStruct((4, geo.final_share), F32),
        ],
        in_specs=[hbm] * 5 + [vmem] * 4,
        out_specs=[hbm] * 2 + [vmem] * 6,
        scratch_shapes=[
            pltpu.VMEM((rows, reach, width), BF16),
            pltpu.VMEM((rows, reach, width), BF16),
            pltpu.VMEM((rows, reach, width), BF16),
            pltpu.VMEM((rows, 2, EDGE, width), BF16),
            pltpu.VMEM((TAPS * width, width), BF16),
            pltpu.VMEM((width, hidden), BF16),
            pltpu.VMEM((hidden, width), BF16),
            pltpu.VMEM((2 * geo.chunks + 1, geo.tokens, width), BF16),
            pltpu.VMEM((length, TAPS * width), BF16),
            pltpu.VMEM((2 * geo.tokens, width // 2), BF16),
            pltpu.VMEM((geo.tokens, width), BF16),
            pltpu.VMEM((geo.tokens, width), BF16),
            pltpu.VMEM((geo.tokens, width), BF16),
            pltpu.VMEM((geo.tokens, 128), F32),
            pltpu.VMEM((rows, length, width), F32),
            pltpu.VMEM((rows, length, width), BF16),
            pltpu.VMEM((geo.tokens, width), BF16),
            pltpu.VMEM((geo.tokens, width), BF16),
            pltpu.VMEM((geo.tokens, width), BF16),
            pltpu.VMEM((geo.part_chunks, geo.tokens, width), BF16),
            pltpu.VMEM((geo.part_chunks, geo.tokens, width), BF16),
            pltpu.VMEM((rows, length, width), BF16),
            pltpu.VMEM((TAPS, rows, length), jnp.int32),
            pltpu.VMEM((TAPS, rows, length), jnp.int32),
            pltpu.VMEM((geo.tokens, 128), F32),
            pltpu.VMEM((geo.tokens, 128), F32),
            pltpu.VMEM((geo.tokens, 128), F32),
            pltpu.VMEM(slices, BF16),
            pltpu.VMEM(slices, BF16),
            pltpu.VMEM((16, width), F32),
            pltpu.VMEM((stages, 16, width), F32),
            pltpu.VMEM((stages, 16, width), F32),
            dma((3,)),
            dma((2,)),
            dma((2,)),
            dma((2,)),
            dma((2,)),
            dma((2,)),
            dma((rows, 3)),
            dma((rows, 3)),
            dma((rows,)),
            dma((rows,)),
            dma,
            dma,
            dma((rows, 4)),
            dma((rows, 4)),
            dma((rows,)),
            dma((rows,)),
            dma((rows,)),
            dma((rows,)),
            dma((rows,)),
            dma((rows,)),
            dma((rows, 2)),
            dma((rows, 2)),
            dma((rows,)),
            dma((rows,)),
            dma((rows,)),
            dma((rows,)),
            dma((geo.slices, len(geo.bits))),
            dma((geo.slices, len(geo.bits))),
            dma((stages,)),
            dma((stages,)),
        ],
        compiler_params=pltpu.CompilerParams(
            collective_id=0, has_side_effects=True, vmem_limit_bytes=63 * 2**20
        ),
    )(
        tokens,
        cotangent,
        jnp.transpose(conv_weight[0], (1, 0, 2)).reshape(TAPS * width, width),
        up_weight[0],
        down_weight[0],
        tap_masks[0],
        up_bias,
        jnp.transpose(norm_gains[0]),
        jnp.transpose(shift_terms[0]),
    )
    made = pl.pallas_call(
        hand_over,
        out_shape=[jax.ShapeDtypeStruct(array.shape, array.dtype) for array in made],
        in_specs=[hbm] * len(made),
        out_specs=[hbm] * len(made),
        scratch_shapes=[pltpu.VMEM(array.shape, array.dtype) for array in made] + [dma((len(made),))] * 2,
    )(*made)
    act, grads, conv_grad, up_grad, down_grad, bias_grad, gain_grad, shift_grad = made
    conv_grad = jnp.transpose(conv_grad, (1, 0, 2))
    if geo.low > 1:
        groups = [list(range(at, at + geo.low)) for at in range(0, seq, geo.low)]
        conv_grad, up_grad, down_grad = (
            lax.psum_scatter(
                grad, "seq", scatter_dimension=0, axis_index_groups=groups, tiled=True
            )
            for grad in (conv_grad, up_grad, down_grad)
        )
    return (
        act[None],
        grads[None],
        conv_grad[None],
        up_grad[None],
        bias_grad,
        down_grad[None],
        jnp.transpose(gain_grad)[None],
        jnp.transpose(shift_grad)[None],
    )


def solution(mesh):
    placed = (
        P("dp", "seq", None),
        P("dp", "seq", None),
        P("section", None, "dp", "seq"),
        P("section", None, None, None),
        P("section", None, None),
        P("section", None),
        P("section", None, None),
        P("section", None, None),
        P("section", None, None),
    )
    return jax.shard_map(
        functools.partial(per_device, mesh.shape["dp"], mesh.shape["seq"]),
        mesh=mesh,
        in_specs=placed,
        out_specs=(
            P("section", "dp", "seq", None),
            P("section", "dp", "seq", None),
            P("section", ("dp", "seq"), None, None),
            P("section", ("dp", "seq"), None),
            P("section", ("dp", "seq")),
            P("section", ("dp", "seq"), None),
            P("section", ("dp", "seq"), None),
            P("section", ("dp", "seq"), None),
        ),
        check_vma=False,
    )
```

```python
import functools

import jax
import jax.numpy as jnp
from jax import lax
from jax.experimental import pallas as pl
from jax.experimental.pallas import tpu as pltpu
from jax.sharding import PartitionSpec as P

TAPS = 9
CENTRE = TAPS // 2
TIGHT = 2
WIDE = 32
HALO = CENTRE * WIDE
EDGE = 16
EPS = 1e-05
MESH = pl.DeviceIdType.MESH
BF16 = jnp.bfloat16
F32 = jnp.float32
LAG = 3
FIRST_GROUPS = 2
PLAN = (
    ("conv", 4), ("conv", 3), ("conv", 1), (8, 0), ("other", 0), ("up", 1), (7, 0), (8, 1), ("conv", 0), (5, 0),
    ("first", 0), ("conv", 2), ("down", 0), (8, 2), ("up", 0), (4, 0), (7, 1), ("down", 1), (1, 0), (0, 0), (4, 1),
    (6, 0), (7, 2), (5, 1), (2, 0), (1, 1), (3, 0), (6, 1), (5, 2), (0, 1), ("first", 1), (5, 3), (7, 3), (4, 2),
    (3, 1), (2, 1), (6, 2), (1, 2), (8, 3), (0, 2), (3, 2), (6, 3), (4, 3), (1, 3), (0, 3), (2, 2),
)
ALONG = (5, 7, 8)
TANH_SCALE = 0.7978845608028654
TANH_CUBE = TANH_SCALE * 0.044715


def gelu_pair(z):
    square = z * z
    half = 0.5 + 0.5 * jnp.tanh(z * (TANH_SCALE + TANH_CUBE * square))
    value = z * half
    return value, half + value * (1.0 - half) * (2.0 * TANH_SCALE + 6.0 * TANH_CUBE * square)


def normalise(values):
    centred = values - jnp.mean(values, axis=-1, keepdims=True)
    scale = lax.rsqrt(jnp.mean(centred * centred, axis=-1, keepdims=True) + EPS)
    return centred * scale, scale


def norm_backward(weighted, unit):
    return (
        weighted
        - jnp.mean(weighted, axis=-1, keepdims=True)
        - unit * jnp.mean(weighted * unit, axis=-1, keepdims=True)
    )


def column_sum(values):
    return jnp.sum(values, axis=0, keepdims=True)


def dot(a, b):
    return jnp.dot(a, b, preferred_element_type=F32)


def dot_nt(a, b):
    return lax.dot_general(a, b, (((1,), (1,)), ((), ())), preferred_element_type=F32)


def dot_tn(a, b):
    return lax.dot_general(a, b, (((0,), (0,)), ((), ())), preferred_element_type=F32)


class Geometry:
    def __init__(self, dp, seq, rows, length, width, hidden):
        self.dp, self.seq = dp, seq
        self.rows, self.length, self.width = rows, length, width
        self.tokens = rows * length
        self.chunks = hidden // width
        self.low = max(1, 16 * dp * seq // width)
        self.owners = dp * seq // self.low
        self.share = width // self.owners
        self.final_share = width // (dp * seq)
        self.bias_share = hidden // (dp * seq)
        dp_bits = [("dp", 1 << i) for i in range(dp.bit_length() - 1)]
        seq_all = [("seq", 1 << i) for i in range(seq.bit_length() - 1)]
        seq_bits = [bit for bit in seq_all if bit[1] >= self.low]
        self.bits = dp_bits + seq_bits
        self.all_bits = dp_bits + seq_all
        self.dp_bits = dp_bits
        self.pairs = (TAPS + 1) // 2
        self.part_chunks = self.chunks // 2
        self.slices = 2 * self.part_chunks + self.pairs
        low_bit, high_bit, lines = dp_bits[:1], dp_bits[-1:], seq_bits
        self.orders = [low_bit + lines + high_bit] * self.part_chunks + [low_bit + lines] * self.part_chunks
        self.orders += [high_bit + lines + low_bit] * self.pairs
        for j in range(self.slices):
            if j in ALONG:
                self.orders[j] = lines[:1] + self.orders[j][:1] + self.orders[j][2:]
        planned = len(self.bits) == 4 and rows == 4 and self.chunks == 4
        self.plan = PLAN if planned else self.plain_plan()

    def plain_plan(self):
        first_down, first_conv = self.part_chunks, 2 * self.part_chunks
        work = [("other", 0)]
        work += [("down", i) for i in range(self.part_chunks)]
        work += [("up", i) for i in range(self.part_chunks)]
        work += [("conv", p) for p in range(self.pairs)]
        work += [("first", group) for group in range(FIRST_GROUPS)]
        due = {}
        for turn, (kind, at) in enumerate(work):
            begun = {"up": [at], "conv": [first_conv + at]}.get(kind, [])
            if kind == "down" and at == self.part_chunks - 1:
                begun = range(first_down, first_conv)
            for j in begun:
                for i in range(len(self.orders[j])):
                    due.setdefault(turn + LAG * (i + 1), []).append((j, i))
        plan = []
        for turn in range(max(max(due) + 1, len(work))):
            plan += work[turn : turn + 1] + due.get(turn, [])
        return plan


def body(
    geo,
    tokens_hbm,
    cotangent_hbm,
    conv_hbm,
    up_hbm,
    down_hbm,
    masks,
    bias,
    gains,
    shifts,
    act_hbm,
    grads_hbm,
    conv_out,
    up_out,
    down_out,
    bias_out,
    gain_out,
    shift_out,
    fields,
    conv_grads,
    near_edges,
    conv_w,
    up_w,
    down_w,
    slabs,
    taps,
    halves,
    unit_one,
    slope_one,
    unit_two,
    scale_two,
    mixed_grads,
    given,
    ffn_grads,
    mixed_other,
    ffn_grads_other,
    upper_other,
    hidden_other,
    results,
    masks_other,
    masks_second,
    columns,
    columns_second,
    conv_total,
    partial,
    arrived,
    sums,
    sums_sent,
    sums_arrived,
    load_sem,
    row_load_sem,
    token_edge_send,
    token_edge_recv,
    masks_send,
    masks_recv,
    pass_send,
    pass_recv,
    field_send,
    field_recv,
    weight_send,
    weight_recv,
    back_send,
    back_recv,
    half_send,
    half_recv,
    mixed_send,
    mixed_recv,
    ffn_send,
    ffn_recv,
    near_send,
    near_recv,
    act_sem,
    grads_sem,
    grads_send,
    grads_recv,
    part_send,
    part_recv,
    sums_send,
    sums_recv,
):
    rows, length, width, chunks = geo.rows, geo.length, geo.width, geo.chunks
    tokens, half_width = geo.tokens, geo.width // 2
    section = lax.axis_index("section")
    dp = lax.axis_index("dp")
    seq = lax.axis_index("seq")
    mine = {"dp": dp, "seq": seq}
    in_first = section == 0
    in_second = section == 1
    has_left = (seq + geo.seq - 1) // geo.seq
    has_right = 1 - (seq + 1) // geo.seq
    on_left, on_right = has_left == 1, has_right == 1
    own = slice(HALO, HALO + length)
    near = slice(HALO - EDGE, HALO + length + EDGE)

    def bit_of(bit):
        axis, size = bit
        return (mine[axis] // size) % 2

    def partner(bit):
        axis, size = bit
        other = mine[axis] + (1 - 2 * bit_of(bit)) * size
        return (section, other, seq) if axis == "dp" else (section, dp, other)

    def remote(source, target, sends, receives, device):
        return pltpu.make_async_remote_copy(
            src_ref=source,
            dst_ref=target,
            send_sem=sends,
            recv_sem=receives,
            device_id=device,
            device_id_type=MESH,
        )

    core = (1 - section, dp, seq)
    left, right = (section, dp, seq - 1), (section, dp, seq + 1)
    first_core, second_core = (0, dp, seq), (1, dp, seq)
    conv_bit, ffn_bit = geo.dp_bits[0], geo.dp_bits[-1]
    pair, ffn_pair = partner(conv_bit), partner(ffn_bit)
    my_half, my_part = bit_of(conv_bit), bit_of(ffn_bit)
    part_chunks = geo.part_chunks
    mine_at = pl.ds(pl.multiple_of(my_half * half_width, half_width), half_width)
    other_at = pl.ds(pl.multiple_of((1 - my_half) * half_width, half_width), half_width)

    loads = [
        pltpu.make_async_copy(conv_hbm, conv_w, load_sem.at[0]),
        pltpu.make_async_copy(up_hbm, up_w, load_sem.at[1]),
        pltpu.make_async_copy(down_hbm, down_w, load_sem.at[2]),
    ]
    token_load = pltpu.make_async_copy(tokens_hbm, fields.at[0:rows, own], row_load_sem.at[0])
    given_load = pltpu.make_async_copy(cotangent_hbm, given, row_load_sem.at[1])
    pl.when(in_first)(token_load.start)
    for load in loads:
        load.start()
    pl.when(in_second)(given_load.start)

    @pl.when(has_left == 0)
    def _():
        fields[0:rows, :HALO] = jnp.zeros((rows, HALO, width), BF16)
        conv_grads[:, :HALO] = jnp.zeros((rows, HALO, width), BF16)

    @pl.when(has_right == 0)
    def _():
        fields[0:rows, HALO + length :] = jnp.zeros((rows, HALO, width), BF16)
        conv_grads[:, HALO + length :] = jnp.zeros((rows, HALO, width), BF16)

    sums[...] = jnp.zeros(sums.shape, F32)

    barrier = pltpu.get_barrier_semaphore()

    def greet(device):
        pl.semaphore_signal(barrier, inc=1, device_id=device, device_id_type=MESH)

    for bit in geo.all_bits:
        greet(partner(bit))
    greet(core)
    for flag, at in ((on_left, seq - 1), (on_right, seq + 1)):

        @pl.when(flag)
        def _(at=at):
            greet((section, dp, at))
            greet((1 - section, dp, at))

    pl.semaphore_wait(barrier, len(geo.all_bits) + 1 + 2 * has_left + 2 * has_right)

    tokens_right = remote(
        tokens_hbm.at[:, length - EDGE : length],
        fields.at[0:rows, HALO - EDGE : HALO],
        token_edge_send.at[0],
        token_edge_recv.at[0],
        right,
    )
    tokens_left = remote(
        tokens_hbm.at[:, 0:EDGE],
        fields.at[0:rows, HALO + length : HALO + length + EDGE],
        token_edge_send.at[1],
        token_edge_recv.at[1],
        left,
    )

    @pl.when(in_first)
    def _():
        pl.when(on_right)(tokens_right.start)
        pl.when(on_left)(tokens_left.start)

    masks_across = remote(masks, masks_other, masks_send.at[0], masks_recv.at[0], pair)
    masks_back = remote(masks, masks_second, masks_send.at[1], masks_recv.at[1], first_core)
    masks_across.start()
    pl.when(in_second)(masks_back.start)

    def to_columns(source, target, base=0):
        for r in range(rows):
            plane = source[:, r, :].astype(F32)
            padded = jnp.concatenate([plane, jnp.zeros((128 - TAPS, length), F32)], axis=0)
            target[base + r * length : base + (r + 1) * length, :] = jnp.transpose(padded)

    to_columns(masks, columns)

    def span(m):
        return pl.ds(pl.multiple_of(m * length, length), length)

    def one_tap(source, mask_columns, m, k, dilation):
        values = source[m, pl.ds(HALO + (k - CENTRE) * dilation, length), :]
        if k == CENTRE:
            return values
        lane = jnp.broadcast_to(mask_columns[span(m), k : k + 1], (length, 128)).astype(BF16)
        return values * jnp.concatenate([lane] * (width // 128), axis=1)

    def pass_copies(m):
        return (
            remote(results.at[m], fields.at[m, own], pass_send.at[m, 0], pass_recv.at[m, 0], second_core),
            remote(
                results.at[m, length - HALO : length],
                fields.at[m, 0:HALO],
                pass_send.at[m, 1],
                pass_recv.at[m, 1],
                (1, dp, seq + 1),
            ),
            remote(
                results.at[m, 0:HALO],
                fields.at[m, HALO + length : HALO + length + HALO],
                pass_send.at[m, 2],
                pass_recv.at[m, 2],
                (1, dp, seq - 1),
            ),
        )

    def back_copies(m):
        return (
            remote(conv_grads.at[m, own], conv_grads.at[m, own], back_send.at[m, 0], back_recv.at[m, 0], first_core),
            remote(mixed_grads.at[m], mixed_grads.at[m], back_send.at[m, 1], back_recv.at[m, 1], first_core),
            remote(
                conv_grads.at[m, HALO + length - HALO : HALO + length],
                conv_grads.at[m, 0:HALO],
                back_send.at[m, 2],
                back_recv.at[m, 2],
                (0, dp, seq + 1),
            ),
            remote(
                conv_grads.at[m, HALO : HALO + HALO],
                conv_grads.at[m, HALO + length : HALO + length + HALO],
                back_send.at[m, 3],
                back_recv.at[m, 3],
                (0, dp, seq - 1),
            ),
        )

    def near_copies(m):
        return (
            remote(
                conv_grads.at[m, HALO + length - EDGE : HALO + length],
                near_edges.at[m, 0],
                near_send.at[m, 0],
                near_recv.at[m, 0],
                right,
            ),
            remote(
                conv_grads.at[m, HALO : HALO + EDGE],
                near_edges.at[m, 1],
                near_send.at[m, 1],
                near_recv.at[m, 1],
                left,
            ),
        )

    def field_copy(m):
        return remote(fields.at[m], fields.at[rows + m], field_send.at[m], field_recv.at[m], pair)

    near_fields = remote(
        fields.at[0:rows, near], fields.at[rows : 2 * rows, near], field_send.at[0], field_recv.at[0], pair
    )

    def half_copy(m):
        return remote(
            conv_grads.at[m, own, other_at],
            halves.at[pl.ds(pl.multiple_of(tokens + m * length, length), length)],
            half_send.at[m],
            half_recv.at[m],
            pair,
        )

    def mixed_copy(m):
        here = span(m)
        return remote(
            slabs.at[2 * chunks, here], mixed_other.at[here], mixed_send.at[m], mixed_recv.at[m], ffn_pair
        )

    def ffn_copy(m):
        here = span(m)
        return remote(ffn_grads.at[here], ffn_grads_other.at[here], ffn_send.at[m], ffn_recv.at[m], ffn_pair)

    weight_copy = remote(conv_w, conv_w, weight_send, weight_recv, first_core)

    def act_copy(m):
        return pltpu.make_async_copy(results.at[m], act_hbm.at[m], act_sem.at[m])

    def grads_copy(m):
        return pltpu.make_async_copy(mixed_grads.at[m], grads_hbm.at[m], grads_sem.at[m])

    def grads_across(m):
        return remote(mixed_grads.at[m], grads_hbm.at[m], grads_send.at[m], grads_recv.at[m], second_core)

    for load in loads:
        load.wait()

    @pl.when(in_first)
    def _():
        token_load.wait()
        pl.when(on_left)(tokens_right.wait_recv)
        pl.when(on_right)(tokens_left.wait_recv)
        near_fields.start()

    gain_one, gain_two = gains[0:1, :], gains[1:2, :]
    shift_conv, shift_one = shifts[0:1, :], shifts[1:2, :]
    shift_ffn, shift_two = shifts[2:3, :], shifts[3:4, :]

    def forward(m, carry):
        here = span(m)

        @pl.when(in_second)
        def _():
            whole, low, high = pass_copies(m)
            whole.wait_recv()
            pl.when(on_left)(low.wait_recv)
            pl.when(on_right)(high.wait_recv)
            field_copy(m).start()
            pl.when(m == rows - 1)(weight_copy.start)

        for flag, dilation in ((in_first, TIGHT), (in_second, WIDE)):

            @pl.when(flag)
            def _(dilation=dilation):
                for k in range(TAPS):
                    taps[:, k * width : (k + 1) * width] = one_tap(fields, columns, m, k, dilation)

        value, slope = gelu_pair(dot(taps[...], conv_w[...]) + shift_conv)
        unit, scale = normalise(value)
        unit_one[here, :] = unit.astype(BF16)
        slope_one[here, :] = (slope * scale).astype(BF16)
        mixed = fields[m, own, :].astype(F32) + unit * gain_one + shift_one
        mixed_low = mixed.astype(BF16)
        slabs[2 * chunks, here, :] = mixed_low
        mixed_copy(m).start()
        ffn = None
        for c in range(chunks):
            part = slice(c * width, (c + 1) * width)
            value, slope = gelu_pair(dot(mixed_low, up_w[:, part]) + bias[:, part])
            low = value.astype(BF16)
            slabs[c, here, :] = low
            slabs[chunks + c, here, :] = slope.astype(BF16)
            term = dot(low, down_w[part, :])
            ffn = term if ffn is None else ffn + term
        unit, scale = normalise(ffn + shift_ffn)
        unit_two[here, :] = unit.astype(BF16)
        scale_two[here, :] = jnp.broadcast_to(scale, (length, 128))
        results[m] = (mixed + unit * gain_two + shift_two).astype(BF16)
        act_copy(m).start()

        @pl.when(in_first)
        def _():
            whole, low, high = pass_copies(m)
            pl.when(on_right)(low.start)
            pl.when(on_left)(high.start)
            whole.start()

        return carry

    lax.fori_loop(0, rows, forward, 0)

    masks_across.wait_recv()
    to_columns(masks_other, columns, tokens)

    @pl.when(in_first)
    def _():
        masks_back.wait_recv()
        to_columns(masks_second, columns_second)

    def conv_back(m, mask_columns, dilation):
        grad = mixed_grads[m]
        for k in range(TAPS):
            at = (TAPS - 1 - k) * width
            grad = grad + dot_nt(one_tap(conv_grads, mask_columns, m, k, dilation), conv_w[at : at + width, :])
        return grad

    def chunk_of(i):
        return my_part * part_chunks + i

    def chunk_span(i):
        return pl.ds(pl.multiple_of(chunk_of(i) * width, width), width)

    def other_forward(m, carry):
        here = span(m)
        mixed_copy(m).wait_recv()
        for i in range(part_chunks):
            at = chunk_span(i)
            value, slope = gelu_pair(dot(mixed_other[here, :], up_w[:, at]) + bias[:, at])
            upper_other[i, here, :] = value.astype(BF16)
            hidden_other[i, here, :] = slope.astype(BF16)
        return carry

    def other_backward(m, carry):
        here = span(m)
        ffn_copy(m).wait_recv()
        for i in range(part_chunks):
            grad = dot_nt(ffn_grads_other[here, :], down_w[chunk_span(i), :])
            hidden_other[i, here, :] = (grad * hidden_other[i, here, :].astype(F32)).astype(BF16)
        return carry

    def second_input(m):
        whole, sides, low, high = back_copies(m)
        whole.wait_recv()
        sides.wait_recv()
        pl.when(on_left)(low.wait_recv)
        pl.when(on_right)(high.wait_recv)
        low = conv_back(m, columns_second, WIDE).astype(BF16)
        given[m] = low
        mixed_grads[m] = low.astype(F32)
        grads_across(m).start()

    @pl.when(in_first)
    def _():
        lax.fori_loop(0, rows, other_forward, 0)
        weight_copy.wait_recv()

    pl.when(in_second)(given_load.wait)

    def backward_ffn(m, carry):
        pl.when(in_first)(lambda: second_input(m))
        here = span(m)
        grad = given[m].astype(F32)
        unit = unit_two[here, :].astype(F32)
        grad_ffn = norm_backward(grad * gain_two, unit) * scale_two[here, 0:1]
        sums[1:2, :] += column_sum(grad * unit)
        sums[5:6, :] += column_sum(grad)
        sums[4:5, :] += column_sum(grad_ffn)
        grad_ffn_low = grad_ffn.astype(BF16)
        ffn_grads[here, :] = grad_ffn_low
        ffn_copy(m).start()
        mixed = grad
        for c in range(chunks):
            part = slice(c * width, (c + 1) * width)
            grad_hidden = dot_nt(grad_ffn_low, down_w[part, :]) * slabs[chunks + c, here, :].astype(F32)
            sums[8 + c : 9 + c, :] += column_sum(grad_hidden)
            low = grad_hidden.astype(BF16)
            slabs[chunks + c, here, :] = low
            mixed = mixed + dot_nt(low, up_w[:, part])
        pl.when(in_first)(grads_across(m).wait_send)
        mixed_grads[m] = mixed
        unit = unit_one[here, :].astype(F32)
        grad_conv = norm_backward(mixed * gain_one, unit) * slope_one[here, :].astype(F32)
        sums[0:1, :] += column_sum(mixed * unit)
        sums[3:4, :] += column_sum(mixed)
        sums[2:3, :] += column_sum(grad_conv)
        conv_grads[m, own, :] = grad_conv.astype(BF16)

        @pl.when(in_second)
        def _():
            whole, sides, low, high = back_copies(m)
            pl.when(on_right)(low.start)
            pl.when(on_left)(high.start)
            whole.start()
            sides.start()

        @pl.when(in_first)
        def _():
            low, high = near_copies(m)
            pl.when(on_right)(low.start)
            pl.when(on_left)(high.start)

        half_copy(m).start()
        halves[here, :] = conv_grads[m, own, mine_at]
        return carry

    lax.fori_loop(0, rows, backward_ffn, 0)
    pl.when(in_first)(loads[0].start)

    @pl.when(in_second)
    def _():
        lax.fori_loop(0, rows, other_forward, 0)

    def sums_copy(i):
        return remote(
            sums_sent.at[i], sums_arrived.at[i], sums_send.at[i], sums_recv.at[i], partner(geo.all_bits[i])
        )

    def sums_begin(i):
        sums_sent[i] = sums[...]
        sums_copy(i).start()

    def sums_end(i):
        sums_copy(i).wait_recv()
        sums[...] += sums_arrived[i]

    owners, share = geo.owners, geo.share
    my_bits = {bit: bit_of(bit) for bit in geo.bits}
    partners = {bit: partner(bit) for bit in geo.bits}
    per_dp = geo.seq // geo.low
    first_down, first_conv = part_chunks, 2 * part_chunks

    def columns_of(j):
        single = j == geo.slices - 1 and TAPS % 2 == 1
        return slice(0, half_width) if single else slice(0, width)

    def place(j, owner_dp, owner_seq):
        where = 0
        weight = owners
        for axis, size in geo.orders[j]:
            weight //= 2
            index = owner_dp if axis == "dp" else owner_seq * geo.low
            where = where + ((index // size) % 2 + my_bits[axis, size]) % 2 * weight
        return where

    def part_copy(j, i):
        half, at = owners >> (i + 1), columns_of(j)
        return remote(
            partial.at[j, half : 2 * half, :, at],
            arrived.at[j, half : 2 * half, :, at],
            part_send.at[j, i],
            part_recv.at[j, i],
            partners[geo.orders[j][i]],
        )

    def total_of(j, i):
        half, at = owners >> (i + 1), columns_of(j)
        return partial[j, 0:half, :, at].astype(F32) + arrived[j, half : 2 * half, :, at].astype(F32)

    def advance(j, i):
        part_copy(j, i - 1).wait_recv()
        partial[j, 0 : owners >> i, :, columns_of(j)] = total_of(j, i - 1).astype(BF16)
        part_copy(j, i).start()

    def finish(j):
        last = len(geo.orders[j]) - 1
        part_copy(j, last).wait_recv()
        if j < first_down:
            for part, total in ((my_part, partial[j, 0]), (1 - my_part, arrived[j, 1])):
                at = (part * part_chunks + j) * width
                up_out[:, pl.ds(pl.multiple_of(at, width), width)] = total.astype(F32)
        elif j < first_conv:
            total = total_of(j, last)
            for r in range(2):
                at = (2 * (j - first_down) + r) * share
                down_out[at : at + share, :] = total[r]
        else:
            for q in range(2):
                k = 2 * (j - first_conv) + q
                if k < TAPS:
                    at = slice(q * half_width, (q + 1) * half_width)
                    conv_out[k, :, mine_at] = partial[j, 0, :, at].astype(F32)
                    conv_out[k, :, other_at] = arrived[j, 1, :, at].astype(F32)

    def up_slice(j):
        places = [place(j, owner // per_dp, owner % per_dp) for owner in range(owners)]

        def half(n, carry):
            at = pl.ds(pl.multiple_of(n * half_width, half_width), half_width)
            grad = dot_tn(slabs[2 * chunks], slabs[chunks + chunk_of(j), :, at])
            grad = grad + dot_tn(mixed_other[...], hidden_other[j, :, at])
            for owner in range(owners):
                partial[j, places[owner], :, at] = grad[owner * share : (owner + 1) * share].astype(BF16)
            return carry

        lax.fori_loop(0, 2, half, 0)
        part_copy(j, 0).start()

    def down_slab(i):
        each = owners // chunks
        places = {
            (w, s): place(first_down + s, (chunk_of(i) * each + w) // per_dp, (chunk_of(i) * each + w) % per_dp)
            for w in range(each)
            for s in range(part_chunks)
        }

        def half(n, carry):
            at = pl.ds(pl.multiple_of(n * half_width, half_width), half_width)
            grad = dot_tn(slabs[chunk_of(i)], ffn_grads[:, at])
            grad = grad + dot_tn(upper_other[i], ffn_grads_other[:, at])
            for (w, s), where in places.items():
                for r in range(2):
                    low = ((w * part_chunks + s) * 2 + r) * share
                    partial[first_down + s, where + r, :, at] = grad[low : low + share].astype(BF16)
            return carry

        lax.fori_loop(0, 2, half, 0)
        if i == part_chunks - 1:
            for s in range(part_chunks):
                part_copy(first_down + s, 0).start()

    conv_begun = []

    def conv_slice(p):
        j = first_conv + p
        if not conv_begun:
            conv_begun.append(p)
            for m in range(rows):
                half_copy(m).wait_recv()
            pl.when(in_first)(near_fields.wait_recv)

            @pl.when(in_second)
            def _():
                for m in range(rows):
                    field_copy(m).wait_recv()

        for q in range(2):
            k = 2 * p + q
            if k >= TAPS:
                continue
            at = slice(q * half_width, (q + 1) * half_width)
            places = [place(j, owner // per_dp, owner % per_dp) for owner in range(owners)]
            for flag, dilation in ((in_first, TIGHT), (in_second, WIDE)):

                @pl.when(flag)
                def _(dilation=dilation):
                    def side(chip, carry):
                        grad = None
                        for r in range(rows):
                            m = chip * rows + r
                            term = dot_tn(one_tap(fields, columns, m, k, dilation), halves[span(m), :])
                            grad = term if grad is None else grad + term
                        conv_total[...] = jnp.where(chip == 0, grad, conv_total[...] + grad)
                        return carry

                    lax.fori_loop(0, 2, side, 0)

            for owner in range(owners):
                partial[j, places[owner], :, at] = conv_total[owner * share : (owner + 1) * share].astype(BF16)
        part_copy(j, 0).start()

    input_begun = []

    def first_input(m, carry):
        low, high = near_copies(m)

        @pl.when(on_left)
        def _():
            low.wait_recv()
            conv_grads[m, HALO - EDGE : HALO, :] = near_edges[m, 0]

        @pl.when(on_right)
        def _():
            high.wait_recv()
            conv_grads[m, HALO + length : HALO + length + EDGE, :] = near_edges[m, 1]

        mixed_grads[m] = conv_back(m, columns, TIGHT)
        grads_copy(m).start()
        return carry

    def first_inputs(group):
        if not input_begun:
            input_begun.append(group)
            loads[0].wait()
        each = rows // FIRST_GROUPS
        lax.fori_loop(group * each, (group + 1) * each, first_input, 0)

    def share_sums():
        index = dp * geo.seq + seq
        lane = lax.broadcasted_iota(jnp.int32, (128, width), 1)
        line = lax.broadcasted_iota(jnp.int32, (128, width), 0)
        exact = functools.partial(
            lax.dot_general,
            dimension_numbers=(((1,), (1,)), ((), ())),
            precision=lax.Precision.HIGHEST,
            preferred_element_type=F32,
        )
        picked = exact(sums[...], (lane == line + index * geo.final_share).astype(F32))
        gain_out[...] = picked[0:2, : geo.final_share]
        shift_out[...] = picked[2:6, : geo.final_share]
        start = index * geo.bias_share
        picked = exact(sums[...], (lane == line + start % width).astype(F32))
        wanted = lax.broadcasted_iota(jnp.int32, picked.shape, 0) == 8 + start // width
        bias_out[...] = column_sum(jnp.where(wanted, picked, 0.0))[:, : geo.bias_share]

    def gradients_back():
        lax.fori_loop(0, rows, other_backward, 0)

    def work_of(kind, at):
        if kind == "first":
            return lambda: pl.when(in_first)(lambda: first_inputs(at))
        if kind == "other":
            return gradients_back
        return functools.partial({"up": up_slice, "down": down_slab, "conv": conv_slice}[kind], at)

    sums_begin(0)
    stride = 6
    sums_done = 0
    for at, (what, which) in enumerate(geo.plan):
        if isinstance(what, str):
            work_of(what, which)()
        elif which + 1 < len(geo.orders[what]):
            advance(what, which + 1)
        else:
            finish(what)
        if (at + 1) % stride == 0 and sums_done < len(geo.all_bits):
            sums_end(sums_done)
            sums_done += 1
            if sums_done < len(geo.all_bits):
                sums_begin(sums_done)
            else:
                share_sums()

    for j in range(geo.slices):
        for i in range(len(geo.orders[j])):
            part_copy(j, i).wait_send()
    for i in range(len(geo.all_bits)):
        sums_copy(i).wait_send()
    masks_across.wait_send()

    def settle_row(m, carry):
        act_copy(m).wait()
        half_copy(m).wait_send()
        mixed_copy(m).wait_send()
        ffn_copy(m).wait_send()

        @pl.when(in_first)
        def _():
            grads_copy(m).wait()
            whole, low, high = pass_copies(m)
            pl.when(on_right)(low.wait_send)
            pl.when(on_left)(high.wait_send)
            whole.wait_send()
            low, high = near_copies(m)
            pl.when(on_right)(low.wait_send)
            pl.when(on_left)(high.wait_send)

        @pl.when(in_second)
        def _():
            field_copy(m).wait_send()
            whole, sides, low, high = back_copies(m)
            pl.when(on_right)(low.wait_send)
            pl.when(on_left)(high.wait_send)
            whole.wait_send()
            sides.wait_send()
            grads_across(m).wait_recv()

        return carry

    lax.fori_loop(0, rows, settle_row, 0)

    @pl.when(in_first)
    def _():
        pl.when(on_right)(tokens_right.wait_send)
        pl.when(on_left)(tokens_left.wait_send)
        near_fields.wait_send()

    @pl.when(in_second)
    def _():
        masks_back.wait_send()
        weight_copy.wait_send()


def hand_over(*refs):
    sems_in, sems_out = refs[-2:]
    count = len(refs) // 3
    sources, targets, held = refs[:count], refs[count : 2 * count], refs[2 * count : 3 * count]
    copies_in = [pltpu.make_async_copy(sources[i], held[i], sems_in.at[i]) for i in range(count)]
    copies_out = [pltpu.make_async_copy(held[i], targets[i], sems_out.at[i]) for i in range(count)]
    for copy in copies_in:
        copy.start()
    for i in range(count):
        copies_in[i].wait()
        copies_out[i].start()
    for copy in copies_out:
        copy.wait()


def per_device(
    dp,
    seq,
    tokens,
    cotangent,
    tap_masks,
    conv_weight,
    up_weight,
    up_bias,
    down_weight,
    norm_gains,
    shift_terms,
):
    rows, length, width = tokens.shape
    hidden = up_weight.shape[2]
    geo = Geometry(dp, seq, rows, length, width, hidden)
    reach = length + 2 * HALO
    vmem = pl.BlockSpec(memory_space=pltpu.VMEM)
    hbm = pl.BlockSpec(memory_space=pl.ANY)
    dma = pltpu.SemaphoreType.DMA
    stages = len(geo.all_bits)
    slices = (geo.slices, geo.owners, geo.share, width)
    made = pl.pallas_call(
        functools.partial(body, geo),
        out_shape=[
            jax.ShapeDtypeStruct((rows, length, width), BF16),
            jax.ShapeDtypeStruct((rows, length, width), F32),
            jax.ShapeDtypeStruct((TAPS, geo.share, width), F32),
            jax.ShapeDtypeStruct((geo.share, hidden), F32),
            jax.ShapeDtypeStruct((geo.chunks * geo.share, width), F32),
            jax.ShapeDtypeStruct((1, geo.bias_share), F32),
            jax.ShapeDtypeStruct((2, geo.final_share), F32),
            jax.ShapeDtypeStruct((4, geo.final_share), F32),
        ],
        in_specs=[hbm] * 5 + [vmem] * 4,
        out_specs=[hbm] * 2 + [vmem] * 6,
        scratch_shapes=[
            pltpu.VMEM((2 * rows, reach, width), BF16),
            pltpu.VMEM((rows, reach, width), BF16),
            pltpu.VMEM((rows, 2, EDGE, width), BF16),
            pltpu.VMEM((TAPS * width, width), BF16),
            pltpu.VMEM((width, hidden), BF16),
            pltpu.VMEM((hidden, width), BF16),
            pltpu.VMEM((2 * geo.chunks + 1, geo.tokens, width), BF16),
            pltpu.VMEM((length, TAPS * width), BF16),
            pltpu.VMEM((2 * geo.tokens, width // 2), BF16),
            pltpu.VMEM((geo.tokens, width), BF16),
            pltpu.VMEM((geo.tokens, width), BF16),
            pltpu.VMEM((geo.tokens, width), BF16),
            pltpu.VMEM((geo.tokens, 128), F32),
            pltpu.VMEM((rows, length, width), F32),
            pltpu.VMEM((rows, length, width), BF16),
            pltpu.VMEM((geo.tokens, width), BF16),
            pltpu.VMEM((geo.tokens, width), BF16),
            pltpu.VMEM((geo.tokens, width), BF16),
            pltpu.VMEM((geo.part_chunks, geo.tokens, width), BF16),
            pltpu.VMEM((geo.part_chunks, geo.tokens, width), BF16),
            pltpu.VMEM((rows, length, width), BF16),
            pltpu.VMEM((TAPS, rows, length), jnp.int32),
            pltpu.VMEM((TAPS, rows, length), jnp.int32),
            pltpu.VMEM((2 * geo.tokens, 128), F32),
            pltpu.VMEM((geo.tokens, 128), F32),
            pltpu.VMEM((width, width // 2), F32),
            pltpu.VMEM(slices, BF16),
            pltpu.VMEM(slices, BF16),
            pltpu.VMEM((16, width), F32),
            pltpu.VMEM((stages, 16, width), F32),
            pltpu.VMEM((stages, 16, width), F32),
            dma((3,)),
            dma((2,)),
            dma((2,)),
            dma((2,)),
            dma((2,)),
            dma((2,)),
            dma((rows, 3)),
            dma((rows, 3)),
            dma((rows,)),
            dma((rows,)),
            dma,
            dma,
            dma((rows, 4)),
            dma((rows, 4)),
            dma((rows,)),
            dma((rows,)),
            dma((rows,)),
            dma((rows,)),
            dma((rows,)),
            dma((rows,)),
            dma((rows, 2)),
            dma((rows, 2)),
            dma((rows,)),
            dma((rows,)),
            dma((rows,)),
            dma((rows,)),
            dma((geo.slices, len(geo.bits))),
            dma((geo.slices, len(geo.bits))),
            dma((stages,)),
            dma((stages,)),
        ],
        compiler_params=pltpu.CompilerParams(
            collective_id=0, has_side_effects=True, vmem_limit_bytes=63 * 2**20
        ),
    )(
        tokens,
        cotangent,
        jnp.transpose(conv_weight[0], (1, 0, 2)).reshape(TAPS * width, width),
        up_weight[0],
        down_weight[0],
        tap_masks[0],
        up_bias,
        jnp.transpose(norm_gains[0]),
        jnp.transpose(shift_terms[0]),
    )
    made = pl.pallas_call(
        hand_over,
        out_shape=[jax.ShapeDtypeStruct(array.shape, array.dtype) for array in made],
        in_specs=[hbm] * len(made),
        out_specs=[hbm] * len(made),
        scratch_shapes=[pltpu.VMEM(array.shape, array.dtype) for array in made] + [dma((len(made),))] * 2,
    )(*made)
    act, grads, conv_grad, up_grad, down_grad, bias_grad, gain_grad, shift_grad = made
    conv_grad = jnp.transpose(conv_grad, (1, 0, 2))
    if geo.low > 1:
        groups = [list(range(at, at + geo.low)) for at in range(0, seq, geo.low)]
        conv_grad, up_grad, down_grad = (
            lax.psum_scatter(
                grad, "seq", scatter_dimension=0, axis_index_groups=groups, tiled=True
            )
            for grad in (conv_grad, up_grad, down_grad)
        )
    return (
        act[None],
        grads[None],
        conv_grad[None],
        up_grad[None],
        bias_grad,
        down_grad[None],
        jnp.transpose(gain_grad)[None],
        jnp.transpose(shift_grad)[None],
    )


def solution(mesh):
    placed = (
        P("dp", "seq", None),
        P("dp", "seq", None),
        P("section", None, "dp", "seq"),
        P("section", None, None, None),
        P("section", None, None),
        P("section", None),
        P("section", None, None),
        P("section", None, None),
        P("section", None, None),
    )
    return jax.shard_map(
        functools.partial(per_device, mesh.shape["dp"], mesh.shape["seq"]),
        mesh=mesh,
        in_specs=placed,
        out_specs=(
            P("section", "dp", "seq", None),
            P("section", "dp", "seq", None),
            P("section", ("dp", "seq"), None, None),
            P("section", ("dp", "seq"), None),
            P("section", ("dp", "seq")),
            P("section", ("dp", "seq"), None),
            P("section", ("dp", "seq"), None),
            P("section", ("dp", "seq"), None),
        ),
        check_vma=False,
    )
```

```python
import functools

import jax
import jax.numpy as jnp
from jax import lax
from jax.experimental import pallas as pl
from jax.experimental.pallas import tpu as pltpu
from jax.sharding import PartitionSpec as P

TAPS = 9
CENTRE = TAPS // 2
TIGHT = 2
WIDE = 32
HALO = CENTRE * WIDE
EDGE = 16
EPS = 1e-05
MESH = pl.DeviceIdType.MESH
BF16 = jnp.bfloat16
F32 = jnp.float32
LAG = 3
FIRST_GROUPS = 2
PLAN = (
    ("first", 0), ("conv", 4), ("conv", 3), ("conv", 1), (8, 0), ("other", 0), ("up", 1), (7, 0), ("first", 1),
    (8, 1), ("conv", 0), (5, 0), ("conv", 2), ("down", 0), (8, 2), ("up", 0), (4, 0), (7, 1), ("down", 1), (1, 0),
    (0, 0), (4, 1), (6, 0), (7, 2), (5, 1), (2, 0), (1, 1), (3, 0), (6, 1), (5, 2), (0, 1), (5, 3), (7, 3), (4, 2),
    (3, 1), (2, 1), (6, 2), (1, 2), (8, 3), (0, 2), (3, 2), (6, 3), (4, 3), (1, 3), (0, 3), (2, 2),
)
ALONG = (5, 7, 8)
TANH_SCALE = 0.7978845608028654
TANH_CUBE = TANH_SCALE * 0.044715


def gelu_pair(z):
    square = z * z
    half = 0.5 + 0.5 * jnp.tanh(z * (TANH_SCALE + TANH_CUBE * square))
    value = z * half
    return value, half + value * (1.0 - half) * (2.0 * TANH_SCALE + 6.0 * TANH_CUBE * square)


def normalise(values):
    centred = values - jnp.mean(values, axis=-1, keepdims=True)
    scale = lax.rsqrt(jnp.mean(centred * centred, axis=-1, keepdims=True) + EPS)
    return centred * scale, scale


def norm_backward(weighted, unit):
    return (
        weighted
        - jnp.mean(weighted, axis=-1, keepdims=True)
        - unit * jnp.mean(weighted * unit, axis=-1, keepdims=True)
    )


def column_sum(values):
    return jnp.sum(values, axis=0, keepdims=True)


def dot(a, b):
    return jnp.dot(a, b, preferred_element_type=F32)


def dot_nt(a, b):
    return lax.dot_general(a, b, (((1,), (1,)), ((), ())), preferred_element_type=F32)


def dot_tn(a, b):
    return lax.dot_general(a, b, (((0,), (0,)), ((), ())), preferred_element_type=F32)


class Geometry:
    def __init__(self, dp, seq, rows, length, width, hidden):
        self.dp, self.seq = dp, seq
        self.rows, self.length, self.width = rows, length, width
        self.tokens = rows * length
        self.chunks = hidden // width
        self.low = max(1, 16 * dp * seq // width)
        self.owners = dp * seq // self.low
        self.share = width // self.owners
        self.final_share = width // (dp * seq)
        self.bias_share = hidden // (dp * seq)
        dp_bits = [("dp", 1 << i) for i in range(dp.bit_length() - 1)]
        seq_all = [("seq", 1 << i) for i in range(seq.bit_length() - 1)]
        seq_bits = [bit for bit in seq_all if bit[1] >= self.low]
        self.bits = dp_bits + seq_bits
        self.all_bits = dp_bits + seq_all
        self.dp_bits = dp_bits
        self.pairs = (TAPS + 1) // 2
        self.part_chunks = self.chunks // 2
        self.slices = 2 * self.part_chunks + self.pairs
        low_bit, high_bit, lines = dp_bits[:1], dp_bits[-1:], seq_bits
        self.orders = [low_bit + lines + high_bit] * self.part_chunks + [low_bit + lines] * self.part_chunks
        self.orders += [high_bit + lines + low_bit] * self.pairs
        for j in range(self.slices):
            if j in ALONG:
                self.orders[j] = lines[:1] + self.orders[j][:1] + self.orders[j][2:]
        planned = len(self.bits) == 4 and rows == 4 and self.chunks == 4
        self.plan = PLAN if planned else self.plain_plan()

    def plain_plan(self):
        first_down, first_conv = self.part_chunks, 2 * self.part_chunks
        work = [("other", 0)]
        work += [("down", i) for i in range(self.part_chunks)]
        work += [("up", i) for i in range(self.part_chunks)]
        work += [("conv", p) for p in range(self.pairs)]
        work += [("first", group) for group in range(FIRST_GROUPS)]
        due = {}
        for turn, (kind, at) in enumerate(work):
            begun = {"up": [at], "conv": [first_conv + at]}.get(kind, [])
            if kind == "down" and at == self.part_chunks - 1:
                begun = range(first_down, first_conv)
            for j in begun:
                for i in range(len(self.orders[j])):
                    due.setdefault(turn + LAG * (i + 1), []).append((j, i))
        plan = []
        for turn in range(max(max(due) + 1, len(work))):
            plan += work[turn : turn + 1] + due.get(turn, [])
        return plan


def body(
    geo,
    tokens_hbm,
    cotangent_hbm,
    conv_hbm,
    up_hbm,
    down_hbm,
    masks,
    bias,
    gains,
    shifts,
    act_hbm,
    grads_hbm,
    conv_out,
    up_out,
    down_out,
    bias_out,
    gain_out,
    shift_out,
    fields,
    conv_grads,
    near_edges,
    conv_w,
    up_w,
    down_w,
    slabs,
    taps,
    halves,
    unit_one,
    slope_one,
    unit_two,
    scale_two,
    mixed_grads,
    given,
    ffn_grads,
    mixed_other,
    ffn_grads_other,
    upper_other,
    hidden_other,
    results,
    masks_other,
    masks_second,
    columns,
    columns_second,
    conv_total,
    partial,
    arrived,
    sums,
    sums_sent,
    sums_arrived,
    load_sem,
    row_load_sem,
    token_edge_send,
    token_edge_recv,
    masks_send,
    masks_recv,
    pass_send,
    pass_recv,
    field_send,
    field_recv,
    weight_send,
    weight_recv,
    back_send,
    back_recv,
    half_send,
    half_recv,
    mixed_send,
    mixed_recv,
    ffn_send,
    ffn_recv,
    near_send,
    near_recv,
    act_sem,
    grads_sem,
    grads_send,
    grads_recv,
    part_send,
    part_recv,
    sums_send,
    sums_recv,
):
    rows, length, width, chunks = geo.rows, geo.length, geo.width, geo.chunks
    tokens, half_width = geo.tokens, geo.width // 2
    section = lax.axis_index("section")
    dp = lax.axis_index("dp")
    seq = lax.axis_index("seq")
    mine = {"dp": dp, "seq": seq}
    in_first = section == 0
    in_second = section == 1
    has_left = (seq + geo.seq - 1) // geo.seq
    has_right = 1 - (seq + 1) // geo.seq
    on_left, on_right = has_left == 1, has_right == 1
    own = slice(HALO, HALO + length)
    near = slice(HALO - EDGE, HALO + length + EDGE)

    def bit_of(bit):
        axis, size = bit
        return (mine[axis] // size) % 2

    def partner(bit):
        axis, size = bit
        other = mine[axis] + (1 - 2 * bit_of(bit)) * size
        return (section, other, seq) if axis == "dp" else (section, dp, other)

    def remote(source, target, sends, receives, device):
        return pltpu.make_async_remote_copy(
            src_ref=source,
            dst_ref=target,
            send_sem=sends,
            recv_sem=receives,
            device_id=device,
            device_id_type=MESH,
        )

    core = (1 - section, dp, seq)
    left, right = (section, dp, seq - 1), (section, dp, seq + 1)
    first_core, second_core = (0, dp, seq), (1, dp, seq)
    conv_bit, ffn_bit = geo.dp_bits[0], geo.dp_bits[-1]
    pair, ffn_pair = partner(conv_bit), partner(ffn_bit)
    my_half, my_part = bit_of(conv_bit), bit_of(ffn_bit)
    part_chunks = geo.part_chunks
    mine_at = pl.ds(pl.multiple_of(my_half * half_width, half_width), half_width)
    other_at = pl.ds(pl.multiple_of((1 - my_half) * half_width, half_width), half_width)

    loads = [
        pltpu.make_async_copy(conv_hbm, conv_w, load_sem.at[0]),
        pltpu.make_async_copy(up_hbm, up_w, load_sem.at[1]),
        pltpu.make_async_copy(down_hbm, down_w, load_sem.at[2]),
    ]
    token_load = pltpu.make_async_copy(tokens_hbm, fields.at[0:rows, own], row_load_sem.at[0])
    given_load = pltpu.make_async_copy(cotangent_hbm, given, row_load_sem.at[1])
    pl.when(in_first)(token_load.start)
    for load in loads:
        load.start()
    pl.when(in_second)(given_load.start)

    barrier = pltpu.get_barrier_semaphore()

    def greet(device):
        pl.semaphore_signal(barrier, inc=1, device_id=device, device_id_type=MESH)

    for bit in geo.all_bits:
        greet(partner(bit))
    greet(core)
    for flag, at in ((on_left, seq - 1), (on_right, seq + 1)):

        @pl.when(flag)
        def _(at=at):
            greet((section, dp, at))
            greet((1 - section, dp, at))

    @pl.when(has_left == 0)
    def _():
        fields[0:rows, :HALO] = jnp.zeros((rows, HALO, width), BF16)
        conv_grads[:, :HALO] = jnp.zeros((rows, HALO, width), BF16)

    @pl.when(has_right == 0)
    def _():
        fields[0:rows, HALO + length :] = jnp.zeros((rows, HALO, width), BF16)
        conv_grads[:, HALO + length :] = jnp.zeros((rows, HALO, width), BF16)

    sums[...] = jnp.zeros(sums.shape, F32)
    pl.semaphore_wait(barrier, len(geo.all_bits) + 1 + 2 * has_left + 2 * has_right)

    tokens_right = remote(
        tokens_hbm.at[:, length - EDGE : length],
        fields.at[0:rows, HALO - EDGE : HALO],
        token_edge_send.at[0],
        token_edge_recv.at[0],
        right,
    )
    tokens_left = remote(
        tokens_hbm.at[:, 0:EDGE],
        fields.at[0:rows, HALO + length : HALO + length + EDGE],
        token_edge_send.at[1],
        token_edge_recv.at[1],
        left,
    )

    @pl.when(in_first)
    def _():
        pl.when(on_right)(tokens_right.start)
        pl.when(on_left)(tokens_left.start)

    masks_across = remote(masks, masks_other, masks_send.at[0], masks_recv.at[0], pair)
    masks_back = remote(masks, masks_second, masks_send.at[1], masks_recv.at[1], first_core)
    masks_across.start()
    pl.when(in_second)(masks_back.start)

    def to_columns(source, target, base=0):
        for r in range(rows):
            plane = source[:, r, :].astype(F32)
            padded = jnp.concatenate([plane, jnp.zeros((128 - TAPS, length), F32)], axis=0)
            target[base + r * length : base + (r + 1) * length, :] = jnp.transpose(padded)

    to_columns(masks, columns)

    def span(m):
        return pl.ds(pl.multiple_of(m * length, length), length)

    def one_tap(source, mask_columns, m, k, dilation):
        values = source[m, pl.ds(HALO + (k - CENTRE) * dilation, length), :]
        if k == CENTRE:
            return values
        lane = jnp.broadcast_to(mask_columns[span(m), k : k + 1], (length, 128)).astype(BF16)
        return values * jnp.concatenate([lane] * (width // 128), axis=1)

    def pass_copies(m):
        return (
            remote(results.at[m], fields.at[m, own], pass_send.at[m, 0], pass_recv.at[m, 0], second_core),
            remote(
                results.at[m, length - HALO : length],
                fields.at[m, 0:HALO],
                pass_send.at[m, 1],
                pass_recv.at[m, 1],
                (1, dp, seq + 1),
            ),
            remote(
                results.at[m, 0:HALO],
                fields.at[m, HALO + length : HALO + length + HALO],
                pass_send.at[m, 2],
                pass_recv.at[m, 2],
                (1, dp, seq - 1),
            ),
        )

    def back_copies(m):
        return (
            remote(conv_grads.at[m, own], conv_grads.at[m, own], back_send.at[m, 0], back_recv.at[m, 0], first_core),
            remote(mixed_grads.at[m], mixed_grads.at[m], back_send.at[m, 1], back_recv.at[m, 1], first_core),
            remote(
                conv_grads.at[m, HALO + length - HALO : HALO + length],
                conv_grads.at[m, 0:HALO],
                back_send.at[m, 2],
                back_recv.at[m, 2],
                (0, dp, seq + 1),
            ),
            remote(
                conv_grads.at[m, HALO : HALO + HALO],
                conv_grads.at[m, HALO + length : HALO + length + HALO],
                back_send.at[m, 3],
                back_recv.at[m, 3],
                (0, dp, seq - 1),
            ),
        )

    def near_copies(m):
        return (
            remote(
                conv_grads.at[m, HALO + length - EDGE : HALO + length],
                near_edges.at[m, 0],
                near_send.at[m, 0],
                near_recv.at[m, 0],
                right,
            ),
            remote(
                conv_grads.at[m, HALO : HALO + EDGE],
                near_edges.at[m, 1],
                near_send.at[m, 1],
                near_recv.at[m, 1],
                left,
            ),
        )

    def field_copy(m):
        return remote(fields.at[m], fields.at[rows + m], field_send.at[m], field_recv.at[m], pair)

    near_fields = remote(
        fields.at[0:rows, near], fields.at[rows : 2 * rows, near], field_send.at[0], field_recv.at[0], pair
    )

    def half_copy(m):
        return remote(
            conv_grads.at[m, own, other_at],
            halves.at[pl.ds(pl.multiple_of(tokens + m * length, length), length)],
            half_send.at[m],
            half_recv.at[m],
            pair,
        )

    def mixed_copy(m):
        here = span(m)
        return remote(
            slabs.at[2 * chunks, here], mixed_other.at[here], mixed_send.at[m], mixed_recv.at[m], ffn_pair
        )

    def ffn_copy(m):
        here = span(m)
        return remote(ffn_grads.at[here], ffn_grads_other.at[here], ffn_send.at[m], ffn_recv.at[m], ffn_pair)

    weight_copy = remote(conv_w, conv_w, weight_send, weight_recv, first_core)

    def act_copy(m):
        return pltpu.make_async_copy(results.at[m], act_hbm.at[m], act_sem.at[m])

    def grads_copy(m):
        return pltpu.make_async_copy(mixed_grads.at[m], grads_hbm.at[m], grads_sem.at[m])

    def grads_across(m):
        return remote(mixed_grads.at[m], grads_hbm.at[m], grads_send.at[m], grads_recv.at[m], second_core)

    for load in loads:
        load.wait()

    @pl.when(in_first)
    def _():
        token_load.wait()
        pl.when(on_left)(tokens_right.wait_recv)
        pl.when(on_right)(tokens_left.wait_recv)
        near_fields.start()

    gain_one, gain_two = gains[0:1, :], gains[1:2, :]
    shift_conv, shift_one = shifts[0:1, :], shifts[1:2, :]
    shift_ffn, shift_two = shifts[2:3, :], shifts[3:4, :]

    def forward(m, carry):
        here = span(m)

        @pl.when(in_second)
        def _():
            whole, low, high = pass_copies(m)
            whole.wait_recv()
            pl.when(on_left)(low.wait_recv)
            pl.when(on_right)(high.wait_recv)
            field_copy(m).start()
            pl.when(m == rows - 1)(weight_copy.start)

        for flag, dilation in ((in_first, TIGHT), (in_second, WIDE)):

            @pl.when(flag)
            def _(dilation=dilation):
                for k in range(TAPS):
                    taps[:, k * width : (k + 1) * width] = one_tap(fields, columns, m, k, dilation)

        value, slope = gelu_pair(dot(taps[...], conv_w[...]) + shift_conv)
        unit, scale = normalise(value)
        unit_one[here, :] = unit.astype(BF16)
        slope_one[here, :] = (slope * scale).astype(BF16)
        mixed = fields[m, own, :].astype(F32) + unit * gain_one + shift_one
        mixed_low = mixed.astype(BF16)
        slabs[2 * chunks, here, :] = mixed_low
        mixed_copy(m).start()
        ffn = None
        for c in range(chunks):
            part = slice(c * width, (c + 1) * width)
            value, slope = gelu_pair(dot(mixed_low, up_w[:, part]) + bias[:, part])
            low = value.astype(BF16)
            slabs[c, here, :] = low
            slabs[chunks + c, here, :] = slope.astype(BF16)
            term = dot(low, down_w[part, :])
            ffn = term if ffn is None else ffn + term
        unit, scale = normalise(ffn + shift_ffn)
        unit_two[here, :] = unit.astype(BF16)
        scale_two[here, :] = jnp.broadcast_to(scale, (length, 128))
        results[m] = (mixed + unit * gain_two + shift_two).astype(BF16)
        act_copy(m).start()

        @pl.when(in_first)
        def _():
            whole, low, high = pass_copies(m)
            pl.when(on_right)(low.start)
            pl.when(on_left)(high.start)
            whole.start()

        return carry

    lax.fori_loop(0, rows, forward, 0)

    masks_across.wait_recv()
    to_columns(masks_other, columns, tokens)

    @pl.when(in_first)
    def _():
        masks_back.wait_recv()
        to_columns(masks_second, columns_second)

    def conv_back(m, mask_columns, dilation):
        grad = mixed_grads[m]
        for k in range(TAPS):
            at = (TAPS - 1 - k) * width
            grad = grad + dot_nt(one_tap(conv_grads, mask_columns, m, k, dilation), conv_w[at : at + width, :])
        return grad

    def chunk_of(i):
        return my_part * part_chunks + i

    def chunk_span(i):
        return pl.ds(pl.multiple_of(chunk_of(i) * width, width), width)

    def other_forward(m, carry):
        here = span(m)
        mixed_copy(m).wait_recv()
        for i in range(part_chunks):
            at = chunk_span(i)
            value, slope = gelu_pair(dot(mixed_other[here, :], up_w[:, at]) + bias[:, at])
            upper_other[i, here, :] = value.astype(BF16)
            hidden_other[i, here, :] = slope.astype(BF16)
        return carry

    def other_backward(m, carry):
        here = span(m)
        ffn_copy(m).wait_recv()
        for i in range(part_chunks):
            grad = dot_nt(ffn_grads_other[here, :], down_w[chunk_span(i), :])
            hidden_other[i, here, :] = (grad * hidden_other[i, here, :].astype(F32)).astype(BF16)
        return carry

    def second_input(m):
        whole, sides, low, high = back_copies(m)
        whole.wait_recv()
        sides.wait_recv()
        pl.when(on_left)(low.wait_recv)
        pl.when(on_right)(high.wait_recv)
        low = conv_back(m, columns_second, WIDE).astype(BF16)
        given[m] = low
        mixed_grads[m] = low.astype(F32)
        grads_across(m).start()

    @pl.when(in_first)
    def _():
        lax.fori_loop(0, rows, other_forward, 0)
        weight_copy.wait_recv()

    pl.when(in_second)(given_load.wait)

    def backward_ffn(m, carry):
        @pl.when(in_first)
        def _():
            second_input(m)
            pl.when(m == rows - 1)(loads[0].start)

        here = span(m)
        grad = given[m].astype(F32)
        unit = unit_two[here, :].astype(F32)
        grad_ffn = norm_backward(grad * gain_two, unit) * scale_two[here, 0:1]
        sums[1:2, :] += column_sum(grad * unit)
        sums[5:6, :] += column_sum(grad)
        sums[4:5, :] += column_sum(grad_ffn)
        grad_ffn_low = grad_ffn.astype(BF16)
        ffn_grads[here, :] = grad_ffn_low
        ffn_copy(m).start()
        mixed = grad
        for c in range(chunks):
            part = slice(c * width, (c + 1) * width)
            grad_hidden = dot_nt(grad_ffn_low, down_w[part, :]) * slabs[chunks + c, here, :].astype(F32)
            sums[8 + c : 9 + c, :] += column_sum(grad_hidden)
            low = grad_hidden.astype(BF16)
            slabs[chunks + c, here, :] = low
            mixed = mixed + dot_nt(low, up_w[:, part])
        pl.when(in_first)(grads_across(m).wait_send)
        mixed_grads[m] = mixed
        unit = unit_one[here, :].astype(F32)
        grad_conv = norm_backward(mixed * gain_one, unit) * slope_one[here, :].astype(F32)
        sums[0:1, :] += column_sum(mixed * unit)
        sums[3:4, :] += column_sum(mixed)
        sums[2:3, :] += column_sum(grad_conv)
        conv_grads[m, own, :] = grad_conv.astype(BF16)

        @pl.when(in_second)
        def _():
            whole, sides, low, high = back_copies(m)
            pl.when(on_right)(low.start)
            pl.when(on_left)(high.start)
            whole.start()
            sides.start()

        @pl.when(in_first)
        def _():
            low, high = near_copies(m)
            pl.when(on_right)(low.start)
            pl.when(on_left)(high.start)

        half_copy(m).start()
        halves[here, :] = conv_grads[m, own, mine_at]
        return carry

    lax.fori_loop(0, rows, backward_ffn, 0)

    @pl.when(in_second)
    def _():
        lax.fori_loop(0, rows, other_forward, 0)

    def sums_copy(i):
        return remote(
            sums_sent.at[i], sums_arrived.at[i], sums_send.at[i], sums_recv.at[i], partner(geo.all_bits[i])
        )

    def sums_begin(i):
        sums_sent[i] = sums[...]
        sums_copy(i).start()

    def sums_end(i):
        sums_copy(i).wait_recv()
        sums[...] += sums_arrived[i]

    owners, share = geo.owners, geo.share
    my_bits = {bit: bit_of(bit) for bit in geo.bits}
    partners = {bit: partner(bit) for bit in geo.bits}
    per_dp = geo.seq // geo.low
    first_down, first_conv = part_chunks, 2 * part_chunks

    def columns_of(j):
        single = j == geo.slices - 1 and TAPS % 2 == 1
        return slice(0, half_width) if single else slice(0, width)

    def place(j, owner_dp, owner_seq):
        where = 0
        weight = owners
        for axis, size in geo.orders[j]:
            weight //= 2
            index = owner_dp if axis == "dp" else owner_seq * geo.low
            where = where + ((index // size) % 2 + my_bits[axis, size]) % 2 * weight
        return where

    def part_copy(j, i):
        half, at = owners >> (i + 1), columns_of(j)
        return remote(
            partial.at[j, half : 2 * half, :, at],
            arrived.at[j, half : 2 * half, :, at],
            part_send.at[j, i],
            part_recv.at[j, i],
            partners[geo.orders[j][i]],
        )

    def total_of(j, i):
        half, at = owners >> (i + 1), columns_of(j)
        return partial[j, 0:half, :, at].astype(F32) + arrived[j, half : 2 * half, :, at].astype(F32)

    def advance(j, i):
        part_copy(j, i - 1).wait_recv()
        partial[j, 0 : owners >> i, :, columns_of(j)] = total_of(j, i - 1).astype(BF16)
        part_copy(j, i).start()

    def finish(j):
        last = len(geo.orders[j]) - 1
        part_copy(j, last).wait_recv()
        if j < first_down:
            for part, total in ((my_part, partial[j, 0]), (1 - my_part, arrived[j, 1])):
                at = (part * part_chunks + j) * width
                up_out[:, pl.ds(pl.multiple_of(at, width), width)] = total.astype(F32)
        elif j < first_conv:
            total = total_of(j, last)
            for r in range(2):
                at = (2 * (j - first_down) + r) * share
                down_out[at : at + share, :] = total[r]
        else:
            for q in range(2):
                k = 2 * (j - first_conv) + q
                if k < TAPS:
                    at = slice(q * half_width, (q + 1) * half_width)
                    conv_out[k, :, mine_at] = partial[j, 0, :, at].astype(F32)
                    conv_out[k, :, other_at] = arrived[j, 1, :, at].astype(F32)

    def up_slice(j):
        places = [place(j, owner // per_dp, owner % per_dp) for owner in range(owners)]

        def half(n, carry):
            at = pl.ds(pl.multiple_of(n * half_width, half_width), half_width)
            grad = dot_tn(slabs[2 * chunks], slabs[chunks + chunk_of(j), :, at])
            grad = grad + dot_tn(mixed_other[...], hidden_other[j, :, at])
            for owner in range(owners):
                partial[j, places[owner], :, at] = grad[owner * share : (owner + 1) * share].astype(BF16)
            return carry

        lax.fori_loop(0, 2, half, 0)
        part_copy(j, 0).start()

    def down_slab(i):
        each = owners // chunks
        places = {
            (w, s): place(first_down + s, (chunk_of(i) * each + w) // per_dp, (chunk_of(i) * each + w) % per_dp)
            for w in range(each)
            for s in range(part_chunks)
        }

        def half(n, carry):
            at = pl.ds(pl.multiple_of(n * half_width, half_width), half_width)
            grad = dot_tn(slabs[chunk_of(i)], ffn_grads[:, at])
            grad = grad + dot_tn(upper_other[i], ffn_grads_other[:, at])
            for (w, s), where in places.items():
                for r in range(2):
                    low = ((w * part_chunks + s) * 2 + r) * share
                    partial[first_down + s, where + r, :, at] = grad[low : low + share].astype(BF16)
            return carry

        lax.fori_loop(0, 2, half, 0)
        if i == part_chunks - 1:
            for s in range(part_chunks):
                part_copy(first_down + s, 0).start()

    conv_begun = []

    def conv_slice(p):
        j = first_conv + p
        if not conv_begun:
            conv_begun.append(p)
            for m in range(rows):
                half_copy(m).wait_recv()
            pl.when(in_first)(near_fields.wait_recv)

            @pl.when(in_second)
            def _():
                for m in range(rows):
                    field_copy(m).wait_recv()

        for q in range(2):
            k = 2 * p + q
            if k >= TAPS:
                continue
            at = slice(q * half_width, (q + 1) * half_width)
            places = [place(j, owner // per_dp, owner % per_dp) for owner in range(owners)]
            for flag, dilation in ((in_first, TIGHT), (in_second, WIDE)):

                @pl.when(flag)
                def _(dilation=dilation):
                    def side(chip, carry):
                        grad = None
                        for r in range(rows):
                            m = chip * rows + r
                            term = dot_tn(one_tap(fields, columns, m, k, dilation), halves[span(m), :])
                            grad = term if grad is None else grad + term
                        conv_total[...] = jnp.where(chip == 0, grad, conv_total[...] + grad)
                        return carry

                    lax.fori_loop(0, 2, side, 0)

            for owner in range(owners):
                partial[j, places[owner], :, at] = conv_total[owner * share : (owner + 1) * share].astype(BF16)
        part_copy(j, 0).start()

    input_begun = []

    def first_input(m, carry):
        low, high = near_copies(m)

        @pl.when(on_left)
        def _():
            low.wait_recv()
            conv_grads[m, HALO - EDGE : HALO, :] = near_edges[m, 0]

        @pl.when(on_right)
        def _():
            high.wait_recv()
            conv_grads[m, HALO + length : HALO + length + EDGE, :] = near_edges[m, 1]

        mixed_grads[m] = conv_back(m, columns, TIGHT)
        grads_copy(m).start()
        return carry

    def first_inputs(group):
        if not input_begun:
            input_begun.append(group)
            loads[0].wait()
        each = rows // FIRST_GROUPS
        lax.fori_loop(group * each, (group + 1) * each, first_input, 0)

    def share_sums():
        index = dp * geo.seq + seq
        lane = lax.broadcasted_iota(jnp.int32, (128, width), 1)
        line = lax.broadcasted_iota(jnp.int32, (128, width), 0)
        exact = functools.partial(
            lax.dot_general,
            dimension_numbers=(((1,), (1,)), ((), ())),
            precision=lax.Precision.HIGHEST,
            preferred_element_type=F32,
        )
        picked = exact(sums[...], (lane == line + index * geo.final_share).astype(F32))
        gain_out[...] = picked[0:2, : geo.final_share]
        shift_out[...] = picked[2:6, : geo.final_share]
        start = index * geo.bias_share
        picked = exact(sums[...], (lane == line + start % width).astype(F32))
        wanted = lax.broadcasted_iota(jnp.int32, picked.shape, 0) == 8 + start // width
        bias_out[...] = column_sum(jnp.where(wanted, picked, 0.0))[:, : geo.bias_share]

    def gradients_back():
        lax.fori_loop(0, rows, other_backward, 0)

    def work_of(kind, at):
        if kind == "first":
            return lambda: pl.when(in_first)(lambda: first_inputs(at))
        if kind == "other":
            return gradients_back
        return functools.partial({"up": up_slice, "down": down_slab, "conv": conv_slice}[kind], at)

    sums_begin(0)
    stride = 6
    sums_done = 0
    for at, (what, which) in enumerate(geo.plan):
        if isinstance(what, str):
            work_of(what, which)()
        elif which + 1 < len(geo.orders[what]):
            advance(what, which + 1)
        else:
            finish(what)
        if (at + 1) % stride == 0 and sums_done < len(geo.all_bits):
            sums_end(sums_done)
            sums_done += 1
            if sums_done < len(geo.all_bits):
                sums_begin(sums_done)
            else:
                share_sums()

    for j in range(geo.slices):
        for i in range(len(geo.orders[j])):
            part_copy(j, i).wait_send()
    for i in range(len(geo.all_bits)):
        sums_copy(i).wait_send()
    masks_across.wait_send()

    def settle_row(m, carry):
        act_copy(m).wait()
        half_copy(m).wait_send()
        mixed_copy(m).wait_send()
        ffn_copy(m).wait_send()

        @pl.when(in_first)
        def _():
            grads_copy(m).wait()
            whole, low, high = pass_copies(m)
            pl.when(on_right)(low.wait_send)
            pl.when(on_left)(high.wait_send)
            whole.wait_send()
            low, high = near_copies(m)
            pl.when(on_right)(low.wait_send)
            pl.when(on_left)(high.wait_send)

        @pl.when(in_second)
        def _():
            field_copy(m).wait_send()
            whole, sides, low, high = back_copies(m)
            pl.when(on_right)(low.wait_send)
            pl.when(on_left)(high.wait_send)
            whole.wait_send()
            sides.wait_send()
            grads_across(m).wait_recv()

        return carry

    lax.fori_loop(0, rows, settle_row, 0)

    @pl.when(in_first)
    def _():
        pl.when(on_right)(tokens_right.wait_send)
        pl.when(on_left)(tokens_left.wait_send)
        near_fields.wait_send()

    @pl.when(in_second)
    def _():
        masks_back.wait_send()
        weight_copy.wait_send()


def hand_over(*refs):
    sems_in, sems_out = refs[-2:]
    count = len(refs) // 3
    sources, targets, held = refs[:count], refs[count : 2 * count], refs[2 * count : 3 * count]
    copies_in = [pltpu.make_async_copy(sources[i], held[i], sems_in.at[i]) for i in range(count)]
    copies_out = [pltpu.make_async_copy(held[i], targets[i], sems_out.at[i]) for i in range(count)]
    for copy in copies_in:
        copy.start()
    for i in range(count):
        copies_in[i].wait()
        copies_out[i].start()
    for copy in copies_out:
        copy.wait()


def per_device(
    dp,
    seq,
    tokens,
    cotangent,
    tap_masks,
    conv_weight,
    up_weight,
    up_bias,
    down_weight,
    norm_gains,
    shift_terms,
):
    rows, length, width = tokens.shape
    hidden = up_weight.shape[2]
    geo = Geometry(dp, seq, rows, length, width, hidden)
    reach = length + 2 * HALO
    vmem = pl.BlockSpec(memory_space=pltpu.VMEM)
    hbm = pl.BlockSpec(memory_space=pl.ANY)
    dma = pltpu.SemaphoreType.DMA
    stages = len(geo.all_bits)
    slices = (geo.slices, geo.owners, geo.share, width)
    made = pl.pallas_call(
        functools.partial(body, geo),
        out_shape=[
            jax.ShapeDtypeStruct((rows, length, width), BF16),
            jax.ShapeDtypeStruct((rows, length, width), F32),
            jax.ShapeDtypeStruct((TAPS, geo.share, width), F32),
            jax.ShapeDtypeStruct((geo.share, hidden), F32),
            jax.ShapeDtypeStruct((geo.chunks * geo.share, width), F32),
            jax.ShapeDtypeStruct((1, geo.bias_share), F32),
            jax.ShapeDtypeStruct((2, geo.final_share), F32),
            jax.ShapeDtypeStruct((4, geo.final_share), F32),
        ],
        in_specs=[hbm] * 5 + [vmem] * 4,
        out_specs=[hbm] * 2 + [vmem] * 6,
        scratch_shapes=[
            pltpu.VMEM((2 * rows, reach, width), BF16),
            pltpu.VMEM((rows, reach, width), BF16),
            pltpu.VMEM((rows, 2, EDGE, width), BF16),
            pltpu.VMEM((TAPS * width, width), BF16),
            pltpu.VMEM((width, hidden), BF16),
            pltpu.VMEM((hidden, width), BF16),
            pltpu.VMEM((2 * geo.chunks + 1, geo.tokens, width), BF16),
            pltpu.VMEM((length, TAPS * width), BF16),
            pltpu.VMEM((2 * geo.tokens, width // 2), BF16),
            pltpu.VMEM((geo.tokens, width), BF16),
            pltpu.VMEM((geo.tokens, width), BF16),
            pltpu.VMEM((geo.tokens, width), BF16),
            pltpu.VMEM((geo.tokens, 128), F32),
            pltpu.VMEM((rows, length, width), F32),
            pltpu.VMEM((rows, length, width), BF16),
            pltpu.VMEM((geo.tokens, width), BF16),
            pltpu.VMEM((geo.tokens, width), BF16),
            pltpu.VMEM((geo.tokens, width), BF16),
            pltpu.VMEM((geo.part_chunks, geo.tokens, width), BF16),
            pltpu.VMEM((geo.part_chunks, geo.tokens, width), BF16),
            pltpu.VMEM((rows, length, width), BF16),
            pltpu.VMEM((TAPS, rows, length), jnp.int32),
            pltpu.VMEM((TAPS, rows, length), jnp.int32),
            pltpu.VMEM((2 * geo.tokens, 128), F32),
            pltpu.VMEM((geo.tokens, 128), F32),
            pltpu.VMEM((width, width // 2), F32),
            pltpu.VMEM(slices, BF16),
            pltpu.VMEM(slices, BF16),
            pltpu.VMEM((16, width), F32),
            pltpu.VMEM((stages, 16, width), F32),
            pltpu.VMEM((stages, 16, width), F32),
            dma((3,)),
            dma((2,)),
            dma((2,)),
            dma((2,)),
            dma((2,)),
            dma((2,)),
            dma((rows, 3)),
            dma((rows, 3)),
            dma((rows,)),
            dma((rows,)),
            dma,
            dma,
            dma((rows, 4)),
            dma((rows, 4)),
            dma((rows,)),
            dma((rows,)),
            dma((rows,)),
            dma((rows,)),
            dma((rows,)),
            dma((rows,)),
            dma((rows, 2)),
            dma((rows, 2)),
            dma((rows,)),
            dma((rows,)),
            dma((rows,)),
            dma((rows,)),
            dma((geo.slices, len(geo.bits))),
            dma((geo.slices, len(geo.bits))),
            dma((stages,)),
            dma((stages,)),
        ],
        compiler_params=pltpu.CompilerParams(
            collective_id=0, has_side_effects=True, vmem_limit_bytes=63 * 2**20
        ),
    )(
        tokens,
        cotangent,
        jnp.transpose(conv_weight[0], (1, 0, 2)).reshape(TAPS * width, width),
        up_weight[0],
        down_weight[0],
        tap_masks[0],
        up_bias,
        jnp.transpose(norm_gains[0]),
        jnp.transpose(shift_terms[0]),
    )
    made = pl.pallas_call(
        hand_over,
        out_shape=[jax.ShapeDtypeStruct(array.shape, array.dtype) for array in made],
        in_specs=[hbm] * len(made),
        out_specs=[hbm] * len(made),
        scratch_shapes=[pltpu.VMEM(array.shape, array.dtype) for array in made] + [dma((len(made),))] * 2,
    )(*made)
    act, grads, conv_grad, up_grad, down_grad, bias_grad, gain_grad, shift_grad = made
    conv_grad = jnp.transpose(conv_grad, (1, 0, 2))
    if geo.low > 1:
        groups = [list(range(at, at + geo.low)) for at in range(0, seq, geo.low)]
        conv_grad, up_grad, down_grad = (
            lax.psum_scatter(
                grad, "seq", scatter_dimension=0, axis_index_groups=groups, tiled=True
            )
            for grad in (conv_grad, up_grad, down_grad)
        )
    return (
        act[None],
        grads[None],
        conv_grad[None],
        up_grad[None],
        bias_grad,
        down_grad[None],
        jnp.transpose(gain_grad)[None],
        jnp.transpose(shift_grad)[None],
    )


def solution(mesh):
    placed = (
        P("dp", "seq", None),
        P("dp", "seq", None),
        P("section", None, "dp", "seq"),
        P("section", None, None, None),
        P("section", None, None),
        P("section", None),
        P("section", None, None),
        P("section", None, None),
        P("section", None, None),
    )
    return jax.shard_map(
        functools.partial(per_device, mesh.shape["dp"], mesh.shape["seq"]),
        mesh=mesh,
        in_specs=placed,
        out_specs=(
            P("section", "dp", "seq", None),
            P("section", "dp", "seq", None),
            P("section", ("dp", "seq"), None, None),
            P("section", ("dp", "seq"), None),
            P("section", ("dp", "seq")),
            P("section", ("dp", "seq"), None),
            P("section", ("dp", "seq"), None),
            P("section", ("dp", "seq"), None),
        ),
        check_vma=False,
    )
```

```python
import functools

import jax
import jax.numpy as jnp
from jax import lax
from jax.experimental import pallas as pl
from jax.experimental.pallas import tpu as pltpu
from jax.sharding import PartitionSpec as P

TAPS = 9
CENTRE = TAPS // 2
TIGHT = 2
WIDE = 32
HALO = CENTRE * WIDE
EDGE = 16
EPS = 1e-05
MESH = pl.DeviceIdType.MESH
BF16 = jnp.bfloat16
F32 = jnp.float32
LAG = 3
FIRST_GROUPS = 2
PLAN = (
    ("first", 0), ("conv", 4), ("conv", 0), ("other", 0), (8, 0), ("up", 1), ("up", 0), (8, 1), ("first", 1),
    ("conv", 2), (4, 0), ("conv", 3), (0, 0), ("conv", 1), (6, 0), (0, 1), ("down", 0), (1, 0), (4, 1), (8, 2),
    (7, 0), (6, 1), ("down", 1), (1, 1), (7, 1), (5, 0), (2, 0), (6, 2), (6, 3), (3, 0), (1, 2), (0, 2), (5, 1),
    (4, 2), (7, 2), (0, 3), (2, 1), (3, 1), (4, 3), (8, 3), (5, 2), (7, 3), (2, 2), (1, 3), (5, 3), (3, 2),
)
ALONG = (1, 4, 8)
TANH_SCALE = 0.7978845608028654
TANH_CUBE = TANH_SCALE * 0.044715


def gelu_pair(z):
    square = z * z
    half = 0.5 + 0.5 * jnp.tanh(z * (TANH_SCALE + TANH_CUBE * square))
    value = z * half
    return value, half + value * (1.0 - half) * (2.0 * TANH_SCALE + 6.0 * TANH_CUBE * square)


def normalise(values):
    centred = values - jnp.mean(values, axis=-1, keepdims=True)
    scale = lax.rsqrt(jnp.mean(centred * centred, axis=-1, keepdims=True) + EPS)
    return centred * scale, scale


def norm_backward(weighted, unit):
    return (
        weighted
        - jnp.mean(weighted, axis=-1, keepdims=True)
        - unit * jnp.mean(weighted * unit, axis=-1, keepdims=True)
    )


def column_sum(values):
    return jnp.sum(values, axis=0, keepdims=True)


def dot(a, b):
    return jnp.dot(a, b, preferred_element_type=F32)


def dot_nt(a, b):
    return lax.dot_general(a, b, (((1,), (1,)), ((), ())), preferred_element_type=F32)


def dot_tn(a, b):
    return lax.dot_general(a, b, (((0,), (0,)), ((), ())), preferred_element_type=F32)


class Geometry:
    def __init__(self, dp, seq, rows, length, width, hidden):
        self.dp, self.seq = dp, seq
        self.rows, self.length, self.width = rows, length, width
        self.tokens = rows * length
        self.chunks = hidden // width
        self.low = max(1, 16 * dp * seq // width)
        self.owners = dp * seq // self.low
        self.share = width // self.owners
        self.final_share = width // (dp * seq)
        self.bias_share = hidden // (dp * seq)
        dp_bits = [("dp", 1 << i) for i in range(dp.bit_length() - 1)]
        seq_all = [("seq", 1 << i) for i in range(seq.bit_length() - 1)]
        seq_bits = [bit for bit in seq_all if bit[1] >= self.low]
        self.bits = dp_bits + seq_bits
        self.all_bits = dp_bits + seq_all
        self.dp_bits = dp_bits
        self.pairs = (TAPS + 1) // 2
        self.part_chunks = self.chunks // 2
        self.slices = 2 * self.part_chunks + self.pairs
        low_bit, high_bit, lines = dp_bits[:1], dp_bits[-1:], seq_bits
        self.orders = [low_bit + lines + high_bit] * self.part_chunks + [low_bit + lines] * self.part_chunks
        self.orders += [high_bit + lines + low_bit] * self.pairs
        for j in range(self.slices):
            if j in ALONG:
                self.orders[j] = lines[:1] + self.orders[j][:1] + self.orders[j][2:]
        planned = len(self.bits) == 4 and rows == 4 and self.chunks == 4
        self.plan = PLAN if planned else self.plain_plan()

    def plain_plan(self):
        first_down, first_conv = self.part_chunks, 2 * self.part_chunks
        work = [("other", 0)]
        work += [("down", i) for i in range(self.part_chunks)]
        work += [("up", i) for i in range(self.part_chunks)]
        work += [("conv", p) for p in range(self.pairs)]
        work += [("first", group) for group in range(FIRST_GROUPS)]
        due = {}
        for turn, (kind, at) in enumerate(work):
            begun = {"up": [at], "conv": [first_conv + at]}.get(kind, [])
            if kind == "down" and at == self.part_chunks - 1:
                begun = range(first_down, first_conv)
            for j in begun:
                for i in range(len(self.orders[j])):
                    due.setdefault(turn + LAG * (i + 1), []).append((j, i))
        plan = []
        for turn in range(max(max(due) + 1, len(work))):
            plan += work[turn : turn + 1] + due.get(turn, [])
        return plan


def body(
    geo,
    tokens_hbm,
    cotangent_hbm,
    conv_hbm,
    up_hbm,
    down_hbm,
    masks,
    bias,
    gains,
    shifts,
    act_hbm,
    grads_hbm,
    conv_out,
    up_out,
    down_out,
    bias_out,
    gain_out,
    shift_out,
    fields,
    conv_grads,
    near_edges,
    conv_w,
    up_w,
    down_w,
    slabs,
    taps,
    halves,
    unit_one,
    slope_one,
    unit_two,
    scale_two,
    mixed_grads,
    given,
    ffn_grads,
    mixed_other,
    ffn_grads_other,
    upper_other,
    hidden_other,
    results,
    masks_other,
    masks_second,
    columns,
    columns_second,
    conv_total,
    partial,
    arrived,
    sums,
    sums_sent,
    sums_arrived,
    load_sem,
    row_load_sem,
    token_edge_send,
    token_edge_recv,
    masks_send,
    masks_recv,
    pass_send,
    pass_recv,
    field_send,
    field_recv,
    weight_send,
    weight_recv,
    back_send,
    back_recv,
    half_send,
    half_recv,
    mixed_send,
    mixed_recv,
    ffn_send,
    ffn_recv,
    near_send,
    near_recv,
    act_sem,
    grads_sem,
    grads_send,
    grads_recv,
    part_send,
    part_recv,
    sums_send,
    sums_recv,
):
    rows, length, width, chunks = geo.rows, geo.length, geo.width, geo.chunks
    tokens, half_width = geo.tokens, geo.width // 2
    section = lax.axis_index("section")
    dp = lax.axis_index("dp")
    seq = lax.axis_index("seq")
    mine = {"dp": dp, "seq": seq}
    in_first = section == 0
    in_second = section == 1
    has_left = (seq + geo.seq - 1) // geo.seq
    has_right = 1 - (seq + 1) // geo.seq
    on_left, on_right = has_left == 1, has_right == 1
    own = slice(HALO, HALO + length)
    near = slice(HALO - EDGE, HALO + length + EDGE)

    def bit_of(bit):
        axis, size = bit
        return (mine[axis] // size) % 2

    def partner(bit):
        axis, size = bit
        other = mine[axis] + (1 - 2 * bit_of(bit)) * size
        return (section, other, seq) if axis == "dp" else (section, dp, other)

    def remote(source, target, sends, receives, device):
        return pltpu.make_async_remote_copy(
            src_ref=source,
            dst_ref=target,
            send_sem=sends,
            recv_sem=receives,
            device_id=device,
            device_id_type=MESH,
        )

    core = (1 - section, dp, seq)
    left, right = (section, dp, seq - 1), (section, dp, seq + 1)
    first_core, second_core = (0, dp, seq), (1, dp, seq)
    conv_bit, ffn_bit = geo.dp_bits[0], geo.dp_bits[-1]
    pair, ffn_pair = partner(conv_bit), partner(ffn_bit)
    my_half, my_part = bit_of(conv_bit), bit_of(ffn_bit)
    part_chunks = geo.part_chunks
    mine_at = pl.ds(pl.multiple_of(my_half * half_width, half_width), half_width)
    other_at = pl.ds(pl.multiple_of((1 - my_half) * half_width, half_width), half_width)

    loads = [
        pltpu.make_async_copy(conv_hbm, conv_w, load_sem.at[0]),
        pltpu.make_async_copy(up_hbm, up_w, load_sem.at[1]),
        pltpu.make_async_copy(down_hbm, down_w, load_sem.at[2]),
    ]
    token_load = pltpu.make_async_copy(tokens_hbm, fields.at[0:rows, own], row_load_sem.at[0])
    given_load = pltpu.make_async_copy(cotangent_hbm, given, row_load_sem.at[1])
    pl.when(in_first)(token_load.start)
    for load in loads:
        load.start()
    pl.when(in_second)(given_load.start)

    barrier = pltpu.get_barrier_semaphore()

    def greet(device):
        pl.semaphore_signal(barrier, inc=1, device_id=device, device_id_type=MESH)

    for bit in geo.all_bits:
        greet(partner(bit))
    greet(core)
    for flag, at in ((on_left, seq - 1), (on_right, seq + 1)):

        @pl.when(flag)
        def _(at=at):
            greet((section, dp, at))
            greet((1 - section, dp, at))

    @pl.when(has_left == 0)
    def _():
        fields[0:rows, :HALO] = jnp.zeros((rows, HALO, width), BF16)
        conv_grads[:, :HALO] = jnp.zeros((rows, HALO, width), BF16)

    @pl.when(has_right == 0)
    def _():
        fields[0:rows, HALO + length :] = jnp.zeros((rows, HALO, width), BF16)
        conv_grads[:, HALO + length :] = jnp.zeros((rows, HALO, width), BF16)

    sums[...] = jnp.zeros(sums.shape, F32)
    pl.semaphore_wait(barrier, len(geo.all_bits) + 1 + 2 * has_left + 2 * has_right)

    tokens_right = remote(
        tokens_hbm.at[:, length - EDGE : length],
        fields.at[0:rows, HALO - EDGE : HALO],
        token_edge_send.at[0],
        token_edge_recv.at[0],
        right,
    )
    tokens_left = remote(
        tokens_hbm.at[:, 0:EDGE],
        fields.at[0:rows, HALO + length : HALO + length + EDGE],
        token_edge_send.at[1],
        token_edge_recv.at[1],
        left,
    )

    @pl.when(in_first)
    def _():
        pl.when(on_right)(tokens_right.start)
        pl.when(on_left)(tokens_left.start)

    masks_across = remote(masks, masks_other, masks_send.at[0], masks_recv.at[0], pair)
    masks_back = remote(masks, masks_second, masks_send.at[1], masks_recv.at[1], first_core)
    masks_across.start()
    pl.when(in_second)(masks_back.start)

    def to_columns(source, target, base=0):
        for r in range(rows):
            plane = source[:, r, :].astype(F32)
            padded = jnp.concatenate([plane, jnp.zeros((128 - TAPS, length), F32)], axis=0)
            target[base + r * length : base + (r + 1) * length, :] = jnp.transpose(padded)

    to_columns(masks, columns)

    def span(m):
        return pl.ds(pl.multiple_of(m * length, length), length)

    def one_tap(source, mask_columns, m, k, dilation):
        values = source[m, pl.ds(HALO + (k - CENTRE) * dilation, length), :]
        if k == CENTRE:
            return values
        lane = jnp.broadcast_to(mask_columns[span(m), k : k + 1], (length, 128)).astype(BF16)
        return values * jnp.concatenate([lane] * (width // 128), axis=1)

    def pass_copies(m):
        return (
            remote(results.at[m], fields.at[m, own], pass_send.at[m, 0], pass_recv.at[m, 0], second_core),
            remote(
                results.at[m, length - HALO : length],
                fields.at[m, 0:HALO],
                pass_send.at[m, 1],
                pass_recv.at[m, 1],
                (1, dp, seq + 1),
            ),
            remote(
                results.at[m, 0:HALO],
                fields.at[m, HALO + length : HALO + length + HALO],
                pass_send.at[m, 2],
                pass_recv.at[m, 2],
                (1, dp, seq - 1),
            ),
        )

    def back_copies(m):
        return (
            remote(conv_grads.at[m, own], conv_grads.at[m, own], back_send.at[m, 0], back_recv.at[m, 0], first_core),
            remote(mixed_grads.at[m], mixed_grads.at[m], back_send.at[m, 1], back_recv.at[m, 1], first_core),
            remote(
                conv_grads.at[m, HALO + length - HALO : HALO + length],
                conv_grads.at[m, 0:HALO],
                back_send.at[m, 2],
                back_recv.at[m, 2],
                (0, dp, seq + 1),
            ),
            remote(
                conv_grads.at[m, HALO : HALO + HALO],
                conv_grads.at[m, HALO + length : HALO + length + HALO],
                back_send.at[m, 3],
                back_recv.at[m, 3],
                (0, dp, seq - 1),
            ),
        )

    def near_copies(m):
        return (
            remote(
                conv_grads.at[m, HALO + length - EDGE : HALO + length],
                near_edges.at[m, 0],
                near_send.at[m, 0],
                near_recv.at[m, 0],
                right,
            ),
            remote(
                conv_grads.at[m, HALO : HALO + EDGE],
                near_edges.at[m, 1],
                near_send.at[m, 1],
                near_recv.at[m, 1],
                left,
            ),
        )

    def field_copy(m):
        return remote(fields.at[m], fields.at[rows + m], field_send.at[m], field_recv.at[m], pair)

    near_fields = remote(
        fields.at[0:rows, near], fields.at[rows : 2 * rows, near], field_send.at[0], field_recv.at[0], pair
    )

    def half_copy(m):
        return remote(
            conv_grads.at[m, own, other_at],
            halves.at[pl.ds(pl.multiple_of(tokens + m * length, length), length)],
            half_send.at[m],
            half_recv.at[m],
            pair,
        )

    def mixed_copy(m):
        here = span(m)
        return remote(
            slabs.at[2 * chunks, here], mixed_other.at[here], mixed_send.at[m], mixed_recv.at[m], ffn_pair
        )

    def ffn_copy(m):
        here = span(m)
        return remote(ffn_grads.at[here], ffn_grads_other.at[here], ffn_send.at[m], ffn_recv.at[m], ffn_pair)

    weight_copy = remote(conv_w, conv_w, weight_send, weight_recv, first_core)

    def act_copy(m):
        return pltpu.make_async_copy(results.at[m], act_hbm.at[m], act_sem.at[m])

    def grads_copy(m):
        return pltpu.make_async_copy(mixed_grads.at[m], grads_hbm.at[m], grads_sem.at[m])

    def grads_across(m):
        return remote(mixed_grads.at[m], grads_hbm.at[m], grads_send.at[m], grads_recv.at[m], second_core)

    for load in loads:
        load.wait()

    @pl.when(in_first)
    def _():
        token_load.wait()
        pl.when(on_left)(tokens_right.wait_recv)
        pl.when(on_right)(tokens_left.wait_recv)
        near_fields.start()

    gain_one, gain_two = gains[0:1, :], gains[1:2, :]
    shift_conv, shift_one = shifts[0:1, :], shifts[1:2, :]
    shift_ffn, shift_two = shifts[2:3, :], shifts[3:4, :]

    def forward(m, carry):
        here = span(m)

        @pl.when(in_second)
        def _():
            whole, low, high = pass_copies(m)
            whole.wait_recv()
            pl.when(on_left)(low.wait_recv)
            pl.when(on_right)(high.wait_recv)
            field_copy(m).start()
            pl.when(m == rows - 1)(weight_copy.start)

        for flag, dilation in ((in_first, TIGHT), (in_second, WIDE)):

            @pl.when(flag)
            def _(dilation=dilation):
                for k in range(TAPS):
                    taps[:, k * width : (k + 1) * width] = one_tap(fields, columns, m, k, dilation)

        value, slope = gelu_pair(dot(taps[...], conv_w[...]) + shift_conv)
        unit, scale = normalise(value)
        unit_one[here, :] = unit.astype(BF16)
        slope_one[here, :] = (slope * scale).astype(BF16)
        mixed = fields[m, own, :].astype(F32) + unit * gain_one + shift_one
        mixed_low = mixed.astype(BF16)
        slabs[2 * chunks, here, :] = mixed_low
        mixed_copy(m).start()
        ffn = None
        for c in range(chunks):
            part = slice(c * width, (c + 1) * width)
            value, slope = gelu_pair(dot(mixed_low, up_w[:, part]) + bias[:, part])
            low = value.astype(BF16)
            slabs[c, here, :] = low
            slabs[chunks + c, here, :] = slope.astype(BF16)
            term = dot(low, down_w[part, :])
            ffn = term if ffn is None else ffn + term
        unit, scale = normalise(ffn + shift_ffn)
        unit_two[here, :] = unit.astype(BF16)
        scale_two[here, :] = jnp.broadcast_to(scale, (length, 128))
        results[m] = (mixed + unit * gain_two + shift_two).astype(BF16)
        act_copy(m).start()

        @pl.when(in_first)
        def _():
            whole, low, high = pass_copies(m)
            pl.when(on_right)(low.start)
            pl.when(on_left)(high.start)
            whole.start()

        return carry

    lax.fori_loop(0, rows, forward, 0)

    masks_across.wait_recv()
    to_columns(masks_other, columns, tokens)

    @pl.when(in_first)
    def _():
        masks_back.wait_recv()
        to_columns(masks_second, columns_second)

    def conv_back(m, mask_columns, dilation):
        grad = mixed_grads[m]
        for k in range(TAPS):
            at = (TAPS - 1 - k) * width
            grad = grad + dot_nt(one_tap(conv_grads, mask_columns, m, k, dilation), conv_w[at : at + width, :])
        return grad

    def chunk_of(i):
        return my_part * part_chunks + i

    def chunk_span(i):
        return pl.ds(pl.multiple_of(chunk_of(i) * width, width), width)

    def other_forward(m, carry):
        here = span(m)
        mixed_copy(m).wait_recv()
        for i in range(part_chunks):
            at = chunk_span(i)
            value, slope = gelu_pair(dot(mixed_other[here, :], up_w[:, at]) + bias[:, at])
            upper_other[i, here, :] = value.astype(BF16)
            hidden_other[i, here, :] = slope.astype(BF16)
        return carry

    def other_backward(m, carry):
        here = span(m)
        ffn_copy(m).wait_recv()
        for i in range(part_chunks):
            grad = dot_nt(ffn_grads_other[here, :], down_w[chunk_span(i), :])
            hidden_other[i, here, :] = (grad * hidden_other[i, here, :].astype(F32)).astype(BF16)
        return carry

    def second_input(m):
        whole, sides, low, high = back_copies(m)
        whole.wait_recv()
        sides.wait_recv()
        pl.when(on_left)(low.wait_recv)
        pl.when(on_right)(high.wait_recv)
        low = conv_back(m, columns_second, WIDE).astype(BF16)
        given[m] = low
        mixed_grads[m] = low.astype(F32)
        grads_across(m).start()

    @pl.when(in_first)
    def _():
        lax.fori_loop(0, rows, other_forward, 0)
        weight_copy.wait_recv()

    pl.when(in_second)(given_load.wait)

    def backward_ffn(m, carry):
        @pl.when(in_first)
        def _():
            second_input(m)
            pl.when(m == rows - 1)(loads[0].start)

        here = span(m)
        grad = given[m].astype(F32)
        unit = unit_two[here, :].astype(F32)
        grad_ffn = norm_backward(grad * gain_two, unit) * scale_two[here, 0:1]
        sums[1:2, :] += column_sum(grad * unit)
        sums[5:6, :] += column_sum(grad)
        sums[4:5, :] += column_sum(grad_ffn)
        grad_ffn_low = grad_ffn.astype(BF16)
        ffn_grads[here, :] = grad_ffn_low
        ffn_copy(m).start()
        mixed = grad
        for c in range(chunks):
            part = slice(c * width, (c + 1) * width)
            grad_hidden = dot_nt(grad_ffn_low, down_w[part, :]) * slabs[chunks + c, here, :].astype(F32)
            sums[8 + c : 9 + c, :] += column_sum(grad_hidden)
            low = grad_hidden.astype(BF16)
            slabs[chunks + c, here, :] = low
            mixed = mixed + dot_nt(low, up_w[:, part])
        pl.when(in_first)(grads_across(m).wait_send)
        mixed_grads[m] = mixed
        unit = unit_one[here, :].astype(F32)
        grad_conv = norm_backward(mixed * gain_one, unit) * slope_one[here, :].astype(F32)
        sums[0:1, :] += column_sum(mixed * unit)
        sums[3:4, :] += column_sum(mixed)
        sums[2:3, :] += column_sum(grad_conv)
        conv_grads[m, own, :] = grad_conv.astype(BF16)

        @pl.when(in_second)
        def _():
            whole, sides, low, high = back_copies(m)
            pl.when(on_right)(low.start)
            pl.when(on_left)(high.start)
            whole.start()
            sides.start()

        @pl.when(in_first)
        def _():
            low, high = near_copies(m)
            pl.when(on_right)(low.start)
            pl.when(on_left)(high.start)

        half_copy(m).start()
        halves[here, :] = conv_grads[m, own, mine_at]
        return carry

    lax.fori_loop(0, rows, backward_ffn, 0)

    @pl.when(in_second)
    def _():
        lax.fori_loop(0, rows, other_forward, 0)

    def sums_copy(i):
        return remote(
            sums_sent.at[i], sums_arrived.at[i], sums_send.at[i], sums_recv.at[i], partner(geo.all_bits[i])
        )

    def sums_begin(i):
        sums_sent[i] = sums[...]
        sums_copy(i).start()

    def sums_end(i):
        sums_copy(i).wait_recv()
        sums[...] += sums_arrived[i]

    owners, share = geo.owners, geo.share
    my_bits = {bit: bit_of(bit) for bit in geo.bits}
    partners = {bit: partner(bit) for bit in geo.bits}
    per_dp = geo.seq // geo.low
    first_down, first_conv = part_chunks, 2 * part_chunks

    def columns_of(j):
        single = j == geo.slices - 1 and TAPS % 2 == 1
        return slice(0, half_width) if single else slice(0, width)

    def place(j, owner_dp, owner_seq):
        where = 0
        weight = owners
        for axis, size in geo.orders[j]:
            weight //= 2
            index = owner_dp if axis == "dp" else owner_seq * geo.low
            where = where + ((index // size) % 2 + my_bits[axis, size]) % 2 * weight
        return where

    def part_copy(j, i):
        half, at = owners >> (i + 1), columns_of(j)
        return remote(
            partial.at[j, half : 2 * half, :, at],
            arrived.at[j, half : 2 * half, :, at],
            part_send.at[j, i],
            part_recv.at[j, i],
            partners[geo.orders[j][i]],
        )

    def total_of(j, i):
        half, at = owners >> (i + 1), columns_of(j)
        return partial[j, 0:half, :, at].astype(F32) + arrived[j, half : 2 * half, :, at].astype(F32)

    def advance(j, i):
        part_copy(j, i - 1).wait_recv()
        partial[j, 0 : owners >> i, :, columns_of(j)] = total_of(j, i - 1).astype(BF16)
        part_copy(j, i).start()

    def finish(j):
        last = len(geo.orders[j]) - 1
        part_copy(j, last).wait_recv()
        if j < first_down:
            for part, total in ((my_part, partial[j, 0]), (1 - my_part, arrived[j, 1])):
                at = (part * part_chunks + j) * width
                up_out[:, pl.ds(pl.multiple_of(at, width), width)] = total.astype(F32)
        elif j < first_conv:
            total = total_of(j, last)
            for r in range(2):
                at = (2 * (j - first_down) + r) * share
                down_out[at : at + share, :] = total[r]
        else:
            for q in range(2):
                k = 2 * (j - first_conv) + q
                if k < TAPS:
                    at = slice(q * half_width, (q + 1) * half_width)
                    conv_out[k, :, mine_at] = partial[j, 0, :, at].astype(F32)
                    conv_out[k, :, other_at] = arrived[j, 1, :, at].astype(F32)

    def up_slice(j):
        places = [place(j, owner // per_dp, owner % per_dp) for owner in range(owners)]

        def half(n, carry):
            at = pl.ds(pl.multiple_of(n * half_width, half_width), half_width)
            grad = dot_tn(slabs[2 * chunks], slabs[chunks + chunk_of(j), :, at])
            grad = grad + dot_tn(mixed_other[...], hidden_other[j, :, at])
            for owner in range(owners):
                partial[j, places[owner], :, at] = grad[owner * share : (owner + 1) * share].astype(BF16)
            return carry

        lax.fori_loop(0, 2, half, 0)
        part_copy(j, 0).start()

    def down_slab(i):
        each = owners // chunks
        places = {
            (w, s): place(first_down + s, (chunk_of(i) * each + w) // per_dp, (chunk_of(i) * each + w) % per_dp)
            for w in range(each)
            for s in range(part_chunks)
        }

        def half(n, carry):
            at = pl.ds(pl.multiple_of(n * half_width, half_width), half_width)
            grad = dot_tn(slabs[chunk_of(i)], ffn_grads[:, at])
            grad = grad + dot_tn(upper_other[i], ffn_grads_other[:, at])
            for (w, s), where in places.items():
                for r in range(2):
                    low = ((w * part_chunks + s) * 2 + r) * share
                    partial[first_down + s, where + r, :, at] = grad[low : low + share].astype(BF16)
            return carry

        lax.fori_loop(0, 2, half, 0)
        if i == part_chunks - 1:
            for s in range(part_chunks):
                part_copy(first_down + s, 0).start()

    conv_begun = []

    def conv_slice(p):
        j = first_conv + p
        if not conv_begun:
            conv_begun.append(p)
            for m in range(rows):
                half_copy(m).wait_recv()
            pl.when(in_first)(near_fields.wait_recv)

            @pl.when(in_second)
            def _():
                for m in range(rows):
                    field_copy(m).wait_recv()

        for q in range(2):
            k = 2 * p + q
            if k >= TAPS:
                continue
            at = slice(q * half_width, (q + 1) * half_width)
            places = [place(j, owner // per_dp, owner % per_dp) for owner in range(owners)]
            for flag, dilation in ((in_first, TIGHT), (in_second, WIDE)):

                @pl.when(flag)
                def _(dilation=dilation):
                    def side(chip, carry):
                        grad = None
                        for r in range(rows):
                            m = chip * rows + r
                            term = dot_tn(one_tap(fields, columns, m, k, dilation), halves[span(m), :])
                            grad = term if grad is None else grad + term
                        conv_total[...] = jnp.where(chip == 0, grad, conv_total[...] + grad)
                        return carry

                    lax.fori_loop(0, 2, side, 0)

            for owner in range(owners):
                partial[j, places[owner], :, at] = conv_total[owner * share : (owner + 1) * share].astype(BF16)
        part_copy(j, 0).start()

    input_begun = []

    def first_input(m, carry):
        low, high = near_copies(m)

        @pl.when(on_left)
        def _():
            low.wait_recv()
            conv_grads[m, HALO - EDGE : HALO, :] = near_edges[m, 0]

        @pl.when(on_right)
        def _():
            high.wait_recv()
            conv_grads[m, HALO + length : HALO + length + EDGE, :] = near_edges[m, 1]

        mixed_grads[m] = conv_back(m, columns, TIGHT)
        grads_copy(m).start()
        return carry

    def first_inputs(group):
        if not input_begun:
            input_begun.append(group)
            loads[0].wait()
        each = rows // FIRST_GROUPS
        lax.fori_loop(group * each, (group + 1) * each, first_input, 0)

    def share_sums():
        index = dp * geo.seq + seq
        lane = lax.broadcasted_iota(jnp.int32, (128, width), 1)
        line = lax.broadcasted_iota(jnp.int32, (128, width), 0)
        exact = functools.partial(
            lax.dot_general,
            dimension_numbers=(((1,), (1,)), ((), ())),
            precision=lax.Precision.HIGHEST,
            preferred_element_type=F32,
        )
        picked = exact(sums[...], (lane == line + index * geo.final_share).astype(F32))
        gain_out[...] = picked[0:2, : geo.final_share]
        shift_out[...] = picked[2:6, : geo.final_share]
        start = index * geo.bias_share
        picked = exact(sums[...], (lane == line + start % width).astype(F32))
        wanted = lax.broadcasted_iota(jnp.int32, picked.shape, 0) == 8 + start // width
        bias_out[...] = column_sum(jnp.where(wanted, picked, 0.0))[:, : geo.bias_share]

    def gradients_back():
        lax.fori_loop(0, rows, other_backward, 0)

    def work_of(kind, at):
        if kind == "first":
            return lambda: pl.when(in_first)(lambda: first_inputs(at))
        if kind == "other":
            return gradients_back
        return functools.partial({"up": up_slice, "down": down_slab, "conv": conv_slice}[kind], at)

    sums_begin(0)
    stride = 6
    sums_done = 0
    for at, (what, which) in enumerate(geo.plan):
        if isinstance(what, str):
            work_of(what, which)()
        elif which + 1 < len(geo.orders[what]):
            advance(what, which + 1)
        else:
            finish(what)
        if (at + 1) % stride == 0 and sums_done < len(geo.all_bits):
            sums_end(sums_done)
            sums_done += 1
            if sums_done < len(geo.all_bits):
                sums_begin(sums_done)
            else:
                share_sums()

    for j in range(geo.slices):
        for i in range(len(geo.orders[j])):
            part_copy(j, i).wait_send()
    for i in range(len(geo.all_bits)):
        sums_copy(i).wait_send()
    masks_across.wait_send()

    def settle_row(m, carry):
        act_copy(m).wait()
        half_copy(m).wait_send()
        mixed_copy(m).wait_send()
        ffn_copy(m).wait_send()

        @pl.when(in_first)
        def _():
            grads_copy(m).wait()
            whole, low, high = pass_copies(m)
            pl.when(on_right)(low.wait_send)
            pl.when(on_left)(high.wait_send)
            whole.wait_send()
            low, high = near_copies(m)
            pl.when(on_right)(low.wait_send)
            pl.when(on_left)(high.wait_send)

        @pl.when(in_second)
        def _():
            field_copy(m).wait_send()
            whole, sides, low, high = back_copies(m)
            pl.when(on_right)(low.wait_send)
            pl.when(on_left)(high.wait_send)
            whole.wait_send()
            sides.wait_send()
            grads_across(m).wait_recv()

        return carry

    lax.fori_loop(0, rows, settle_row, 0)

    @pl.when(in_first)
    def _():
        pl.when(on_right)(tokens_right.wait_send)
        pl.when(on_left)(tokens_left.wait_send)
        near_fields.wait_send()

    @pl.when(in_second)
    def _():
        masks_back.wait_send()
        weight_copy.wait_send()


def hand_over(*refs):
    sems_in, sems_out = refs[-2:]
    count = len(refs) // 3
    sources, targets, held = refs[:count], refs[count : 2 * count], refs[2 * count : 3 * count]
    copies_in = [pltpu.make_async_copy(sources[i], held[i], sems_in.at[i]) for i in range(count)]
    copies_out = [pltpu.make_async_copy(held[i], targets[i], sems_out.at[i]) for i in range(count)]
    for copy in copies_in:
        copy.start()
    for i in range(count):
        copies_in[i].wait()
        copies_out[i].start()
    for copy in copies_out:
        copy.wait()


def per_device(
    dp,
    seq,
    tokens,
    cotangent,
    tap_masks,
    conv_weight,
    up_weight,
    up_bias,
    down_weight,
    norm_gains,
    shift_terms,
):
    rows, length, width = tokens.shape
    hidden = up_weight.shape[2]
    geo = Geometry(dp, seq, rows, length, width, hidden)
    reach = length + 2 * HALO
    vmem = pl.BlockSpec(memory_space=pltpu.VMEM)
    hbm = pl.BlockSpec(memory_space=pl.ANY)
    dma = pltpu.SemaphoreType.DMA
    stages = len(geo.all_bits)
    slices = (geo.slices, geo.owners, geo.share, width)
    made = pl.pallas_call(
        functools.partial(body, geo),
        out_shape=[
            jax.ShapeDtypeStruct((rows, length, width), BF16),
            jax.ShapeDtypeStruct((rows, length, width), F32),
            jax.ShapeDtypeStruct((TAPS, geo.share, width), F32),
            jax.ShapeDtypeStruct((geo.share, hidden), F32),
            jax.ShapeDtypeStruct((geo.chunks * geo.share, width), F32),
            jax.ShapeDtypeStruct((1, geo.bias_share), F32),
            jax.ShapeDtypeStruct((2, geo.final_share), F32),
            jax.ShapeDtypeStruct((4, geo.final_share), F32),
        ],
        in_specs=[hbm] * 5 + [vmem] * 4,
        out_specs=[hbm] * 2 + [vmem] * 6,
        scratch_shapes=[
            pltpu.VMEM((2 * rows, reach, width), BF16),
            pltpu.VMEM((rows, reach, width), BF16),
            pltpu.VMEM((rows, 2, EDGE, width), BF16),
            pltpu.VMEM((TAPS * width, width), BF16),
            pltpu.VMEM((width, hidden), BF16),
            pltpu.VMEM((hidden, width), BF16),
            pltpu.VMEM((2 * geo.chunks + 1, geo.tokens, width), BF16),
            pltpu.VMEM((length, TAPS * width), BF16),
            pltpu.VMEM((2 * geo.tokens, width // 2), BF16),
            pltpu.VMEM((geo.tokens, width), BF16),
            pltpu.VMEM((geo.tokens, width), BF16),
            pltpu.VMEM((geo.tokens, width), BF16),
            pltpu.VMEM((geo.tokens, 128), F32),
            pltpu.VMEM((rows, length, width), F32),
            pltpu.VMEM((rows, length, width), BF16),
            pltpu.VMEM((geo.tokens, width), BF16),
            pltpu.VMEM((geo.tokens, width), BF16),
            pltpu.VMEM((geo.tokens, width), BF16),
            pltpu.VMEM((geo.part_chunks, geo.tokens, width), BF16),
            pltpu.VMEM((geo.part_chunks, geo.tokens, width), BF16),
            pltpu.VMEM((rows, length, width), BF16),
            pltpu.VMEM((TAPS, rows, length), jnp.int32),
            pltpu.VMEM((TAPS, rows, length), jnp.int32),
            pltpu.VMEM((2 * geo.tokens, 128), F32),
            pltpu.VMEM((geo.tokens, 128), F32),
            pltpu.VMEM((width, width // 2), F32),
            pltpu.VMEM(slices, BF16),
            pltpu.VMEM(slices, BF16),
            pltpu.VMEM((16, width), F32),
            pltpu.VMEM((stages, 16, width), F32),
            pltpu.VMEM((stages, 16, width), F32),
            dma((3,)),
            dma((2,)),
            dma((2,)),
            dma((2,)),
            dma((2,)),
            dma((2,)),
            dma((rows, 3)),
            dma((rows, 3)),
            dma((rows,)),
            dma((rows,)),
            dma,
            dma,
            dma((rows, 4)),
            dma((rows, 4)),
            dma((rows,)),
            dma((rows,)),
            dma((rows,)),
            dma((rows,)),
            dma((rows,)),
            dma((rows,)),
            dma((rows, 2)),
            dma((rows, 2)),
            dma((rows,)),
            dma((rows,)),
            dma((rows,)),
            dma((rows,)),
            dma((geo.slices, len(geo.bits))),
            dma((geo.slices, len(geo.bits))),
            dma((stages,)),
            dma((stages,)),
        ],
        compiler_params=pltpu.CompilerParams(
            collective_id=0, has_side_effects=True, vmem_limit_bytes=63 * 2**20
        ),
    )(
        tokens,
        cotangent,
        jnp.transpose(conv_weight[0], (1, 0, 2)).reshape(TAPS * width, width),
        up_weight[0],
        down_weight[0],
        tap_masks[0],
        up_bias,
        jnp.transpose(norm_gains[0]),
        jnp.transpose(shift_terms[0]),
    )
    made = pl.pallas_call(
        hand_over,
        out_shape=[jax.ShapeDtypeStruct(array.shape, array.dtype) for array in made],
        in_specs=[hbm] * len(made),
        out_specs=[hbm] * len(made),
        scratch_shapes=[pltpu.VMEM(array.shape, array.dtype) for array in made] + [dma((len(made),))] * 2,
    )(*made)
    act, grads, conv_grad, up_grad, down_grad, bias_grad, gain_grad, shift_grad = made
    conv_grad = jnp.transpose(conv_grad, (1, 0, 2))
    if geo.low > 1:
        groups = [list(range(at, at + geo.low)) for at in range(0, seq, geo.low)]
        conv_grad, up_grad, down_grad = (
            lax.psum_scatter(
                grad, "seq", scatter_dimension=0, axis_index_groups=groups, tiled=True
            )
            for grad in (conv_grad, up_grad, down_grad)
        )
    return (
        act[None],
        grads[None],
        conv_grad[None],
        up_grad[None],
        bias_grad,
        down_grad[None],
        jnp.transpose(gain_grad)[None],
        jnp.transpose(shift_grad)[None],
    )


def solution(mesh):
    placed = (
        P("dp", "seq", None),
        P("dp", "seq", None),
        P("section", None, "dp", "seq"),
        P("section", None, None, None),
        P("section", None, None),
        P("section", None),
        P("section", None, None),
        P("section", None, None),
        P("section", None, None),
    )
    return jax.shard_map(
        functools.partial(per_device, mesh.shape["dp"], mesh.shape["seq"]),
        mesh=mesh,
        in_specs=placed,
        out_specs=(
            P("section", "dp", "seq", None),
            P("section", "dp", "seq", None),
            P("section", ("dp", "seq"), None, None),
            P("section", ("dp", "seq"), None),
            P("section", ("dp", "seq")),
            P("section", ("dp", "seq"), None),
            P("section", ("dp", "seq"), None),
            P("section", ("dp", "seq"), None),
        ),
        check_vma=False,
    )
```
